512 devices in a mesh: grp: 4 (over x), seq: 32 (over y_lo, z, core), tp: 4 (over y_hi).
Axes of the slice: x: 4, y: 8 (y_hi: 4, y_lo: 2; y = y_hi * 2 + y_lo), z: 8, core: 2. Of those that a mesh axis runs over, the one named last changes fastest.
Arguments:
- latent: bfloat16 [8192, 3072], P('seq'), may hold values from -6 to 6
- condition: bfloat16 [8192, 3072], P('seq'), may hold values from -6 to 6
- modulation: float32 [2, 3, 3072], replicated, may hold values from -3 to 3
- qk_gain: float32 [2, 2, 128], replicated, may hold values from 1.2 to 2.4
- qkv_weight: bfloat16 [2, 3, 3072, 2048], P(None, None, 'seq', ('grp', 'tp')), may hold values from -0.109375 to 0.109375
- out_weight: bfloat16 [2, 2048, 3072], P(None, ('grp', 'tp'), 'seq'), may hold values from -0.25 to 0.25
Outputs:
- mixed: bfloat16 [8192, 3072], P('seq', ('grp', 'tp'))
The draws below stay inside these ranges and needn't reach their ends.
All inputs are finite; a program needn't handle non-finite values.
Results may differ from the reference program's by a relative error of at most 0.015.
Values may be sent and summed in bfloat16 or wider, within the bound.
A program may use at most 128 MiB of HBM per device.

```python
import math
import jax
import jax.numpy as jnp
from jax import lax

D = 3072
HEAD = 128
TOKENS = 8192
HD = 2048


def with_spikes(drawn, rng, source, target, shards_of, factor):
    def block_of(axis_at):
        return (jnp.arange(drawn.shape[axis_at]) // (drawn.shape[axis_at] // shards_of)).reshape((-1,) + (1,) * (drawn.ndim - 1 - axis_at))

    near = jax.random.permutation(rng, shards_of)[block_of(target)]
    second = (block_of(target) + shards_of // 2) % shards_of
    return jnp.where((block_of(source) == near) | (block_of(source) == second), factor * drawn, drawn)


def shard_levels(key, shape, pieces, least, top_value):
    loudness, own = 1.0, jax.random.fold_in(key, 6)
    for dim, parts in pieces:
        draws = jnp.exp(jax.random.uniform(jax.random.fold_in(own, dim), (parts,), jnp.float32, least / len(pieces), top_value / len(pieces)))
        loudness = loudness * jnp.repeat(draws, shape[dim] // parts).reshape([-1 if axis == dim else 1 for axis in range(len(shape))])
    return loudness


def gaussian(key, extent, width, reach, shards=(), kind=jnp.bfloat16):
    loudness = shard_levels(key, extent, shards, -0.22, 0.18) if shards else 1.0
    values = jax.random.normal(key, extent, jnp.float32) * width * loudness
    return jnp.minimum(jnp.maximum(values, -reach), reach).astype(kind)


def noise_with(stream_key, extent, deviation, limit, cuts, heavy, kind=jnp.bfloat16):
    values = deviation * jax.random.normal(stream_key, extent, jnp.float32)
    if cuts:
        values = values * shard_levels(stream_key, extent, cuts, -0.22, 0.18)
    return jnp.clip(with_spikes(values, jax.random.fold_in(stream_key, 3), *heavy), -limit, limit).astype(kind)


def setup_inputs(seed: int = 0) -> dict:
    splits = jax.random.split(jax.random.key(seed), 7)
    return {
        "latent": gaussian(splits[0], (TOKENS, D), 1.0, 6.0, ((0, 32),)),
        "condition": gaussian(splits[1], (TOKENS, D), 1.0, 6.0, ((0, 32),)),
        "modulation": gaussian(splits[2], (2, 3, D), 0.6, 3.0, (), jnp.float32),
        "qk_gain": jnp.clip(jnp.exp(jax.random.uniform(splits[3], (2, 2, HEAD), jnp.float32, math.log(1.2), math.log(2.4))), 1.2, 2.4),
        "qkv_weight": gaussian(splits[4], (2, 3, D, HD), D ** -0.5, 0.109375, ((2, 32), (3, 16))),
        "out_weight": noise_with(splits[5], (2, HD, D), HD ** -0.5, 0.25, ((1, 16), (2, 32)), (1, 2, 32, 2.75)),
    }


def layer_norm(states):
    center = states - lax.optimization_barrier(jnp.mean(states, axis=-1, keepdims=True))
    variance = lax.optimization_barrier(jnp.mean(center * center, axis=-1, keepdims=True))
    return center / jnp.sqrt(variance + 1e-06)

def head_norm(values_in, gain_row):
    power = lax.optimization_barrier(jnp.mean(values_in * values_in, axis=-1, keepdims=True))
    return values_in / jnp.sqrt(power + 1e-06) * gain_row

def one_head(operands):
    query_head, key_head, value_head = operands
    scores = jnp.dot(query_head, key_head.T, preferred_element_type=jnp.float32) / jnp.sqrt(jnp.float32(HEAD))
    weights = jnp.exp(scores)
    denominator = lax.optimization_barrier(jnp.sum(weights, axis=-1, keepdims=True))
    numerator = jnp.dot(weights.astype(jnp.bfloat16), value_head, preferred_element_type=jnp.float32)
    return (numerator / denominator).astype(jnp.bfloat16)

def reference(latent, condition, modulation, qk_gain, qkv_weight, out_weight):
    residual = latent.astype(jnp.float32)
    inputs = [residual + condition.astype(jnp.float32), residual]
    summed = jnp.zeros(residual.shape, jnp.float32)
    rows_all = residual.shape[0]
    for block_index in range(2):
        normed = (layer_norm(inputs[block_index]) * (1.0 + modulation[block_index, 1]) + modulation[block_index, 0]).astype(jnp.bfloat16)
        query_full = jnp.dot(normed, qkv_weight[block_index, 0], preferred_element_type=jnp.float32)
        key_full = jnp.dot(normed, qkv_weight[block_index, 1], preferred_element_type=jnp.float32)
        value_full = jnp.dot(normed, qkv_weight[block_index, 2], preferred_element_type=jnp.float32)
        head_count = query_full.shape[1] // HEAD
        query_full = head_norm(query_full.reshape(rows_all, head_count, HEAD), qk_gain[block_index, 0]).astype(jnp.bfloat16)
        key_full = head_norm(key_full.reshape(rows_all, head_count, HEAD), qk_gain[block_index, 1]).astype(jnp.bfloat16)
        value_full = value_full.reshape(rows_all, head_count, HEAD).astype(jnp.bfloat16)
        attended = lax.map(one_head, (query_full.transpose(1, 0, 2), key_full.transpose(1, 0, 2), value_full.transpose(1, 0, 2)))
        attended = attended.transpose(1, 0, 2).reshape(rows_all, head_count * HEAD)
        summed = summed + modulation[block_index, 2] * jnp.dot(attended, out_weight[block_index], preferred_element_type=jnp.float32)
    return (residual + summed).astype(jnp.bfloat16)
```

```python
import math

import jax
import jax.numpy as jnp
from jax import lax
from jax.experimental import pallas as pl
from jax.experimental.pallas import tpu as pltpu
from jax.sharding import PartitionSpec as P

MESH = pl.DeviceIdType.MESH
BF16, F32 = jnp.bfloat16, jnp.float32
Z = 8
ROWS = 256
CHIP = 2 * ROWS
D = 3072
HEAD = 128
WROWS = 96
N_SEMS = 112


def kernel(
    lat, cond, mod, gain, wsh, owt, out,
    wbuf, xbuf, xst, qbuf, kv, qkvst, owb, acc, abuf, ast, pst, rbuf,
    send_sems, recv_sems,
):
    x, s, tp = lax.axis_index("grp"), lax.axis_index("seq"), lax.axis_index("tp")
    y, z, c = s // 16, (s // 2) % 8, s % 2

    def seq_of(y_, z_, c_):
        return y_ * 16 + z_ * 2 + c_

    sib = {"seq": seq_of(y, z, 1 - c)}
    row = {"seq": seq_of(1 - y, z, c)}
    diag = {"seq": seq_of(1 - y, z, 1 - c)}
    right = {"seq": seq_of(y, (z + 1) % Z, c)}
    left = {"seq": seq_of(y, (z + 7) % Z, c)}

    def zm(t):
        return (z + Z - t) % Z

    def zp(t):
        return (z + t) % Z

    px, py, pz = y * 2 + z // 4, x // 2, z % 4 + 4 * (x % 2)
    moves = px != x
    partner = {"grp": px, "seq": seq_of(py, pz, c)}

    barrier = pltpu.get_barrier_semaphore()

    def greet(device):
        pl.semaphore_signal(barrier, inc=1, device_id=device, device_id_type=MESH)

    flat = x * 4 + y * 2 + c
    for i in range(1, 16):
        f = (flat + i) % 16
        greet({"grp": f // 4, "seq": seq_of((f // 2) % 2, z, f % 2)})
    greet(right)
    greet(left)
    for i in range(1, 4):
        greet({"tp": (tp + i) % 4})

    @pl.when(moves)
    def _():
        greet(partner)

    pl.semaphore_wait(barrier, 20 + jnp.where(moves, 1, 0))

    ids = iter(range(N_SEMS))
    sent = []

    def remote(src, dst, device, i):
        return pltpu.make_async_remote_copy(
            src_ref=src, dst_ref=dst, send_sem=send_sems.at[i], recv_sem=recv_sems.at[i],
            device_id=device, device_id_type=MESH,
        )

    def push(src, dst, device):
        i = next(ids)
        copy = remote(src, dst, device, i)
        copy.start()
        sent.append(copy)
        return i

    def arrived(land, i):
        remote(land, land, sib, i).wait_recv()

    def ring_send(view, t):
        if t < 3:
            a, b = view(zm(t), None), view(zp(t), None)
        else:
            a, b = view(zm(t), 0), view(zp(t), 1)
        return push(a, a, right), push(b, b, left)

    def ring_wait(view, t, got):
        if t < 4:
            arrived(view(zm(t), None), got[0])
            arrived(view(zp(t), None), got[1])
        else:
            arrived(view(zm(t), 0), got[0])
            arrived(view(zp(t), 1), got[1])

    ow_id = next(ids)
    ow_copy = remote(owt, owb.at[seq_of(py, pz, c)], partner, ow_id)

    w_sib = push(wsh.at[1 - c], wbuf.at[:, y, z, pl.ds(pl.multiple_of(c * WROWS, 32), WROWS)], sib)

    @pl.when(moves)
    def _():
        ow_copy.start()

    @pl.when(jnp.logical_not(moves))
    def _():
        owb[s] = owt[...]

    for j in range(3):
        wbuf[j, y, z, pl.ds(pl.multiple_of(c * WROWS, 32), WROWS), :] = wsh[c, j]

    def layer_norm(block, store, lo, hi):
        use = jnp.where(block == 0, 1.0, 0.0).astype(F32)
        scale = 1.0 + mod[block, 1:2, :]
        shift = mod[block, 0:1, :]

        def step(i, carry):
            at = pl.ds(pl.multiple_of(i * 16, 16), 16)
            v = lat[at, :].astype(F32) + use * cond[at, :].astype(F32)
            center = v - jnp.mean(v, axis=-1, keepdims=True)
            var = jnp.mean(center * center, axis=-1, keepdims=True)
            store(at, (center * lax.rsqrt(var + 1e-6) * scale + shift).astype(BF16))
            return carry

        lax.fori_loop(lo, hi, step, 0)

    def store_stage(at, v):
        xst[at, :] = v

    def store_own(at, v):
        xbuf[c, at, :] = v

    layer_norm(1 - c, store_stage, 0, 4)
    arrived(wbuf.at[:, y, z, pl.ds(pl.multiple_of((1 - c) * WROWS, 32), WROWS)], w_sib)

    def half(h):
        return slice(None) if h is None else pl.ds(h * WROWS, WROWS)

    def view_b(zz, h):
        return wbuf.at[0:2, y, zz, half(h)]

    def view_a(zz, h):
        return wbuf.at[2, :, zz, half(h)]

    b_y, b_y_land = [], []

    def forward_b(zz):
        b_y.append(push(wbuf.at[0:2, y, zz], wbuf.at[0:2, y, zz], row))
        b_y_land.append(wbuf.at[0:2, 1 - y, zz])

    a_y = push(wbuf.at[2, y, z], wbuf.at[2, y, z], row)
    got_b = ring_send(view_b, 0)
    forward_b(z)
    layer_norm(1 - c, store_stage, 4, 8)
    arrived(wbuf.at[2, 1 - y, z], a_y)
    got_a = ring_send(view_a, 0)
    layer_norm(1 - c, store_stage, 8, 16)
    x_sib = push(xst, xbuf.at[c], sib)
    for t in range(1, 5):
        ring_wait(view_b, t, got_b)
        if t < 4:
            got_b = ring_send(view_b, t)
        ring_wait(view_a, t, got_a)
        if t < 4:
            got_a = ring_send(view_a, t)
            forward_b(zm(t))
            forward_b(zp(t))
            layer_norm(c, store_own, 5 * (t - 1), 5 * t + (t == 3))
        else:
            forward_b(zp(t))

    def view_o(zz, h):
        base = seq_of(y, zz, c)
        return owb.at[base] if h is None else owb.at[base, pl.ds(h * 48, 48)]

    @pl.when(moves)
    def _():
        ow_copy.wait_send()
        arrived(owb.at[s], ow_id)

    got_o = ring_send(view_o, 0)
    for land, i in zip(b_y_land, b_y):
        arrived(land, i)
    arrived(xbuf.at[1 - c], x_sib)

    def head_norm(v, g):
        return v * lax.rsqrt(jnp.mean(v * v, axis=-1, keepdims=True) + 1e-6) * g

    q_gain = gain[c, 0:1, :] * (math.log2(math.e) / math.sqrt(HEAD))
    k_gain = gain[c, 1:2, :]
    for m in range(2):
        xs = xbuf[m]
        wk = wbuf[2].reshape(D, HEAD)
        wv = wbuf[1].reshape(D, HEAD)
        wq = wbuf[0].reshape(D, HEAD)
        at = slice(m * ROWS, (m + 1) * ROWS)
        kvals = jnp.dot(xs, jnp.concatenate([wk, wv], axis=1), preferred_element_type=F32)
        qkvst[0, at, :] = head_norm(kvals[:, :HEAD], k_gain).astype(BF16)
        qkvst[1, at, :] = kvals[:, HEAD:].astype(BF16)
        qvals = jnp.dot(xs, wq, preferred_element_type=F32)
        qkvst[2, at, :] = head_norm(qvals, q_gain).astype(BF16)
        ring_wait(view_o, m + 1, got_o)
        got_o = ring_send(view_o, m + 1)

    stays = y == c
    kv_id, q_id = next(ids), next(ids)
    kv_copy = remote(qkvst.at[0:2], kv.at[y, z], diag, kv_id)
    q_copy = remote(qkvst.at[2], qbuf, diag, q_id)

    @pl.when(stays)
    def _():
        kv[y, z] = qkvst[0:2]
        qbuf[...] = qkvst[2]

    @pl.when(jnp.logical_not(stays))
    def _():
        kv_copy.start()
        q_copy.start()
        arrived(kv.at[c, z], kv_id)

    def view_k(zz, h):
        return kv.at[c, zz, 0] if h is None else kv.at[c, zz, 0, pl.ds(h * ROWS, ROWS)]

    def view_v(zz, h):
        return kv.at[c, zz, 1] if h is None else kv.at[c, zz, 1, pl.ds(h * ROWS, ROWS)]

    acc[...] = jnp.zeros_like(acc)
    ones = jnp.ones((CHIP, HEAD), BF16)

    def attend(r, zz):
        keys = kv[r, zz, 0]
        values = jnp.concatenate([kv[r, zz, 1], ones], axis=1)
        for m in range(2):
            at = slice(m * ROWS, (m + 1) * ROWS)
            scores = lax.dot_general(
                qbuf[at, :], keys, (((1,), (1,)), ((), ())), preferred_element_type=F32
            )
            weights = jnp.exp2(scores).astype(BF16)
            acc[at, :] += jnp.dot(weights, values, preferred_element_type=F32)

    def attend_both(r, t):
        def step(i, carry):
            attend(r, (z + Z + (2 * i - 1) * t) % Z)
            return carry

        lax.fori_loop(0, 2, step, 0)

    def share(zz):
        return push(kv.at[c, zz], kv.at[c, zz], sib), kv.at[1 - c, zz]

    got_k = ring_send(view_k, 0)
    got_v = ring_send(view_v, 0)
    own = share(z)

    @pl.when(jnp.logical_not(stays))
    def _():
        arrived(qbuf, q_id)

    attend(c, z)
    arrived(own[1], own[0])
    attend(1 - c, z)
    for t in range(1, 5):
        ring_wait(view_k, t, got_k)
        if t < 4:
            got_k = ring_send(view_k, t)
        ring_wait(view_v, t, got_v)
        if t < 4:
            got_v = ring_send(view_v, t)
            shared = [share(zm(t)), share(zp(t))]
            if t == 1:
                ring_wait(view_o, 3, got_o)
                got_o = ring_send(view_o, 3)
            if t == 2:
                ring_wait(view_o, 4, got_o)
                view = owb16(owb, y, c)
                o_y = [push(v, v, row) for v in view]
            if t == 3:
                for i, v in zip(o_y, owb16(owb, 1 - y, c)):
                    arrived(v, i)
                o_s = [push(v, v, sib) for r in range(2) for v in owb16(owb, r, c)]
            attend_both(c, t)
            for i, land in shared:
                arrived(land, i)
            attend_both(1 - c, t)
        else:
            last = share(zp(t))
            attend(c, zp(t))
            arrived(last[1], last[0])
            attend(1 - c, zp(t))

    for m in range(2):
        part = acc[m * ROWS:(m + 1) * ROWS, :]
        ast[m] = jnp.transpose(part[:, :HEAD] / part[:, HEAD:]).astype(BF16)
    own_core = jnp.logical_and(c == y, True)
    a_ids = []
    for d in (2, 1, 3, 0):
        i0 = next(ids)
        i1 = next(ids)
        a_ids.append((d, i0, i1))
        for m in range(2):
            device = {"grp": (x + d) % 4, "seq": seq_of(c, z, m)}
            copy = pltpu.make_async_remote_copy(
                src_ref=ast.at[m], dst_ref=abuf.at[x, y],
                send_sem=send_sems.at[i0 + m], recv_sem=recv_sems.at[i0 + y],
                device_id=device, device_id_type=MESH,
            )
            if d == 0:
                is_self = jnp.logical_and(own_core, c == m)

                @pl.when(is_self)
                def _(m=m):
                    abuf[x, y] = ast[m]

                @pl.when(jnp.logical_not(is_self))
                def _(copy=copy):
                    copy.start()
            else:
                copy.start()
                sent.append(copy)

    for d, i0, i1 in a_ids:
        src = (x + 4 - d) % 4
        for b in range(2):
            if d == 0:
                @pl.when(jnp.logical_not(jnp.logical_and(c == y, y == b)))
                def _(b=b, i0=i0):
                    arrived(abuf.at[src, b], i0 + b)
            else:
                arrived(abuf.at[src, b], i0 + b)
    for i, v in zip(o_s, [v for r in range(2) for v in owb16(owb, r, 1 - c)]):
        arrived(v, i)

    def project(yh):
        total = None
        for xx in range(4):
            ow = owb[pl.ds(xx * 8 + yh * 2, 2)].reshape(2 * WROWS, 2 * HEAD)
            a = abuf[xx].reshape(2 * HEAD, ROWS)
            term = jnp.dot(ow, a, preferred_element_type=F32)
            total = term if total is None else total + term
        return total

    r_ids = []
    for d in (2, 1, 3):
        yh = (tp + d) % 4
        pst[d] = project(yh).astype(BF16)
        r_ids.append((d, push(pst.at[d], rbuf.at[d], {"tp": yh})))
    total = project(tp)
    for d, i in r_ids:
        arrived(rbuf.at[d], i)
    for d in range(1, 4):
        total = total + rbuf[d].astype(F32)
    out[...] = total

    for copy in sent:
        copy.wait_send()

    @pl.when(jnp.logical_not(stays))
    def _():
        kv_copy.wait_send()
        q_copy.wait_send()

    d, i0, i1 = a_ids[3]
    for m in range(2):
        @pl.when(jnp.logical_not(jnp.logical_and(own_core, c == m)))
        def _(m=m):
            remote(ast.at[m], abuf.at[x, y], sib, i0 + m).wait_send()


def owb16(owb, r, c):
    return [owb.at[r * 16 + zz * 2 + c] for zz in range(Z)]


def body(latent, condition, modulation, qk_gain, qkv_weight, out_weight):
    s = lax.axis_index("seq")
    gate = lax.dynamic_slice_in_dim(modulation[:, 2], s * WROWS, WROWS, 1)
    owt = jnp.transpose(out_weight.astype(F32) * gate[:, None, :], (2, 0, 1))
    owt = owt.reshape(WROWS, 2 * HEAD).astype(BF16)
    w = jnp.stack([qkv_weight[:, 0], qkv_weight[:, 2], qkv_weight[:, 1]], axis=1)
    vm = pl.BlockSpec(memory_space=pltpu.VMEM)
    summed = pl.pallas_call(
        kernel,
        out_shape=jax.ShapeDtypeStruct((2 * WROWS, ROWS), F32),
        in_specs=[vm] * 6,
        out_specs=vm,
        scratch_shapes=[
            pltpu.VMEM((3, 2, Z, 2 * WROWS, HEAD), BF16),
            pltpu.VMEM((2, ROWS, D), BF16),
            pltpu.VMEM((ROWS, D), BF16),
            pltpu.VMEM((CHIP, HEAD), BF16),
            pltpu.VMEM((2, Z, 2, CHIP, HEAD), BF16),
            pltpu.VMEM((3, CHIP, HEAD), BF16),
            pltpu.VMEM((32, WROWS, 2 * HEAD), BF16),
            pltpu.VMEM((CHIP, 2 * HEAD), F32),
            pltpu.VMEM((4, 2, HEAD, ROWS), BF16),
            pltpu.VMEM((2, HEAD, ROWS), BF16),
            pltpu.VMEM((4, 2 * WROWS, ROWS), BF16),
            pltpu.VMEM((4, 2 * WROWS, ROWS), BF16),
            pltpu.SemaphoreType.DMA((N_SEMS,)),
            pltpu.SemaphoreType.DMA((N_SEMS,)),
        ],
        compiler_params=pltpu.CompilerParams(
            collective_id=0, has_side_effects=True, vmem_limit_bytes=50 * 1024 * 1024
        ),
        cost_estimate=pl.CostEstimate(
            flops=3_900_000_000, bytes_accessed=4_000_000, transcendentals=4_200_000
        ),
    )(latent, condition, modulation, qk_gain, w, owt)
    g = lax.axis_index(("grp", "tp"))
    own = lax.dynamic_slice_in_dim(latent, g * 2 * WROWS, 2 * WROWS, 1).astype(F32)
    return (own + summed.T).astype(BF16)


def solution(mesh):
    return jax.shard_map(
        body,
        mesh=mesh,
        in_specs=(
            P("seq", None),
            P("seq", None),
            P(),
            P(),
            P(None, None, "seq", ("grp", "tp")),
            P(None, ("grp", "tp"), "seq"),
        ),
        out_specs=P("seq", ("grp", "tp")),
        check_vma=False,
    )
```

```python
import math

import jax
import jax.numpy as jnp
from jax import lax
from jax.experimental import pallas as pl
from jax.experimental.pallas import tpu as pltpu
from jax.sharding import PartitionSpec as P

MESH = pl.DeviceIdType.MESH
BF16, F32 = jnp.bfloat16, jnp.float32
Z = 8
ROWS = 256
CHIP = 2 * ROWS
D = 3072
HEAD = 128
WROWS = 96
N_SEMS = 160


def kernel(
    lat_in, cond_in, mod_in, gain, gate, wsh, ow_in, out,
    lat, cond, mod, ow, owt, wbuf, xbuf, xst, qbuf, kv, qkvst, owb, acc, abuf, ast, pst, rbuf, res,
    send_sems, recv_sems, load_sems,
):
    loads = []
    for i, (a, b) in enumerate(((ow_in, ow), (mod_in, mod), (lat_in, lat), (cond_in, cond))):
        loads.append(pltpu.make_async_copy(a, b, load_sems.at[i]))
        loads[-1].start()
    x, s, tp = lax.axis_index("grp"), lax.axis_index("seq"), lax.axis_index("tp")
    y, z, c = s // 16, (s // 2) % 8, s % 2

    def seq_of(y_, z_, c_):
        return y_ * 16 + z_ * 2 + c_

    sib = {"seq": seq_of(y, z, 1 - c)}
    row = {"seq": seq_of(1 - y, z, c)}
    diag = {"seq": seq_of(1 - y, z, 1 - c)}
    right = {"seq": seq_of(y, (z + 1) % Z, c)}
    left = {"seq": seq_of(y, (z + 7) % Z, c)}

    def zm(t):
        return (z + Z - t) % Z

    def zp(t):
        return (z + t) % Z

    px, py, pz = y * 2 + z // 4, x // 2, z % 4 + 4 * (x % 2)
    moves = px != x
    partner = {"grp": px, "seq": seq_of(py, pz, c)}

    barrier = pltpu.get_barrier_semaphore()

    def greet(device):
        pl.semaphore_signal(barrier, inc=1, device_id=device, device_id_type=MESH)

    flat = x * 4 + y * 2 + c
    for i in range(1, 16):
        f = (flat + i) % 16
        greet({"grp": f // 4, "seq": seq_of((f // 2) % 2, z, f % 2)})
    greet(right)
    greet(left)
    for i in range(1, 4):
        greet({"tp": (tp + i) % 4})

    @pl.when(moves)
    def _():
        greet(partner)

    pl.semaphore_wait(barrier, 20 + jnp.where(moves, 1, 0))

    ids = iter(range(N_SEMS))
    sent = []

    def remote(src, dst, device, i):
        return pltpu.make_async_remote_copy(
            src_ref=src, dst_ref=dst, send_sem=send_sems.at[i], recv_sem=recv_sems.at[i],
            device_id=device, device_id_type=MESH,
        )

    def push(src, dst, device):
        i = next(ids)
        copy = remote(src, dst, device, i)
        copy.start()
        sent.append(copy)
        return i

    def arrived(land, i):
        remote(land, land, sib, i).wait_recv()

    def ring_send(view, t):
        if t < 3:
            a, b = view(zm(t), None), view(zp(t), None)
        else:
            a, b = view(zm(t), 0), view(zp(t), 1)
        return push(a, a, right), push(b, b, left)

    def ring_wait(view, t, got):
        if t < 4:
            arrived(view(zm(t), None), got[0])
            arrived(view(zp(t), None), got[1])
        else:
            arrived(view(zm(t), 0), got[0])
            arrived(view(zp(t), 1), got[1])

    own_rows = pl.ds(pl.multiple_of(c * WROWS, 32), WROWS)
    sib_rows = pl.ds(pl.multiple_of((1 - c) * WROWS, 32), WROWS)
    w_sib = push(wsh.at[1 - c], wbuf.at[:, y, z, own_rows], sib)
    w_own = pltpu.make_async_copy(wsh.at[c], wbuf.at[:, y, z, own_rows], load_sems.at[4])
    w_own.start()

    ow_id = next(ids)
    ow_copy = remote(owt, owb.at[seq_of(py, pz, c)], partner, ow_id)
    loads[0].wait()
    for block in range(2):
        gates = jnp.transpose(jnp.broadcast_to(gate[block], (HEAD, WROWS)))
        owt[:, block * HEAD:(block + 1) * HEAD] = (ow[block].astype(F32) * gates).astype(BF16)

    @pl.when(moves)
    def _():
        ow_copy.start()

    @pl.when(jnp.logical_not(moves))
    def _():
        owb[s] = owt[...]

    def layer_norm(block, store, lo, hi):
        use = jnp.where(block == 0, 1.0, 0.0).astype(F32)
        scale = 1.0 + mod[1, pl.ds(block, 1), :]
        shift = mod[0, pl.ds(block, 1), :]

        def step(i, carry):
            at = pl.ds(pl.multiple_of(i * 32, 32), 32)
            v = lat[at, :].astype(F32) + use * cond[at, :].astype(F32)
            center = v - jnp.mean(v, axis=-1, keepdims=True)
            var = jnp.mean(center * center, axis=-1, keepdims=True)
            store(at, (center * lax.rsqrt(var + 1e-6) * scale + shift).astype(BF16))
            return carry

        lax.fori_loop(lo, hi, step, 0)

    def store_stage(at, v):
        xst[at, :] = v

    def store_own(at, v):
        xbuf[c, at, :] = v

    w_own.wait()
    arrived(wbuf.at[:, y, z, sib_rows], w_sib)

    def half(h):
        return slice(None) if h is None else pl.ds(h * WROWS, WROWS)

    def view_q(zz, h):
        return wbuf.at[0, y, zz, half(h)]

    def view_b(zz, h):
        return wbuf.at[2, y, zz, half(h)]

    def view_a(zz, h):
        return wbuf.at[1, :, zz, half(h)]

    def view_o(zz, h):
        base = seq_of(y, zz, c)
        return owb.at[base] if h is None else owb.at[base, pl.ds(h * 48, 48)]

    b_y, q_y = [], []

    def forward(j, zz, kept):
        kept.append((push(wbuf.at[j, y, zz], wbuf.at[j, y, zz], row), wbuf.at[j, 1 - y, zz]))

    a_y = push(wbuf.at[1, y, z], wbuf.at[1, y, z], row)
    got_b = ring_send(view_b, 0)
    forward(2, z, b_y)
    for load in loads[1:]:
        load.wait()
    g = x * 4 + tp
    near = lat[:, pl.ds(pl.multiple_of(g * 3 // 2 * HEAD, HEAD), 2 * HEAD)].astype(F32)
    near = jnp.where(g % 2 == 0, near[:, :2 * WROWS], near[:, HEAD // 2:])
    res[...] = jnp.transpose(near)

    layer_norm(1 - c, store_stage, 0, 3)
    arrived(wbuf.at[1, 1 - y, z], a_y)
    got_a = ring_send(view_a, 0)
    layer_norm(1 - c, store_stage, 3, 8)
    x_sib = push(xst, xbuf.at[c], sib)

    @pl.when(moves)
    def _():
        ow_copy.wait_send()
        arrived(owb.at[s], ow_id)

    got_o = ring_send(view_o, 0)
    for t in range(1, 5):
        ring_wait(view_b, t, got_b)
        if t < 4:
            got_b = ring_send(view_b, t)
        ring_wait(view_a, t, got_a)
        if t < 4:
            got_a = ring_send(view_a, t)
            forward(2, zm(t), b_y)
            forward(2, zp(t), b_y)
            if t == 3:
                got_q = ring_send(view_q, 0)
                forward(0, z, q_y)
            layer_norm(c, store_own, (0, 0, 3, 6)[t], (0, 3, 6, 8)[t])
            ring_wait(view_o, t, got_o)
            got_o = ring_send(view_o, t)
        else:
            forward(2, zp(t), b_y)
    for i, land in b_y:
        arrived(land, i)
    arrived(xbuf.at[1 - c], x_sib)

    def q_hop(t, got):
        ring_wait(view_q, t, got)
        if t < 4:
            got = ring_send(view_q, t)
            forward(0, zm(t), q_y)
            forward(0, zp(t), q_y)
            return got
        forward(0, zp(t), q_y)

    def head_norm(v, g):
        return v * lax.rsqrt(jnp.mean(v * v, axis=-1, keepdims=True) + 1e-6) * g

    q_gain = gain[c, 0:1, :] * (math.log2(math.e) / math.sqrt(HEAD))
    k_gain = gain[c, 1:2, :]
    got_q = q_hop(1, got_q)
    for m in range(2):
        xs = xbuf[m]
        wk = wbuf[1].reshape(D, HEAD)
        wv = wbuf[2].reshape(D, HEAD)
        at = slice(m * ROWS, (m + 1) * ROWS)
        kvals = jnp.dot(xs, jnp.concatenate([wk, wv], axis=1), preferred_element_type=F32)
        qkvst[0, at, :] = head_norm(kvals[:, :HEAD], k_gain).astype(BF16)
        qkvst[1, at, :] = kvals[:, HEAD:].astype(BF16)
        if m == 0:
            got_q = q_hop(2, got_q)

    stays = y == c
    kv_ids, q_id = [next(ids), next(ids)], next(ids)
    kv_copies = [remote(qkvst.at[i], kv.at[y, z, i], diag, kv_ids[i]) for i in range(2)]
    q_copy = remote(qkvst.at[2], qbuf, diag, q_id)

    @pl.when(stays)
    def _():
        kv[y, z] = qkvst[0:2]

    @pl.when(jnp.logical_not(stays))
    def _():
        for copy in kv_copies:
            copy.start()

    def view_k(zz, h):
        return kv.at[c, zz, 0] if h is None else kv.at[c, zz, 0, pl.ds(h * ROWS, ROWS)]

    def view_v(zz, h):
        return kv.at[c, zz, 1] if h is None else kv.at[c, zz, 1, pl.ds(h * ROWS, ROWS)]

    acc[...] = jnp.zeros_like(acc)
    ones = jnp.ones((CHIP, HEAD), BF16)

    def attend(r, zz):
        keys = kv[r, zz, 0]
        values = jnp.concatenate([kv[r, zz, 1], ones], axis=1)
        for m in range(2):
            at = slice(m * ROWS, (m + 1) * ROWS)
            scores = lax.dot_general(
                qbuf[at, :], keys, (((1,), (1,)), ((), ())), preferred_element_type=F32
            )
            weights = jnp.exp2(scores).astype(BF16)
            acc[at, :] += jnp.dot(weights, values, preferred_element_type=F32)

    def attend_both(r, t):
        def step(i, carry):
            attend(r, (z + Z + (2 * i - 1) * t) % Z)
            return carry

        lax.fori_loop(0, 2, step, 0)

    def share(zz):
        return push(kv.at[c, zz], kv.at[c, zz], sib), kv.at[1 - c, zz]

    got_q = q_hop(3, got_q)

    def kv_come(i):
        @pl.when(jnp.logical_not(stays))
        def _():
            arrived(kv.at[c, z, i], kv_ids[i])

    kv_come(0)
    got_k = ring_send(view_k, 0)
    kv_come(1)
    got_v = ring_send(view_v, 0)
    shared = {0: [share(z)]}

    q_hop(4, got_q)
    ring_wait(view_o, 4, got_o)
    for i, land in q_y:
        arrived(land, i)
    for m in range(2):
        qvals = jnp.dot(xbuf[m], wbuf[0].reshape(D, HEAD), preferred_element_type=F32)
        qkvst[2, m * ROWS:(m + 1) * ROWS, :] = head_norm(qvals, q_gain).astype(BF16)

    @pl.when(stays)
    def _():
        qbuf[...] = qkvst[2]

    @pl.when(jnp.logical_not(stays))
    def _():
        q_copy.start()

    def attend_shared(t):
        for i, land in shared[t]:
            arrived(land, i)
        if t % 4:
            attend_both(1 - c, t)
        else:
            attend(1 - c, zp(t))

    for t in range(1, 5):
        ring_wait(view_k, t, got_k)
        if t < 4:
            got_k = ring_send(view_k, t)
        ring_wait(view_v, t, got_v)
        if t < 4:
            got_v = ring_send(view_v, t)
            shared[t] = [share(zm(t)), share(zp(t))]
            if t == 1:
                o_y = [push(v, v, row) for v in owb16(owb, y, c)]

                @pl.when(jnp.logical_not(stays))
                def _():
                    arrived(qbuf, q_id)

                attend(c, z)
            attend_both(c, t)
            if t == 2:
                attend_shared(0)
            if t == 3:
                for i, v in zip(o_y, owb16(owb, 1 - y, c)):
                    arrived(v, i)
                o_s = [push(v, v, sib) for r in range(2) for v in owb16(owb, r, c)]
                attend_shared(1)
                attend_shared(2)
        else:
            shared[t] = [share(zp(t))]
            attend(c, zp(t))
            attend_shared(3)
            attend_shared(4)

    a_ids = {}
    for h in range(2):
        for m in range(2):
            lo = m * ROWS + h * HEAD
            part = acc[lo:lo + HEAD, :]
            ast[h, m] = jnp.transpose(part[:, :HEAD] / part[:, HEAD:]).astype(BF16)
        for d in (2, 1, 3, 0):
            i0 = next(ids)
            next(ids)
            for m in range(2):
                copy = pltpu.make_async_remote_copy(
                    src_ref=ast.at[h, m], dst_ref=abuf.at[h, x, y],
                    send_sem=send_sems.at[i0 + m], recv_sem=recv_sems.at[i0 + y],
                    device_id={"grp": (x + d) % 4, "seq": seq_of(c, z, m)}, device_id_type=MESH,
                )
                a_ids[h, d, m] = i0, copy
                if d:
                    copy.start()
                    sent.append(copy)
                else:
                    is_self = jnp.logical_and(stays, c == m)

                    @pl.when(is_self)
                    def _():
                        abuf[h, x, y] = ast[h, m]

                    @pl.when(jnp.logical_not(is_self))
                    def _():
                        copy.start()

    for i, v in zip(o_s, [v for r in range(2) for v in owb16(owb, r, 1 - c)]):
        arrived(v, i)

    def project(h, yh):
        total = None
        for xx in range(4):
            w = owb[pl.ds(xx * 8 + yh * 2, 2)].reshape(2 * WROWS, 2 * HEAD)
            a = abuf[h, xx].reshape(2 * HEAD, HEAD)
            term = jnp.dot(w, a, preferred_element_type=F32)
            total = term if total is None else total + term
        return total

    r_ids, totals = {}, []
    for h in range(2):
        for d in (1, 3, 2, 0):
            i0 = a_ids[h, d, 0][0]
            src = (x + 4 - d) % 4
            for b in range(2):
                if d:
                    arrived(abuf.at[h, src, b], i0 + b)
                else:
                    @pl.when(jnp.logical_not(jnp.logical_and(stays, y == b)))
                    def _():
                        arrived(abuf.at[h, src, b], i0 + b)
        for d in (2, 1, 3):
            yh = (tp + d) % 4
            pst[h, d] = project(h, yh).astype(BF16)
            r_ids[h, d] = push(pst.at[h, d], rbuf.at[h, d], {"tp": yh})
        totals.append(project(h, tp))

    for h in range(2):
        total = totals[h]
        for d in (1, 3, 2):
            arrived(rbuf.at[h, d], r_ids[h, d])
            total = total + rbuf[h, d].astype(F32)
        at = slice(h * HEAD, (h + 1) * HEAD)
        out[:, at] = (res[:, at] + total).astype(BF16)

    for copy in sent:
        copy.wait_send()

    @pl.when(jnp.logical_not(stays))
    def _():
        for copy in kv_copies + [q_copy]:
            copy.wait_send()

    for h in range(2):
        for m in range(2):
            @pl.when(jnp.logical_not(jnp.logical_and(stays, c == m)))
            def _():
                a_ids[h, 0, m][1].wait_send()


def owb16(owb, r, c):
    return [owb.at[r * 16 + zz * 2 + c] for zz in range(Z)]


def body(latent, condition, modulation, qk_gain, qkv_weight, out_weight):
    s = lax.axis_index("seq")
    modulation = jnp.transpose(modulation, (1, 0, 2))
    gate = lax.dynamic_slice(modulation, (2, 0, s * WROWS), (1, 2, WROWS)).reshape(2, 1, WROWS)
    vm = pl.BlockSpec(memory_space=pltpu.VMEM)
    hbm = pl.BlockSpec(memory_space=pltpu.HBM)
    mixed = pl.pallas_call(
        kernel,
        out_shape=jax.ShapeDtypeStruct((2 * WROWS, ROWS), BF16),
        in_specs=[hbm, hbm, hbm, vm, vm, hbm, hbm],
        out_specs=vm,
        scratch_shapes=[
            pltpu.VMEM((ROWS, D), BF16),
            pltpu.VMEM((ROWS, D), BF16),
            pltpu.VMEM((3, 2, D), F32),
            pltpu.VMEM((2, WROWS, HEAD), BF16),
            pltpu.VMEM((WROWS, 2 * HEAD), BF16),
            pltpu.VMEM((3, 2, Z, 2 * WROWS, HEAD), BF16),
            pltpu.VMEM((2, ROWS, D), BF16),
            pltpu.VMEM((ROWS, D), BF16),
            pltpu.VMEM((CHIP, HEAD), BF16),
            pltpu.VMEM((2, Z, 2, CHIP, HEAD), BF16),
            pltpu.VMEM((3, CHIP, HEAD), BF16),
            pltpu.VMEM((32, WROWS, 2 * HEAD), BF16),
            pltpu.VMEM((CHIP, 2 * HEAD), F32),
            pltpu.VMEM((2, 4, 2, HEAD, HEAD), BF16),
            pltpu.VMEM((2, 2, HEAD, HEAD), BF16),
            pltpu.VMEM((2, 4, 2 * WROWS, HEAD), BF16),
            pltpu.VMEM((2, 4, 2 * WROWS, HEAD), BF16),
            pltpu.VMEM((2 * WROWS, ROWS), F32),
            pltpu.SemaphoreType.DMA((N_SEMS,)),
            pltpu.SemaphoreType.DMA((N_SEMS,)),
            pltpu.SemaphoreType.DMA((5,)),
        ],
        compiler_params=pltpu.CompilerParams(
            collective_id=0, has_side_effects=True, vmem_limit_bytes=56 * 1024 * 1024
        ),
        cost_estimate=pl.CostEstimate(
            flops=3_900_000_000, bytes_accessed=4_000_000, transcendentals=4_200_000
        ),
    )(latent, condition, modulation, qk_gain, gate, qkv_weight, jnp.transpose(out_weight, (0, 2, 1)))
    return mixed.T


def solution(mesh):
    return jax.shard_map(
        body,
        mesh=mesh,
        in_specs=(
            P("seq", None),
            P("seq", None),
            P(),
            P(),
            P(None, None, "seq", ("grp", "tp")),
            P(None, ("grp", "tp"), "seq"),
        ),
        out_specs=P("seq", ("grp", "tp")),
        check_vma=False,
    )
```

```python
import math

import jax
import jax.numpy as jnp
from jax import lax
from jax.experimental import pallas as pl
from jax.experimental.pallas import tpu as pltpu
from jax.sharding import PartitionSpec as P

MESH = pl.DeviceIdType.MESH
BF16, F32 = jnp.bfloat16, jnp.float32
Z = 8
ROWS = 256
CHIP = 2 * ROWS
D = 3072
HEAD = 128
WROWS = 96
N_SEMS = 200


def kernel(
    lat_in, cond_in, mod_in, gain, wsh, ow_in, out,
    lat, cond, mod, ow, owt, wbuf, xbuf, xst, qbuf, kbuf, vbuf, kst, vst, qst, owb, acc, abuf, ast, pst, rbuf, res,
    send_sems, recv_sems, load_sems,
):
    loads = []
    for i, (a, b) in enumerate(((ow_in, ow), (mod_in, mod), (lat_in, lat), (cond_in, cond))):
        loads.append(pltpu.make_async_copy(a, b, load_sems.at[i]))
        loads[-1].start()
    x, s, tp = lax.axis_index("grp"), lax.axis_index("seq"), lax.axis_index("tp")
    y, z, c = s // 16, (s // 2) % 8, s % 2

    def seq_of(y_, z_, c_):
        return y_ * 16 + z_ * 2 + c_

    sib = {"seq": seq_of(y, z, 1 - c)}
    row = {"seq": seq_of(1 - y, z, c)}
    diag = {"seq": seq_of(1 - y, z, 1 - c)}
    right = {"seq": seq_of(y, (z + 1) % Z, c)}
    left = {"seq": seq_of(y, (z + 7) % Z, c)}

    def zm(t):
        return (z + Z - t) % Z

    def zp(t):
        return (z + t) % Z

    px, py, pz = y * 2 + z // 4, x // 2, z % 4 + 4 * (x % 2)
    moves = px != x
    partner = {"grp": px, "seq": seq_of(py, pz, c)}

    barrier = pltpu.get_barrier_semaphore()

    def greet(device):
        pl.semaphore_signal(barrier, inc=1, device_id=device, device_id_type=MESH)

    flat = x * 4 + y * 2 + c
    for i in range(1, 16):
        f = (flat + i) % 16
        greet({"grp": f // 4, "seq": seq_of((f // 2) % 2, z, f % 2)})
    for dz in (1, 7):
        for core in (c, 1 - c):
            greet({"seq": seq_of(y, (z + dz) % Z, core)})
    for i in range(1, 4):
        greet({"tp": (tp + i) % 4})

    @pl.when(moves)
    def _():
        greet(partner)

    pl.semaphore_wait(barrier, 22 + jnp.where(moves, 1, 0))

    ids = iter(range(N_SEMS))
    sent = []

    def remote(src, dst, device, i):
        return pltpu.make_async_remote_copy(
            src_ref=src, dst_ref=dst, send_sem=send_sems.at[i], recv_sem=recv_sems.at[i],
            device_id=device, device_id_type=MESH,
        )

    def push(src, dst, device):
        i = next(ids)
        copy = remote(src, dst, device, i)
        copy.start()
        sent.append(copy)
        return i

    def arrived(land, i):
        remote(land, land, sib, i).wait_recv()

    def ring_send(view, t):
        if t < 3:
            a, b = view(zm(t), None), view(zp(t), None)
        else:
            a, b = view(zm(t), 0), view(zp(t), 1)
        return push(a, a, right), push(b, b, left)

    def ring_wait(view, t, got):
        if t < 4:
            arrived(view(zm(t), None), got[0])
            arrived(view(zp(t), None), got[1])
        else:
            arrived(view(zm(t), 0), got[0])
            arrived(view(zp(t), 1), got[1])

    own_rows = pl.ds(pl.multiple_of(c * WROWS, 32), WROWS)
    sib_rows = pl.ds(pl.multiple_of((1 - c) * WROWS, 32), WROWS)
    k_first, y_first = {}, []
    for e, core in enumerate((c, 1 - c)):
        for dz in (1, 7):
            near_by = {"seq": seq_of(y, (z + dz) % Z, core)}
            k_first[dz, e] = push(wsh.at[core, 1], wbuf.at[1, y, z, own_rows], near_by)
        across = {"seq": seq_of(1 - y, z, core)}
        y_first.append(push(wsh.at[core, 1:3], wbuf.at[1:3, y, z, own_rows], across))
    w_sib = push(wsh.at[1 - c], wbuf.at[:, y, z, own_rows], sib)
    w_own = pltpu.make_async_copy(wsh.at[c], wbuf.at[:, y, z, own_rows], load_sems.at[4])
    w_own.start()

    ow_id = next(ids)
    ow_copy = remote(owt, owb.at[seq_of(py, pz, c)], partner, ow_id)
    loads[0].wait()
    loads[1].wait()
    first = s * WROWS
    base = jnp.minimum(first // HEAD * HEAD, D - 2 * HEAD)
    for block in range(2):
        gates = mod[2, block:block + 1, pl.ds(pl.multiple_of(base, HEAD), 2 * HEAD)]
        gates = pltpu.roll(jnp.broadcast_to(gates, (HEAD, 2 * HEAD)), (2 * HEAD + base - first) % (2 * HEAD), 1)
        gates = jnp.transpose(gates[:, :WROWS])
        owt[:, block * HEAD:(block + 1) * HEAD] = (ow[block].astype(F32) * gates).astype(BF16)

    @pl.when(moves)
    def _():
        ow_copy.start()

    @pl.when(jnp.logical_not(moves))
    def _():
        owb[s] = owt[...]

    def layer_norm(block, store, lo, hi):
        use = jnp.where(block == 0, 1.0, 0.0).astype(F32)
        scale = 1.0 + mod[1, pl.ds(block, 1), :]
        shift = mod[0, pl.ds(block, 1), :]

        def step(i, carry):
            at = pl.ds(pl.multiple_of(i * 32, 32), 32)
            v = lat[at, :].astype(F32) + use * cond[at, :].astype(F32)
            center = v - jnp.mean(v, axis=-1, keepdims=True)
            var = jnp.mean(center * center, axis=-1, keepdims=True)
            store(at, (center * lax.rsqrt(var + 1e-6) * scale + shift).astype(BF16))
            return carry

        lax.fori_loop(lo, hi, step, 0)

    def store_stage(at, v):
        xst[at, :] = v

    def store_own(at, v):
        xbuf[c, at, :] = v

    def half(h):
        return slice(None) if h is None else pl.ds(h * WROWS, WROWS)

    def view_q(zz, h):
        return wbuf.at[0, y, zz, half(h)]

    def view_b(zz, h):
        return wbuf.at[1, y, zz, half(h)]

    def view_a(zz, h):
        return wbuf.at[2, :, zz, half(h)]

    def view_o(zz, h):
        base = seq_of(y, zz, c)
        return owb.at[base] if h is None else owb.at[base, pl.ds(h * 48, 48)]

    b_y, q_y = [], []

    def forward(j, zz, kept):
        kept.append((push(wbuf.at[j, y, zz], wbuf.at[j, y, zz], row), wbuf.at[j, 1 - y, zz]))

    w_own.wait()
    arrived(wbuf.at[:, y, z, sib_rows], w_sib)
    for i, rows in zip(y_first, (own_rows, sib_rows)):
        arrived(wbuf.at[1:3, 1 - y, z, rows], i)
    got_a = ring_send(view_a, 0)
    for load in loads[2:]:
        load.wait()
    g = x * 4 + tp
    near = lat[:, pl.ds(pl.multiple_of(g * 3 // 2 * HEAD, HEAD), 2 * HEAD)].astype(F32)
    near = jnp.where(g % 2 == 0, near[:, :2 * WROWS], near[:, HEAD // 2:])
    res[...] = jnp.transpose(near)

    layer_norm(1 - c, store_stage, 0, 4)

    def q_hop(t, got):
        ring_wait(view_q, t, got)
        if t < 4:
            got = ring_send(view_q, t)
            forward(0, zm(t), q_y)
            forward(0, zp(t), q_y)
            return got
        forward(0, zp(t), q_y)

    got_b = None
    for t in range(1, 5):
        if t == 1:
            for dz, zz in ((1, zm(1)), (7, zp(1))):
                for e, rows in enumerate((own_rows, sib_rows)):
                    arrived(wbuf.at[1, y, zz, rows], k_first[dz, e])
        else:
            ring_wait(view_b, t, got_b)
        if t < 4:
            got_b = ring_send(view_b, t)
            forward(1, zm(t), b_y)
            forward(1, zp(t), b_y)
            ring_wait(view_a, t, got_a)
            got_a = ring_send(view_a, t)
            if t == 1:
                got_q = ring_send(view_q, 0)
                forward(0, z, q_y)
                layer_norm(1 - c, store_stage, 4, 8)
                x_sib = push(xst, xbuf.at[c], sib)
            else:
                got_q = q_hop(t - 1, got_q)
                layer_norm(c, store_own, 4 * t - 8, 4 * t - 4)
        else:
            forward(1, zp(t), b_y)
    arrived(xbuf.at[1 - c], x_sib)
    for i, land in b_y:
        arrived(land, i)

    def head_norm(v, g):
        return v * lax.rsqrt(jnp.mean(v * v, axis=-1, keepdims=True) + 1e-6) * g

    q_gain = gain[c, 0:1, :] * (math.log2(math.e) / math.sqrt(HEAD))
    k_gain = gain[c, 1:2, :]

    def project_in(j, m):
        return jnp.dot(xbuf[m], wbuf[j].reshape(D, HEAD), preferred_element_type=F32)

    stays = y == c
    leaves = jnp.logical_not(stays)

    def view_k(zz, h):
        return kbuf.at[c, zz] if h is None else kbuf.at[c, zz, h]

    def view_v(zz, h):
        return vbuf.at[c, zz] if h is None else vbuf.at[c, zz, pl.ds(h * ROWS, ROWS)]

    def first_hop(staged, buf):
        i_diag, i_ring = next(ids), (next(ids), next(ids))
        diag_copy = remote(staged, buf.at[y, z], diag, i_diag)
        mine = buf.at[c, z]
        ring = [remote(mine, mine, device, i) for device, i in zip((right, left), i_ring)]
        sent.extend(ring)

        @pl.when(stays)
        def _():
            buf[y, z] = staged[...]
            for copy in ring:
                copy.start()

        @pl.when(leaves)
        def _():
            diag_copy.start()

        def late():
            @pl.when(leaves)
            def _():
                arrived(mine, i_diag)
                for copy in ring:
                    copy.start()

        return i_ring, diag_copy, late

    for m in range(2):
        kst[m] = jnp.transpose(head_norm(project_in(1, m), k_gain)).astype(BF16)
    got_k, k_diag, late = first_hop(kst, kbuf)
    got_q = q_hop(3, got_q)
    ring_wait(view_a, 4, got_a)
    late_k = late

    @pl.when(moves)
    def _():
        ow_copy.wait_send()
        arrived(owb.at[s], ow_id)

    o_y, o_s = [], []

    def o_pass(zz):
        here, there = owb.at[seq_of(y, zz, c)], owb.at[seq_of(1 - y, zz, c)]
        o_y.append((push(here, here, row), there))
        o_s.append((push(here, here, sib), owb.at[seq_of(y, zz, 1 - c)]))

    def o_hop(t, got):
        ring_wait(view_o, t, got)
        if t < 4:
            got = ring_send(view_o, t)
            o_pass(zm(t))
            o_pass(zp(t))
            return got
        o_pass(zp(t))

    got_o = ring_send(view_o, 0)
    o_pass(z)
    for m in range(2):
        vst[m * ROWS:(m + 1) * ROWS, :] = project_in(2, m).astype(BF16)
    got_v, v_diag, late = first_hop(vst, vbuf)
    late_k()
    late()

    shared = {}

    def share(buf, zz, t):
        mine = buf.at[c, zz]
        shared.setdefault(t, []).append((push(mine, mine, sib), buf.at[1 - c, zz]))

    share(kbuf, z, 0)
    share(vbuf, z, 0)
    q_hop(4, got_q)
    acc[...] = jnp.zeros_like(acc)
    ones = jnp.ones((2 * CHIP, HEAD), BF16)
    for i, land in q_y:
        arrived(land, i)
    for m in range(2):
        qst[m * ROWS:(m + 1) * ROWS, :] = head_norm(project_in(0, m), q_gain).astype(BF16)
    q_id = next(ids)
    q_diag = remote(qst, qbuf, diag, q_id)

    @pl.when(stays)
    def _():
        qbuf[...] = qst[...]

    @pl.when(leaves)
    def _():
        q_diag.start()

    def attend(r, *places):
        values = jnp.concatenate([vbuf[r, zz] for zz in places], axis=0)
        values = jnp.concatenate([values, ones[:len(places) * CHIP]], axis=1)
        for m in range(2):
            at = slice(m * ROWS, (m + 1) * ROWS)
            weights = jnp.concatenate([
                jnp.exp2(jnp.dot(qbuf[at, :], kbuf[r, zz, h], preferred_element_type=F32)).astype(BF16)
                for zz in places for h in range(2)
            ], axis=1)
            acc[at, :] += jnp.dot(weights, values, preferred_element_type=F32)

    def attend_shared(t):
        for i, land in shared[t]:
            arrived(land, i)
        attend(1 - c, *((zm(t), zp(t)) if t % 4 else (zp(t),)))

    for t in range(1, 5):
        ring_wait(view_k, t, got_k)
        if t < 4:
            got_k = ring_send(view_k, t)
            share(kbuf, zm(t), t)
            share(kbuf, zp(t), t)
            ring_wait(view_v, t, got_v)
            got_v = ring_send(view_v, t)
            share(vbuf, zm(t), t)
            share(vbuf, zp(t), t)
            got_o = o_hop(t, got_o)
            if t == 1:
                @pl.when(leaves)
                def _():
                    arrived(qbuf, q_id)

                attend(c, z)
            attend(c, zm(t), zp(t))
            if t == 2:
                attend_shared(0)
            if t == 3:
                attend_shared(1)
                attend_shared(2)
        else:
            share(kbuf, zp(t), t)
            ring_wait(view_v, t, got_v)
            share(vbuf, zp(t), t)
            o_hop(t, got_o)
            attend(c, zp(t))
            attend_shared(3)
            attend_shared(4)

    a_ids, a_copies = [], {}
    for h in range(2):
        i0 = next(ids)
        next(ids)
        a_ids.append(i0)
        for m in range(2):
            lo = m * ROWS + h * HEAD
            part = acc[lo:lo + HEAD, :]
            ast[h, m] = jnp.transpose(part[:, :HEAD] / part[:, HEAD:]).astype(BF16)
            copy = pltpu.make_async_remote_copy(
                src_ref=ast.at[h, m], dst_ref=abuf.at[h, x, y],
                send_sem=send_sems.at[i0 + m], recv_sem=recv_sems.at[i0 + y],
                device_id={"seq": seq_of(c, z, m)}, device_id_type=MESH,
            )
            is_self = jnp.logical_and(stays, c == m)
            a_copies[h, m] = copy, jnp.logical_not(is_self)

            @pl.when(is_self)
            def _():
                abuf[h, x, y] = ast[h, m]

            @pl.when(jnp.logical_not(is_self))
            def _():
                copy.start()

    x_ids = {}
    for h in range(2):
        for k, b in enumerate((y, 1 - y)):
            mine = abuf.at[h, x, b]
            if k:
                arrived(mine, a_ids[h] + b)
            else:
                @pl.when(leaves)
                def _():
                    arrived(mine, a_ids[h] + b)
            for d in (2, 1, 3):
                x_ids[h, k, d] = push(mine, mine, {"grp": (x + d) % 4})

    for i, land in o_y:
        arrived(land, i)
    for zz in range(Z):
        here = owb.at[seq_of(1 - y, zz, c)]
        o_s.append((push(here, here, sib), owb.at[seq_of(1 - y, zz, 1 - c)]))
    for i, land in o_s:
        arrived(land, i)

    def project(h, yh):
        total = None
        for xx in range(4):
            w = owb[pl.ds(xx * 8 + yh * 2, 2)].reshape(2 * WROWS, 2 * HEAD)
            a = abuf[h, xx].reshape(2 * HEAD, HEAD)
            term = jnp.dot(w, a, preferred_element_type=F32)
            total = term if total is None else total + term
        return total

    r_ids, totals = {}, []
    for h in range(2):
        for d in (1, 3, 2):
            for k, b in enumerate((y, 1 - y)):
                arrived(abuf.at[h, (x + 4 - d) % 4, b], x_ids[h, k, d])
        for d in (2, 1, 3):
            yh = (tp + d) % 4
            pst[h, d] = project(h, yh).astype(BF16)
            r_ids[h, d] = push(pst.at[h, d], rbuf.at[h, d], {"tp": yh})
        totals.append(project(h, tp))

    for h in range(2):
        total = totals[h]
        for d in (1, 3, 2):
            arrived(rbuf.at[h, d], r_ids[h, d])
            total = total + rbuf[h, d].astype(F32)
        at = slice(h * HEAD, (h + 1) * HEAD)
        out[:, at] = res[:, at] + total

    for copy in sent:
        copy.wait_send()

    @pl.when(leaves)
    def _():
        for copy in (k_diag, v_diag, q_diag):
            copy.wait_send()

    for copy, remote_target in a_copies.values():
        @pl.when(remote_target)
        def _():
            copy.wait_send()


def body(latent, condition, modulation, qk_gain, qkv_weight, out_weight):
    modulation = jnp.transpose(modulation, (1, 0, 2))
    vm = pl.BlockSpec(memory_space=pltpu.VMEM)
    hbm = pl.BlockSpec(memory_space=pltpu.HBM)
    mixed = pl.pallas_call(
        kernel,
        out_shape=jax.ShapeDtypeStruct((2 * WROWS, ROWS), F32),
        in_specs=[hbm, hbm, hbm, vm, hbm, hbm],
        out_specs=vm,
        scratch_shapes=[
            pltpu.VMEM((ROWS, D), BF16),
            pltpu.VMEM((ROWS, D), BF16),
            pltpu.VMEM((3, 2, D), F32),
            pltpu.VMEM((2, WROWS, HEAD), BF16),
            pltpu.VMEM((WROWS, 2 * HEAD), BF16),
            pltpu.VMEM((3, 2, Z, 2 * WROWS, HEAD), BF16),
            pltpu.VMEM((2, ROWS, D), BF16),
            pltpu.VMEM((ROWS, D), BF16),
            pltpu.VMEM((CHIP, HEAD), BF16),
            pltpu.VMEM((2, Z, 2, HEAD, ROWS), BF16),
            pltpu.VMEM((2, Z, CHIP, HEAD), BF16),
            pltpu.VMEM((2, HEAD, ROWS), BF16),
            pltpu.VMEM((CHIP, HEAD), BF16),
            pltpu.VMEM((CHIP, HEAD), BF16),
            pltpu.VMEM((32, WROWS, 2 * HEAD), BF16),
            pltpu.VMEM((CHIP, 2 * HEAD), F32),
            pltpu.VMEM((2, 4, 2, HEAD, HEAD), BF16),
            pltpu.VMEM((2, 2, HEAD, HEAD), BF16),
            pltpu.VMEM((2, 4, 2 * WROWS, HEAD), BF16),
            pltpu.VMEM((2, 4, 2 * WROWS, HEAD), BF16),
            pltpu.VMEM((2 * WROWS, ROWS), F32),
            pltpu.SemaphoreType.DMA((N_SEMS,)),
            pltpu.SemaphoreType.DMA((N_SEMS,)),
            pltpu.SemaphoreType.DMA((5,)),
        ],
        compiler_params=pltpu.CompilerParams(
            collective_id=0, has_side_effects=True, vmem_limit_bytes=56 * 1024 * 1024
        ),
        cost_estimate=pl.CostEstimate(
            flops=3_900_000_000, bytes_accessed=4_000_000, transcendentals=4_200_000
        ),
    )(latent, condition, modulation, qk_gain, qkv_weight, jnp.transpose(out_weight, (0, 2, 1)))
    return mixed.astype(BF16).T


def solution(mesh):
    return jax.shard_map(
        body,
        mesh=mesh,
        in_specs=(
            P("seq", None),
            P("seq", None),
            P(),
            P(),
            P(None, None, "seq", ("grp", "tp")),
            P(None, ("grp", "tp"), "seq"),
        ),
        out_specs=P("seq", ("grp", "tp")),
        check_vma=False,
    )
```

```python
import math

import jax
import jax.numpy as jnp
from jax import lax
from jax.experimental import pallas as pl
from jax.experimental.pallas import tpu as pltpu
from jax.sharding import PartitionSpec as P

MESH = pl.DeviceIdType.MESH
BF16, F32 = jnp.bfloat16, jnp.float32
Z = 8
ROWS = 256
CHIP = 2 * ROWS
D = 3072
HEAD = 128
WROWS = 96
N_SEMS = 200


def kernel(
    lat_in, cond_in, mod_in, gain, wsh, ow_in, out,
    lat, cond, mod, ow, owt, wbuf, xbuf, xst, qbuf, kbuf, vbuf, kst, vst, qst, owb, acc, abuf, ast, pst, rbuf, res,
    send_sems, recv_sems, load_sems,
):
    loads = []
    for i, (a, b) in enumerate(((ow_in, ow), (mod_in, mod), (lat_in, lat), (cond_in, cond))):
        loads.append(pltpu.make_async_copy(a, b, load_sems.at[i]))
        loads[-1].start()
    x, s, tp = lax.axis_index("grp"), lax.axis_index("seq"), lax.axis_index("tp")
    y, z, c = s // 16, (s // 2) % 8, s % 2

    def seq_of(y_, z_, c_):
        return y_ * 16 + z_ * 2 + c_

    sib = {"seq": seq_of(y, z, 1 - c)}
    row = {"seq": seq_of(1 - y, z, c)}
    diag = {"seq": seq_of(1 - y, z, 1 - c)}
    right = {"seq": seq_of(y, (z + 1) % Z, c)}
    left = {"seq": seq_of(y, (z + 7) % Z, c)}

    def zm(t):
        return (z + Z - t) % Z

    def zp(t):
        return (z + t) % Z

    px, py, pz = y * 2 + z // 4, x // 2, z % 4 + 4 * (x % 2)
    moves = px != x
    partner = {"grp": px, "seq": seq_of(py, pz, c)}

    barrier = pltpu.get_barrier_semaphore()

    def greet(device):
        pl.semaphore_signal(barrier, inc=1, device_id=device, device_id_type=MESH)

    flat = x * 4 + y * 2 + c
    for i in range(1, 16):
        f = (flat + i) % 16
        greet({"grp": f // 4, "seq": seq_of((f // 2) % 2, z, f % 2)})
    for dz in (1, 7):
        for core in (c, 1 - c):
            greet({"seq": seq_of(y, (z + dz) % Z, core)})
    for i in range(1, 4):
        greet({"tp": (tp + i) % 4})

    @pl.when(moves)
    def _():
        greet(partner)

    pl.semaphore_wait(barrier, 22 + jnp.where(moves, 1, 0))

    ids = iter(range(N_SEMS))
    sent = []

    def remote(src, dst, device, i):
        return pltpu.make_async_remote_copy(
            src_ref=src, dst_ref=dst, send_sem=send_sems.at[i], recv_sem=recv_sems.at[i],
            device_id=device, device_id_type=MESH,
        )

    def push(src, dst, device):
        i = next(ids)
        copy = remote(src, dst, device, i)
        copy.start()
        sent.append(copy)
        return i

    def arrived(land, i):
        remote(land, land, sib, i).wait_recv()

    def ring_send(view, t):
        if t < 3:
            a, b = view(zm(t), None), view(zp(t), None)
        else:
            a, b = view(zm(t), 0), view(zp(t), 1)
        return push(a, a, right), push(b, b, left)

    def ring_wait(view, t, got):
        if t < 4:
            arrived(view(zm(t), None), got[0])
            arrived(view(zp(t), None), got[1])
        else:
            arrived(view(zm(t), 0), got[0])
            arrived(view(zp(t), 1), got[1])

    own_rows = pl.ds(pl.multiple_of(c * WROWS, 32), WROWS)
    sib_rows = pl.ds(pl.multiple_of((1 - c) * WROWS, 32), WROWS)
    k_first, y_first = {}, []
    for e, core in enumerate((c, 1 - c)):
        for dz in (1, 7):
            near_by = {"seq": seq_of(y, (z + dz) % Z, core)}
            k_first[dz, e] = push(wsh.at[core, 1], wbuf.at[1, y, z, own_rows], near_by)
        across = {"seq": seq_of(1 - y, z, core)}
        y_first.append(push(wsh.at[core, 1:3], wbuf.at[1:3, y, z, own_rows], across))
    w_sib = push(wsh.at[1 - c], wbuf.at[:, y, z, own_rows], sib)
    w_own = pltpu.make_async_copy(wsh.at[c], wbuf.at[:, y, z, own_rows], load_sems.at[4])
    w_own.start()

    ow_id = next(ids)
    ow_copy = remote(owt, owb.at[seq_of(py, pz, c)], partner, ow_id)
    loads[0].wait()
    loads[1].wait()
    first = s * WROWS
    base = jnp.minimum(first // HEAD * HEAD, D - 2 * HEAD)
    for block in range(2):
        gates = mod[2, block:block + 1, pl.ds(pl.multiple_of(base, HEAD), 2 * HEAD)]
        gates = pltpu.roll(jnp.broadcast_to(gates, (HEAD, 2 * HEAD)), (2 * HEAD + base - first) % (2 * HEAD), 1)
        gates = jnp.transpose(gates[:, :WROWS])
        owt[:, block * HEAD:(block + 1) * HEAD] = (ow[block].astype(F32) * gates).astype(BF16)

    @pl.when(moves)
    def _():
        ow_copy.start()

    @pl.when(jnp.logical_not(moves))
    def _():
        owb[s] = owt[...]

    def layer_norm(block, store, lo, hi):
        use = jnp.where(block == 0, 1.0, 0.0).astype(F32)
        scale = 1.0 + mod[1, pl.ds(block, 1), :]
        shift = mod[0, pl.ds(block, 1), :]

        def step(i, carry):
            at = pl.ds(pl.multiple_of(i * 32, 32), 32)
            v = lat[at, :].astype(F32) + use * cond[at, :].astype(F32)
            center = v - jnp.mean(v, axis=-1, keepdims=True)
            var = jnp.mean(center * center, axis=-1, keepdims=True)
            store(at, (center * lax.rsqrt(var + 1e-6) * scale + shift).astype(BF16))
            return carry

        lax.fori_loop(lo, hi, step, 0)

    def store_stage(at, v):
        xst[at, :] = v

    def store_own(at, v):
        xbuf[c, at, :] = v

    def half(h):
        return slice(None) if h is None else pl.ds(h * WROWS, WROWS)

    def view_q(zz, h):
        return wbuf.at[0, y, zz, half(h)]

    def view_b(zz, h):
        return wbuf.at[1, y, zz, half(h)]

    def view_a(zz, h):
        return wbuf.at[2, :, zz, half(h)]

    def view_o(zz, h):
        base = seq_of(y, zz, c)
        return owb.at[base] if h is None else owb.at[base, pl.ds(h * 48, 48)]

    b_y, q_y = [], []

    def forward(j, zz, kept):
        kept.append((push(wbuf.at[j, y, zz], wbuf.at[j, y, zz], row), wbuf.at[j, 1 - y, zz]))

    w_own.wait()
    arrived(wbuf.at[:, y, z, sib_rows], w_sib)
    for i, rows in zip(y_first, (own_rows, sib_rows)):
        arrived(wbuf.at[1:3, 1 - y, z, rows], i)
    got_a = ring_send(view_a, 0)
    for load in loads[2:]:
        load.wait()
    g = x * 4 + tp
    near = lat[:, pl.ds(pl.multiple_of(g * 3 // 2 * HEAD, HEAD), 2 * HEAD)].astype(F32)
    near = jnp.where(g % 2 == 0, near[:, :2 * WROWS], near[:, HEAD // 2:])
    res[...] = jnp.transpose(near)

    layer_norm(1 - c, store_stage, 0, 4)

    def q_hop(t, got):
        ring_wait(view_q, t, got)
        if t < 4:
            got = ring_send(view_q, t)
            forward(0, zm(t), q_y)
            forward(0, zp(t), q_y)
            return got
        forward(0, zp(t), q_y)

    got_b = None
    for t in range(1, 5):
        if t == 1:
            for dz, zz in ((1, zm(1)), (7, zp(1))):
                for e, rows in enumerate((own_rows, sib_rows)):
                    arrived(wbuf.at[1, y, zz, rows], k_first[dz, e])
        else:
            ring_wait(view_b, t, got_b)
        if t < 4:
            got_b = ring_send(view_b, t)
            forward(1, zm(t), b_y)
            forward(1, zp(t), b_y)
            ring_wait(view_a, t, got_a)
            got_a = ring_send(view_a, t)
            if t == 1:
                got_q = ring_send(view_q, 0)
                forward(0, z, q_y)
                layer_norm(1 - c, store_stage, 4, 8)
                x_sib = push(xst, xbuf.at[c], sib)
            else:
                got_q = q_hop(t - 1, got_q)
                layer_norm(c, store_own, 4 * t - 8, 4 * t - 4)
        else:
            forward(1, zp(t), b_y)
    arrived(xbuf.at[1 - c], x_sib)
    for i, land in b_y:
        arrived(land, i)

    def head_norm(v, g):
        return v * lax.rsqrt(jnp.mean(v * v, axis=-1, keepdims=True) + 1e-6) * g

    q_gain = gain[c, 0:1, :] * (math.log2(math.e) / math.sqrt(HEAD))
    k_gain = gain[c, 1:2, :]

    def project_in(j, store):
        def step(m, carry):
            store(m, jnp.dot(xbuf[m], wbuf[j].reshape(D, HEAD), preferred_element_type=F32))
            return carry

        lax.fori_loop(0, 2, step, 0)

    def rows_of(m):
        return pl.ds(pl.multiple_of(m * ROWS, ROWS), ROWS)

    def store_k(m, v):
        kst[m] = jnp.transpose(head_norm(v, k_gain)).astype(BF16)

    def store_v(m, v):
        vst[rows_of(m), :] = v.astype(BF16)

    def store_q(m, v):
        qst[rows_of(m), :] = head_norm(v, q_gain).astype(BF16)

    stays = y == c
    leaves = jnp.logical_not(stays)

    def view_k(zz, h):
        return kbuf.at[c, zz] if h is None else kbuf.at[c, zz, h]

    def view_v(zz, h):
        return vbuf.at[c, zz] if h is None else vbuf.at[c, zz, pl.ds(h * ROWS, ROWS)]

    def first_hop(staged, buf):
        i_diag, i_ring = next(ids), (next(ids), next(ids))
        diag_copy = remote(staged, buf.at[y, z], diag, i_diag)
        mine = buf.at[c, z]
        ring = [remote(mine, mine, device, i) for device, i in zip((right, left), i_ring)]
        sent.extend(ring)

        @pl.when(stays)
        def _():
            buf[y, z] = staged[...]
            for copy in ring:
                copy.start()

        @pl.when(leaves)
        def _():
            diag_copy.start()

        def late():
            @pl.when(leaves)
            def _():
                arrived(mine, i_diag)
                for copy in ring:
                    copy.start()

        return i_ring, diag_copy, late

    project_in(1, store_k)
    got_k, k_diag, late = first_hop(kst, kbuf)
    got_q = q_hop(3, got_q)
    ring_wait(view_a, 4, got_a)
    late_k = late

    @pl.when(moves)
    def _():
        ow_copy.wait_send()
        arrived(owb.at[s], ow_id)

    o_y, o_s = [], []

    def o_pass(zz):
        here, there = owb.at[seq_of(y, zz, c)], owb.at[seq_of(1 - y, zz, c)]
        o_y.append((push(here, here, row), there))
        o_s.append((push(here, here, sib), owb.at[seq_of(y, zz, 1 - c)]))

    def o_hop(t, got):
        ring_wait(view_o, t, got)
        if t < 4:
            got = ring_send(view_o, t)
            o_pass(zm(t))
            o_pass(zp(t))
            return got
        o_pass(zp(t))

    got_o = ring_send(view_o, 0)
    o_pass(z)
    project_in(2, store_v)
    got_v, v_diag, late = first_hop(vst, vbuf)
    late_k()
    late()

    shared = {}

    def share(buf, zz, t):
        mine = buf.at[c, zz]
        shared.setdefault(t, []).append((push(mine, mine, sib), buf.at[1 - c, zz]))

    share(kbuf, z, 0)
    share(vbuf, z, 0)
    q_hop(4, got_q)
    acc[...] = jnp.zeros_like(acc)
    ones = jnp.ones((2 * CHIP, HEAD), BF16)
    for i, land in q_y:
        arrived(land, i)
    project_in(0, store_q)
    q_id = next(ids)
    q_diag = remote(qst, qbuf, diag, q_id)

    @pl.when(stays)
    def _():
        qbuf[...] = qst[...]

    @pl.when(leaves)
    def _():
        q_diag.start()

    def attend(r, first_t, count):
        def step(i, carry):
            t = first_t + i // 2
            at = rows_of(i % 2)
            places = zp(t - 1), (z + Z - t) % Z
            values = jnp.concatenate([vbuf[r, zz] for zz in places], axis=0)
            weights = jnp.concatenate([
                jnp.exp2(jnp.dot(qbuf[at, :], kbuf[r, zz, h], preferred_element_type=F32)).astype(BF16)
                for zz in places for h in range(2)
            ], axis=1)
            acc[at, :] += jnp.dot(
                weights, jnp.concatenate([values, ones], axis=1), preferred_element_type=F32
            )
            return carry

        lax.fori_loop(0, 2 * count, step, 0)

    def shared_come(t):
        for i, land in shared[t]:
            arrived(land, i)

    for t in range(1, 5):
        ring_wait(view_k, t, got_k)
        if t < 4:
            got_k = ring_send(view_k, t)
            share(kbuf, zm(t), t)
            share(kbuf, zp(t), t)
            ring_wait(view_v, t, got_v)
            got_v = ring_send(view_v, t)
            share(vbuf, zm(t), t)
            share(vbuf, zp(t), t)
            got_o = o_hop(t, got_o)
            if t == 1:
                @pl.when(leaves)
                def _():
                    arrived(qbuf, q_id)

                attend(c, 1, 1)
            else:
                attend(c, t, 1)
                if t == 2:
                    shared_come(0)
                shared_come(t - 1)
                attend(1 - c, t - 1, 1)
        else:
            share(kbuf, zp(t), t)
            ring_wait(view_v, t, got_v)
            share(vbuf, zp(t), t)
            o_hop(t, got_o)
            attend(c, 4, 1)
            shared_come(3)
            shared_come(4)
            attend(1 - c, 3, 2)

    a_ids, a_copies = [], {}
    for h in range(2):
        i0 = next(ids)
        next(ids)
        a_ids.append(i0)
        for m in range(2):
            lo = m * ROWS + h * HEAD
            part = acc[lo:lo + HEAD, :]
            ast[h, m] = jnp.transpose(part[:, :HEAD] / part[:, HEAD:]).astype(BF16)
            copy = pltpu.make_async_remote_copy(
                src_ref=ast.at[h, m], dst_ref=abuf.at[h, x, y],
                send_sem=send_sems.at[i0 + m], recv_sem=recv_sems.at[i0 + y],
                device_id={"seq": seq_of(c, z, m)}, device_id_type=MESH,
            )
            is_self = jnp.logical_and(stays, c == m)
            a_copies[h, m] = copy, jnp.logical_not(is_self)

            @pl.when(is_self)
            def _():
                abuf[h, x, y] = ast[h, m]

            @pl.when(jnp.logical_not(is_self))
            def _():
                copy.start()

    x_ids = {}
    for h in range(2):
        for k, b in enumerate((y, 1 - y)):
            mine = abuf.at[h, x, b]
            if k:
                arrived(mine, a_ids[h] + b)
            else:
                @pl.when(leaves)
                def _():
                    arrived(mine, a_ids[h] + b)
            for d in (2, 1, 3):
                x_ids[h, k, d] = push(mine, mine, {"grp": (x + d) % 4})

    for i, land in o_y:
        arrived(land, i)
    for zz in range(Z):
        here = owb.at[seq_of(1 - y, zz, c)]
        o_s.append((push(here, here, sib), owb.at[seq_of(1 - y, zz, 1 - c)]))
    for i, land in o_s:
        arrived(land, i)

    def project(h, yh):
        total = None
        for xx in range(4):
            w = owb[pl.ds(xx * 8 + yh * 2, 2)].reshape(2 * WROWS, 2 * HEAD)
            a = abuf[h, xx].reshape(2 * HEAD, HEAD)
            term = jnp.dot(w, a, preferred_element_type=F32)
            total = term if total is None else total + term
        return total

    r_ids, totals = {}, []
    for h in range(2):
        for d in (1, 3, 2):
            for k, b in enumerate((y, 1 - y)):
                arrived(abuf.at[h, (x + 4 - d) % 4, b], x_ids[h, k, d])
        r_ids[h] = [next(ids) for _ in range(3)][0] - 1

        def piece(h, d):
            return remote(pst.at[h, d], rbuf.at[h, d], {"tp": (tp + d) % 4}, r_ids[h] + d)

        def step(i, carry):
            d = 1 + (i + 1) % 3
            pst[h, d] = project(h, (tp + d) % 4).astype(BF16)
            piece(h, d).start()
            return carry

        lax.fori_loop(0, 3, step, 0)
        totals.append(project(h, tp))

    for h in range(2):
        total = totals[h]
        for d in (1, 3, 2):
            arrived(rbuf.at[h, d], r_ids[h] + d)
            total = total + rbuf[h, d].astype(F32)
        at = slice(h * HEAD, (h + 1) * HEAD)
        out[:, at] = res[:, at] + total

    for copy in sent:
        copy.wait_send()
    for h in range(2):
        for d in range(1, 4):
            piece(h, d).wait_send()

    @pl.when(leaves)
    def _():
        for copy in (k_diag, v_diag, q_diag):
            copy.wait_send()

    for copy, remote_target in a_copies.values():
        @pl.when(remote_target)
        def _():
            copy.wait_send()


def body(latent, condition, modulation, qk_gain, qkv_weight, out_weight):
    modulation = jnp.transpose(modulation, (1, 0, 2))
    vm = pl.BlockSpec(memory_space=pltpu.VMEM)
    hbm = pl.BlockSpec(memory_space=pltpu.HBM)
    mixed = pl.pallas_call(
        kernel,
        out_shape=jax.ShapeDtypeStruct((2 * WROWS, ROWS), F32),
        in_specs=[hbm, hbm, hbm, vm, hbm, hbm],
        out_specs=vm,
        scratch_shapes=[
            pltpu.VMEM((ROWS, D), BF16),
            pltpu.VMEM((ROWS, D), BF16),
            pltpu.VMEM((3, 2, D), F32),
            pltpu.VMEM((2, WROWS, HEAD), BF16),
            pltpu.VMEM((WROWS, 2 * HEAD), BF16),
            pltpu.VMEM((3, 2, Z, 2 * WROWS, HEAD), BF16),
            pltpu.VMEM((2, ROWS, D), BF16),
            pltpu.VMEM((ROWS, D), BF16),
            pltpu.VMEM((CHIP, HEAD), BF16),
            pltpu.VMEM((2, Z, 2, HEAD, ROWS), BF16),
            pltpu.VMEM((2, Z, CHIP, HEAD), BF16),
            pltpu.VMEM((2, HEAD, ROWS), BF16),
            pltpu.VMEM((CHIP, HEAD), BF16),
            pltpu.VMEM((CHIP, HEAD), BF16),
            pltpu.VMEM((32, WROWS, 2 * HEAD), BF16),
            pltpu.VMEM((CHIP, 2 * HEAD), F32),
            pltpu.VMEM((2, 4, 2, HEAD, HEAD), BF16),
            pltpu.VMEM((2, 2, HEAD, HEAD), BF16),
            pltpu.VMEM((2, 4, 2 * WROWS, HEAD), BF16),
            pltpu.VMEM((2, 4, 2 * WROWS, HEAD), BF16),
            pltpu.VMEM((2 * WROWS, ROWS), F32),
            pltpu.SemaphoreType.DMA((N_SEMS,)),
            pltpu.SemaphoreType.DMA((N_SEMS,)),
            pltpu.SemaphoreType.DMA((5,)),
        ],
        compiler_params=pltpu.CompilerParams(
            collective_id=0, has_side_effects=True, vmem_limit_bytes=56 * 1024 * 1024
        ),
        cost_estimate=pl.CostEstimate(
            flops=3_900_000_000, bytes_accessed=4_000_000, transcendentals=4_200_000
        ),
    )(latent, condition, modulation, qk_gain, qkv_weight, jnp.transpose(out_weight, (0, 2, 1)))
    return mixed.astype(BF16).T


def solution(mesh):
    return jax.shard_map(
        body,
        mesh=mesh,
        in_specs=(
            P("seq", None),
            P("seq", None),
            P(),
            P(),
            P(None, None, "seq", ("grp", "tp")),
            P(None, ("grp", "tp"), "seq"),
        ),
        out_specs=P("seq", ("grp", "tp")),
        check_vma=False,
    )
```

```python
import math

import jax
import jax.numpy as jnp
from jax import lax
from jax.experimental import pallas as pl
from jax.experimental.pallas import tpu as pltpu
from jax.sharding import PartitionSpec as P

MESH = pl.DeviceIdType.MESH
BF16, F32 = jnp.bfloat16, jnp.float32
Z = 8
ROWS = 256
CHIP = 2 * ROWS
D = 3072
HEAD = 128
WROWS = 96
N_SEMS = 200


def kernel(
    lat_in, cond_in, mod_in, gain, wsh, ow_in, out,
    lat, cond, mod, ow, owt, wbuf, xbuf, xst, qbuf, kbuf, vbuf, kst, vst, qst, owb, acc, abuf, ast, pst, rbuf, res,
    send_sems, recv_sems, load_sems,
):
    loads = []
    for i, (a, b) in enumerate(((ow_in, ow), (mod_in, mod), (lat_in, lat), (cond_in, cond))):
        loads.append(pltpu.make_async_copy(a, b, load_sems.at[i]))
        loads[-1].start()
    x, s, tp = lax.axis_index("grp"), lax.axis_index("seq"), lax.axis_index("tp")
    y, z, c = s // 16, (s // 2) % 8, s % 2

    def seq_of(y_, z_, c_):
        return y_ * 16 + z_ * 2 + c_

    sib = {"seq": seq_of(y, z, 1 - c)}
    row = {"seq": seq_of(1 - y, z, c)}
    diag = {"seq": seq_of(1 - y, z, 1 - c)}
    right = {"seq": seq_of(y, (z + 1) % Z, c)}
    left = {"seq": seq_of(y, (z + 7) % Z, c)}

    def zm(t):
        return (z + Z - t) % Z

    def zp(t):
        return (z + t) % Z

    px, py, pz = y * 2 + z // 4, x // 2, z % 4 + 4 * (x % 2)
    moves = px != x
    partner = {"grp": px, "seq": seq_of(py, pz, c)}

    barrier = pltpu.get_barrier_semaphore()

    def greet(device):
        pl.semaphore_signal(barrier, inc=1, device_id=device, device_id_type=MESH)

    flat = x * 4 + y * 2 + c
    for i in range(1, 16):
        f = (flat + i) % 16
        greet({"grp": f // 4, "seq": seq_of((f // 2) % 2, z, f % 2)})
    for dz in (1, 7):
        for core in (c, 1 - c):
            greet({"seq": seq_of(y, (z + dz) % Z, core)})
    for i in range(1, 4):
        greet({"tp": (tp + i) % 4})

    @pl.when(moves)
    def _():
        greet(partner)

    pl.semaphore_wait(barrier, 22 + jnp.where(moves, 1, 0))

    ids = iter(range(N_SEMS))
    sent = []

    def remote(src, dst, device, i):
        return pltpu.make_async_remote_copy(
            src_ref=src, dst_ref=dst, send_sem=send_sems.at[i], recv_sem=recv_sems.at[i],
            device_id=device, device_id_type=MESH,
        )

    def push(src, dst, device):
        i = next(ids)
        copy = remote(src, dst, device, i)
        copy.start()
        sent.append(copy)
        return i

    def arrived(land, i):
        remote(land, land, sib, i).wait_recv()

    def ring_send(view, t):
        if t < 3:
            a, b = view(zm(t), None), view(zp(t), None)
        else:
            a, b = view(zm(t), 0), view(zp(t), 1)
        return push(a, a, right), push(b, b, left)

    def ring_wait(view, t, got):
        if t < 4:
            arrived(view(zm(t), None), got[0])
            arrived(view(zp(t), None), got[1])
        else:
            arrived(view(zm(t), 0), got[0])
            arrived(view(zp(t), 1), got[1])

    own_rows = pl.ds(pl.multiple_of(c * WROWS, 32), WROWS)
    sib_rows = pl.ds(pl.multiple_of((1 - c) * WROWS, 32), WROWS)
    k_first, y_first = {}, []
    for e, core in enumerate((c, 1 - c)):
        for dz in (1, 7):
            near_by = {"seq": seq_of(y, (z + dz) % Z, core)}
            k_first[dz, e] = push(wsh.at[core, 1], wbuf.at[1, y, z, own_rows], near_by)
        across = {"seq": seq_of(1 - y, z, core)}
        y_first.append(push(wsh.at[core, 1:3], wbuf.at[1:3, y, z, own_rows], across))
    w_sib = push(wsh.at[1 - c], wbuf.at[:, y, z, own_rows], sib)
    w_own = pltpu.make_async_copy(wsh.at[c], wbuf.at[:, y, z, own_rows], load_sems.at[4])
    w_own.start()

    ow_id = next(ids)
    ow_copy = remote(owt, owb.at[seq_of(py, pz, c)], partner, ow_id)
    loads[0].wait()
    loads[1].wait()
    first = s * WROWS
    base = jnp.minimum(first // HEAD * HEAD, D - 2 * HEAD)
    for block in range(2):
        gates = mod[2, block:block + 1, pl.ds(pl.multiple_of(base, HEAD), 2 * HEAD)]
        gates = pltpu.roll(jnp.broadcast_to(gates, (HEAD, 2 * HEAD)), (2 * HEAD + base - first) % (2 * HEAD), 1)
        gates = jnp.transpose(gates[:, :WROWS])
        owt[:, block * HEAD:(block + 1) * HEAD] = (ow[block].astype(F32) * gates).astype(BF16)

    @pl.when(moves)
    def _():
        ow_copy.start()

    @pl.when(jnp.logical_not(moves))
    def _():
        owb[s] = owt[...]

    def layer_norm(block, store, lo, hi):
        use = jnp.where(block == 0, 1.0, 0.0).astype(F32)
        scale = 1.0 + mod[1, pl.ds(block, 1), :]
        shift = mod[0, pl.ds(block, 1), :]

        def step(i, carry):
            at = pl.ds(pl.multiple_of(i * 32, 32), 32)
            v = lat[at, :].astype(F32) + use * cond[at, :].astype(F32)
            center = v - jnp.mean(v, axis=-1, keepdims=True)
            var = jnp.mean(center * center, axis=-1, keepdims=True)
            store(at, (center * lax.rsqrt(var + 1e-6) * scale + shift).astype(BF16))
            return carry

        lax.fori_loop(lo, hi, step, 0)

    def store_stage(at, v):
        xst[at, :] = v

    def store_own(at, v):
        xbuf[c, at, :] = v

    def half(h):
        return slice(None) if h is None else pl.ds(h * WROWS, WROWS)

    def view_q(zz, h):
        return wbuf.at[0, y, zz, half(h)]

    def view_b(zz, h):
        return wbuf.at[1, y, zz, half(h)]

    def view_a(zz, h):
        return wbuf.at[2, :, zz, half(h)]

    def view_o(zz, h):
        base = seq_of(y, zz, c)
        return owb.at[base] if h is None else owb.at[base, pl.ds(h * 48, 48)]

    b_y, q_y = [], []

    def forward(j, zz, kept):
        kept.append((push(wbuf.at[j, y, zz], wbuf.at[j, y, zz], row), wbuf.at[j, 1 - y, zz]))

    w_own.wait()
    arrived(wbuf.at[:, y, z, sib_rows], w_sib)
    for i, rows in zip(y_first, (own_rows, sib_rows)):
        arrived(wbuf.at[1:3, 1 - y, z, rows], i)
    got_a = ring_send(view_a, 0)
    for load in loads[2:]:
        load.wait()
    g = x * 4 + tp
    near = lat[:, pl.ds(pl.multiple_of(g * 3 // 2 * HEAD, HEAD), 2 * HEAD)].astype(F32)
    near = jnp.where(g % 2 == 0, near[:, :2 * WROWS], near[:, HEAD // 2:])
    res[...] = jnp.transpose(near)

    layer_norm(1 - c, store_stage, 0, 4)

    def q_hop(t, got):
        ring_wait(view_q, t, got)
        if t < 4:
            got = ring_send(view_q, t)
            forward(0, zm(t), q_y)
            forward(0, zp(t), q_y)
            return got
        forward(0, zp(t), q_y)

    got_b = None
    for t in range(1, 5):
        if t == 1:
            for dz, zz in ((1, zm(1)), (7, zp(1))):
                for e, rows in enumerate((own_rows, sib_rows)):
                    arrived(wbuf.at[1, y, zz, rows], k_first[dz, e])
        else:
            ring_wait(view_b, t, got_b)
        if t < 4:
            got_b = ring_send(view_b, t)
            forward(1, zm(t), b_y)
            forward(1, zp(t), b_y)
            ring_wait(view_a, t, got_a)
            got_a = ring_send(view_a, t)
            if t == 1:
                got_q = ring_send(view_q, 0)
                forward(0, z, q_y)
                layer_norm(1 - c, store_stage, 4, 8)
                x_sib = push(xst, xbuf.at[c], sib)
            else:
                got_q = q_hop(t - 1, got_q)
                layer_norm(c, store_own, 4 * t - 8, 4 * t - 4)
        else:
            forward(1, zp(t), b_y)
    arrived(xbuf.at[1 - c], x_sib)
    for i, land in b_y:
        arrived(land, i)

    def head_norm(v, g):
        return v * lax.rsqrt(jnp.mean(v * v, axis=-1, keepdims=True) + 1e-6) * g

    q_gain = gain[c, 0:1, :] * (math.log2(math.e) / math.sqrt(HEAD))
    k_gain = gain[c, 1:2, :]

    def project_in(j, store):
        def step(m, carry):
            store(m, jnp.dot(xbuf[m], wbuf[j].reshape(D, HEAD), preferred_element_type=F32))
            return carry

        lax.fori_loop(0, 2, step, 0)

    def rows_of(m):
        return pl.ds(pl.multiple_of(m * ROWS, ROWS), ROWS)

    def store_k(m, v):
        kst[m] = jnp.transpose(head_norm(v, k_gain)).astype(BF16)

    def store_v(m, v):
        vst[rows_of(m), :] = v.astype(BF16)

    def store_q(m, v):
        v = head_norm(v, q_gain).astype(BF16)
        for h in range(2):
            qst[h, m] = v[h * HEAD:(h + 1) * HEAD]

    stays = y == c
    leaves = jnp.logical_not(stays)

    def view_k(zz, h):
        return kbuf.at[c, zz] if h is None else kbuf.at[c, zz, h]

    def view_v(zz, h):
        return vbuf.at[c, zz] if h is None else vbuf.at[c, zz, pl.ds(h * ROWS, ROWS)]

    def first_hop(staged, buf):
        i_diag, i_ring = next(ids), (next(ids), next(ids))
        diag_copy = remote(staged, buf.at[y, z], diag, i_diag)
        mine = buf.at[c, z]
        ring = [remote(mine, mine, device, i) for device, i in zip((right, left), i_ring)]
        sent.extend(ring)

        @pl.when(stays)
        def _():
            buf[y, z] = staged[...]
            for copy in ring:
                copy.start()

        @pl.when(leaves)
        def _():
            diag_copy.start()

        def late():
            @pl.when(leaves)
            def _():
                arrived(mine, i_diag)
                for copy in ring:
                    copy.start()

        return i_ring, diag_copy, late

    project_in(1, store_k)
    got_k, k_diag, late = first_hop(kst, kbuf)
    got_q = q_hop(3, got_q)
    ring_wait(view_a, 4, got_a)
    late_k = late

    @pl.when(moves)
    def _():
        ow_copy.wait_send()
        arrived(owb.at[s], ow_id)

    o_y, o_s = [], []

    def o_pass(zz):
        here, there = owb.at[seq_of(y, zz, c)], owb.at[seq_of(1 - y, zz, c)]
        o_y.append((push(here, here, row), there))
        o_s.append((push(here, here, sib), owb.at[seq_of(y, zz, 1 - c)]))

    def o_hop(t, got):
        ring_wait(view_o, t, got)
        if t < 4:
            got = ring_send(view_o, t)
            o_pass(zm(t))
            o_pass(zp(t))
            return got
        o_pass(zp(t))

    got_o = ring_send(view_o, 0)
    o_pass(z)
    project_in(2, store_v)
    got_v, v_diag, late = first_hop(vst, vbuf)
    late_k()
    late()

    shared = {}

    def share(buf, zz, t):
        mine = buf.at[c, zz]
        shared.setdefault(t, []).append((push(mine, mine, sib), buf.at[1 - c, zz]))

    share(kbuf, z, 0)
    share(vbuf, z, 0)
    def k_hop(t, got):
        ring_wait(view_k, t, got)
        if t < 4:
            got = ring_send(view_k, t)
            share(kbuf, zm(t), t)
        share(kbuf, zp(t), t)
        return got

    def v_hop(t, got):
        ring_wait(view_v, t, got)
        if t < 4:
            got = ring_send(view_v, t)
            share(vbuf, zm(t), t)
        share(vbuf, zp(t), t)
        return got

    got_k = k_hop(1, got_k)
    q_hop(4, got_q)
    acc[...] = jnp.zeros_like(acc)
    ones = jnp.ones((CHIP, HEAD), BF16)
    for i, land in q_y:
        arrived(land, i)
    got_v = v_hop(1, got_v)
    project_in(0, store_q)
    q_id = next(ids)
    q_diag = remote(qst, qbuf, diag, q_id)

    @pl.when(stays)
    def _():
        qbuf[...] = qst[...]

    @pl.when(leaves)
    def _():
        q_diag.start()

    def attend(places, halves=(0, 2)):
        lo, hi = halves
        at = slice(lo * ROWS, hi * ROWS)
        queries = qbuf[lo:hi].reshape((hi - lo) * ROWS, HEAD)
        weights = jnp.concatenate([
            jnp.exp2(jnp.dot(queries, kbuf[r, zz, h], preferred_element_type=F32)).astype(BF16)
            for r, zz in places for h in range(2)
        ], axis=1)
        values = jnp.concatenate([
            jnp.concatenate([vbuf[r, zz], ones], axis=1) for r, zz in places
        ], axis=0)
        acc[at, :] += jnp.dot(weights, values, preferred_element_type=F32)

    def shared_come(t):
        for i, land in shared[t]:
            arrived(land, i)

    for t in range(1, 5):
        if t > 1:
            got_k = k_hop(t, got_k)
            got_v = v_hop(t, got_v)
        got_o = o_hop(t, got_o)
        if t == 1:
            @pl.when(leaves)
            def _():
                arrived(qbuf, q_id)

            attend([(c, z), (c, zm(1)), (c, zp(1))])
        if t == 2:
            attend([(c, zm(2)), (c, zp(2))])
            shared_come(0)
            attend([(1 - c, z)])
        if t == 3:
            attend([(c, zm(3)), (c, zp(3))])
            for back in (1, 2):
                shared_come(back)
                attend([(1 - c, zm(back)), (1 - c, zp(back))])
    attend([(c, zp(4))])
    shared_come(3)
    shared_come(4)

    def attend_last(h):
        attend([(1 - c, zm(3)), (1 - c, zp(3)), (1 - c, zp(4))], (h, h + 1))

    a_ids, a_copies = [], {}
    for h in range(2):
        attend_last(h)
        i0 = next(ids)
        next(ids)
        a_ids.append(i0)
        for m in range(2):
            lo = h * ROWS + m * HEAD
            part = acc[lo:lo + HEAD, :]
            ast[h, m] = jnp.transpose(part[:, :HEAD] / part[:, HEAD:]).astype(BF16)
            copy = pltpu.make_async_remote_copy(
                src_ref=ast.at[h, m], dst_ref=abuf.at[h, x, y],
                send_sem=send_sems.at[i0 + m], recv_sem=recv_sems.at[i0 + y],
                device_id={"seq": seq_of(c, z, m)}, device_id_type=MESH,
            )
            is_self = jnp.logical_and(stays, c == m)
            a_copies[h, m] = copy, jnp.logical_not(is_self)

            @pl.when(is_self)
            def _():
                abuf[h, x, y] = ast[h, m]

            @pl.when(jnp.logical_not(is_self))
            def _():
                copy.start()

    x_ids = {}
    for h in range(2):
        for k, b in enumerate((y, 1 - y)):
            mine = abuf.at[h, x, b]
            if k:
                arrived(mine, a_ids[h] + b)
            else:
                @pl.when(leaves)
                def _():
                    arrived(mine, a_ids[h] + b)
            for d in (2, 1, 3):
                x_ids[h, k, d] = push(mine, mine, {"grp": (x + d) % 4})

    for i, land in o_y:
        arrived(land, i)
    for zz in range(Z):
        here = owb.at[seq_of(1 - y, zz, c)]
        o_s.append((push(here, here, sib), owb.at[seq_of(1 - y, zz, 1 - c)]))
    for i, land in o_s:
        arrived(land, i)

    def project(h, yh):
        total = None
        for xx in range(4):
            w = owb[pl.ds(xx * 8 + yh * 2, 2)].reshape(2 * WROWS, 2 * HEAD)
            a = abuf[h, xx].reshape(2 * HEAD, HEAD)
            term = jnp.dot(w, a, preferred_element_type=F32)
            total = term if total is None else total + term
        return total

    r_ids, totals = {}, []
    for h in range(2):
        for d in (1, 3, 2):
            for k, b in enumerate((y, 1 - y)):
                arrived(abuf.at[h, (x + 4 - d) % 4, b], x_ids[h, k, d])
        r_ids[h] = [next(ids) for _ in range(3)][0] - 1

        def piece(h, d):
            return remote(pst.at[h, d], rbuf.at[h, d], {"tp": (tp + d) % 4}, r_ids[h] + d)

        def step(i, carry):
            d = 1 + (i + 1) % 3
            pst[h, d] = project(h, (tp + d) % 4).astype(BF16)
            piece(h, d).start()
            return carry

        lax.fori_loop(0, 3, step, 0)
        totals.append(project(h, tp))

    for h in range(2):
        total = totals[h]
        for d in (1, 3, 2):
            arrived(rbuf.at[h, d], r_ids[h] + d)
            total = total + rbuf[h, d].astype(F32)
        at = slice(h * HEAD, (h + 1) * HEAD)
        out[:, at] = res[:, at] + total

    for copy in sent:
        copy.wait_send()
    for h in range(2):
        for d in range(1, 4):
            piece(h, d).wait_send()

    @pl.when(leaves)
    def _():
        for copy in (k_diag, v_diag, q_diag):
            copy.wait_send()

    for copy, remote_target in a_copies.values():
        @pl.when(remote_target)
        def _():
            copy.wait_send()


def body(latent, condition, modulation, qk_gain, qkv_weight, out_weight):
    modulation = jnp.transpose(modulation, (1, 0, 2))
    vm = pl.BlockSpec(memory_space=pltpu.VMEM)
    hbm = pl.BlockSpec(memory_space=pltpu.HBM)
    mixed = pl.pallas_call(
        kernel,
        out_shape=jax.ShapeDtypeStruct((2 * WROWS, ROWS), F32),
        in_specs=[hbm, hbm, hbm, vm, hbm, hbm],
        out_specs=vm,
        scratch_shapes=[
            pltpu.VMEM((ROWS, D), BF16),
            pltpu.VMEM((ROWS, D), BF16),
            pltpu.VMEM((3, 2, D), F32),
            pltpu.VMEM((2, WROWS, HEAD), BF16),
            pltpu.VMEM((WROWS, 2 * HEAD), BF16),
            pltpu.VMEM((3, 2, Z, 2 * WROWS, HEAD), BF16),
            pltpu.VMEM((2, ROWS, D), BF16),
            pltpu.VMEM((ROWS, D), BF16),
            pltpu.VMEM((2, 2, HEAD, HEAD), BF16),
            pltpu.VMEM((2, Z, 2, HEAD, ROWS), BF16),
            pltpu.VMEM((2, Z, CHIP, HEAD), BF16),
            pltpu.VMEM((2, HEAD, ROWS), BF16),
            pltpu.VMEM((CHIP, HEAD), BF16),
            pltpu.VMEM((2, 2, HEAD, HEAD), BF16),
            pltpu.VMEM((32, WROWS, 2 * HEAD), BF16),
            pltpu.VMEM((CHIP, 2 * HEAD), F32),
            pltpu.VMEM((2, 4, 2, HEAD, HEAD), BF16),
            pltpu.VMEM((2, 2, HEAD, HEAD), BF16),
            pltpu.VMEM((2, 4, 2 * WROWS, HEAD), BF16),
            pltpu.VMEM((2, 4, 2 * WROWS, HEAD), BF16),
            pltpu.VMEM((2 * WROWS, ROWS), F32),
            pltpu.SemaphoreType.DMA((N_SEMS,)),
            pltpu.SemaphoreType.DMA((N_SEMS,)),
            pltpu.SemaphoreType.DMA((5,)),
        ],
        compiler_params=pltpu.CompilerParams(
            collective_id=0, has_side_effects=True, vmem_limit_bytes=56 * 1024 * 1024
        ),
        cost_estimate=pl.CostEstimate(
            flops=3_900_000_000, bytes_accessed=4_000_000, transcendentals=4_200_000
        ),
    )(latent, condition, modulation, qk_gain, qkv_weight, jnp.transpose(out_weight, (0, 2, 1)))
    return mixed.astype(BF16).T


def solution(mesh):
    return jax.shard_map(
        body,
        mesh=mesh,
        in_specs=(
            P("seq", None),
            P("seq", None),
            P(),
            P(),
            P(None, None, "seq", ("grp", "tp")),
            P(None, ("grp", "tp"), "seq"),
        ),
        out_specs=P("seq", ("grp", "tp")),
        check_vma=False,
    )
```

```python
import math

import jax
import jax.numpy as jnp
from jax import lax
from jax.experimental import pallas as pl
from jax.experimental.pallas import tpu as pltpu
from jax.sharding import PartitionSpec as P

MESH = pl.DeviceIdType.MESH
BF16, F32 = jnp.bfloat16, jnp.float32
Z = 8
ROWS = 256
CHIP = 2 * ROWS
D = 3072
HEAD = 128
WROWS = 96
N_SEMS = 200


def kernel(
    lat_in, cond_in, mod_in, gain, wsh, ow_in, out,
    lat, cond, mod, ow, owt, wbuf, xbuf, xst, qbuf, kbuf, vbuf, owb, acc, abuf, ast, pst, rbuf, res,
    send_sems, recv_sems, load_sems,
):
    loads = []
    for i, (a, b) in enumerate(((ow_in, ow), (mod_in, mod), (lat_in, lat), (cond_in, cond))):
        loads.append(pltpu.make_async_copy(a, b, load_sems.at[i]))
        loads[-1].start()
    x, s, tp = lax.axis_index("grp"), lax.axis_index("seq"), lax.axis_index("tp")
    y, z, c = s // 16, (s // 2) % 8, s % 2

    def seq_of(y_, z_, c_):
        return y_ * 16 + z_ * 2 + c_

    sib = {"seq": seq_of(y, z, 1 - c)}
    row = {"seq": seq_of(1 - y, z, c)}
    beyond = {"tp": (tp + c * (3 - 2 * y)) % 4, "seq": seq_of(1 - y, z, y)}
    right = {"seq": seq_of(y, (z + 1) % Z, c)}
    left = {"seq": seq_of(y, (z + 7) % Z, c)}

    def zm(t):
        return (z + Z - t) % Z

    def zp(t):
        return (z + t) % Z

    px, py, pz = y * 2 + z // 4, x // 2, z % 4 + 4 * (x % 2)
    moves = px != x
    partner = {"grp": px, "seq": seq_of(py, pz, c)}

    barrier = pltpu.get_barrier_semaphore()

    def greet(device):
        pl.semaphore_signal(barrier, inc=1, device_id=device, device_id_type=MESH)

    flat = x * 4 + y * 2 + c
    for i in range(1, 16):
        f = (flat + i) % 16
        greet({"grp": f // 4, "seq": seq_of((f // 2) % 2, z, f % 2)})
    for device in (right, left):
        greet(device)
    for i in (1, 3):
        for core in range(2):
            greet({"tp": (tp + i) % 4, "seq": seq_of(1 - y, z, core)})
    for i in range(1, 4):
        greet({"tp": (tp + i) % 4})

    @pl.when(moves)
    def _():
        greet(partner)

    pl.semaphore_wait(barrier, 24 + jnp.where(moves, 1, 0))

    ids = iter(range(N_SEMS))
    sent = []

    def remote(src, dst, device, i):
        return pltpu.make_async_remote_copy(
            src_ref=src, dst_ref=dst, send_sem=send_sems.at[i], recv_sem=recv_sems.at[i],
            device_id=device, device_id_type=MESH,
        )

    def push(src, dst, device):
        i = next(ids)
        copy = remote(src, dst, device, i)
        copy.start()
        sent.append(copy)
        return i

    def arrived(land, i):
        remote(land, land, sib, i).wait_recv()

    def ring_send(view, t):
        if t < 3:
            a, b = view(zm(t), None), view(zp(t), None)
        else:
            a, b = view(zm(t), 0), view(zp(t), 1)
        return push(a, a, right), push(b, b, left)

    def ring_wait(view, t, got):
        if t < 4:
            arrived(view(zm(t), None), got[0])
            arrived(view(zp(t), None), got[1])
        else:
            arrived(view(zm(t), 0), got[0])
            arrived(view(zp(t), 1), got[1])

    stays = y == c
    leaves = jnp.logical_not(stays)
    w_own, w_row = {}, {}
    for j in (1, 2, 0):
        w_row[j] = push(wsh.at[1 - y, j], wbuf.at[j, y, z, c], row)
        w_own[j] = pltpu.make_async_copy(wsh.at[y, j], wbuf.at[j, y, z, c], load_sems.at[4 + j])
        w_own[j].start()

    ow_id = next(ids)
    ow_copy = remote(owt, owb.at[seq_of(py, pz, c)], partner, ow_id)
    loads[0].wait()
    loads[1].wait()
    first = s * WROWS
    base = jnp.minimum(first // HEAD * HEAD, D - 2 * HEAD)
    for block in range(2):
        gates = mod[2, block:block + 1, pl.ds(pl.multiple_of(base, HEAD), 2 * HEAD)]
        gates = pltpu.roll(jnp.broadcast_to(gates, (HEAD, 2 * HEAD)), (2 * HEAD + base - first) % (2 * HEAD), 1)
        gates = jnp.transpose(gates[:, :WROWS])
        owt[:, block * HEAD:(block + 1) * HEAD] = (ow[block].astype(F32) * gates).astype(BF16)

    @pl.when(moves)
    def _():
        ow_copy.start()

    @pl.when(jnp.logical_not(moves))
    def _():
        owb[s] = owt[...]

    def layer_norm(block, store, lo, hi):
        use = jnp.where(block == 0, 1.0, 0.0).astype(F32)
        scale = 1.0 + mod[1, pl.ds(block, 1), :]
        shift = mod[0, pl.ds(block, 1), :]

        def step(i, carry):
            at = pl.ds(pl.multiple_of(i * 32, 32), 32)
            v = lat[at, :].astype(F32) + use * cond[at, :].astype(F32)
            center = v - jnp.mean(v, axis=-1, keepdims=True)
            var = jnp.mean(center * center, axis=-1, keepdims=True)
            store(at, (center * lax.rsqrt(var + 1e-6) * scale + shift).astype(BF16))
            return carry

        lax.fori_loop(lo, hi, step, 0)

    def store_to(k):
        def store(at, v):
            xst[k, at, :] = v

        return store

    def view_w(j):
        def view(zz, h):
            return wbuf.at[j, :, zz, c] if h is None else wbuf.at[j, :, zz, c, pl.ds(h * 48, 48)]

        return view

    w_shared = {0: [], 1: [], 2: []}

    def w_share(j, zz):
        mine = wbuf.at[j, :, zz, c]
        w_shared[j].append((push(mine, mine, sib), wbuf.at[j, :, zz, 1 - c]))

    def w_hop(j, t, got):
        if t == 0:
            w_own[j].wait()
            arrived(wbuf.at[j, 1 - y, z, c], w_row[j])
        else:
            ring_wait(view_w(j), t, got)
        if 0 < t < 4:
            w_share(j, zm(t))
        if t < 4:
            got = ring_send(view_w(j), t)
        w_share(j, zp(t))
        return got

    def w_come(j):
        for i, land in w_shared[j]:
            arrived(land, i)

    def view_o(zz, h):
        base = seq_of(y, zz, c)
        return owb.at[base] if h is None else owb.at[base, pl.ds(h * 48, 48)]

    got_w = {j: w_hop(j, 0, None) for j in (1, 2, 0)}
    for load in loads[2:]:
        load.wait()
    x_base = [next(ids) for _ in range(4)][0]
    beyond_copies = [
        pltpu.make_async_remote_copy(
            src_ref=xst.at[0, pl.ds(part * HEAD, HEAD)], dst_ref=xbuf.at[c, pl.ds(part * HEAD, HEAD)],
            send_sem=send_sems.at[x_base + part], recv_sem=recv_sems.at[x_base + 2 * part + c],
            device_id=beyond, device_id_type=MESH,
        )
        for part in range(2)
    ]
    sent.extend(beyond_copies)
    layer_norm(1 - y, store_to(0), 0, 4)
    beyond_copies[0].start()
    layer_norm(1 - y, store_to(0), 4, 8)
    beyond_copies[1].start()
    g = x * 4 + tp
    near = lat[:, pl.ds(pl.multiple_of(g * 3 // 2 * HEAD, HEAD), 2 * HEAD)].astype(F32)
    near = jnp.where(g % 2 == 0, near[:, :2 * WROWS], near[:, HEAD // 2:])
    res[...] = jnp.transpose(near)

    x_id = next(ids)
    x_local = pltpu.make_async_copy(xst.at[1], xbuf.at[c], load_sems.at[7])
    x_remote = remote(xst.at[1], xbuf.at[c], sib, x_id)
    for t in range(1, 5):
        for j in (1, 2, 0):
            got_w[j] = w_hop(j, t, got_w[j])
        if t < 3:
            layer_norm(y, store_to(1), 4 * t - 4, 4 * t)
        if t == 2:
            @pl.when(stays)
            def _():
                x_local.start()

            @pl.when(leaves)
            def _():
                x_remote.start()

    @pl.when(moves)
    def _():
        ow_copy.wait_send()
        arrived(owb.at[s], ow_id)

    o_y, o_s = [], []

    def o_pass(zz):
        here, there = owb.at[seq_of(y, zz, c)], owb.at[seq_of(1 - y, zz, c)]
        o_y.append((push(here, here, row), there))
        o_s.append((push(here, here, sib), owb.at[seq_of(y, zz, 1 - c)]))

    def o_hop(t, got):
        ring_wait(view_o, t, got)
        if t < 4:
            got = ring_send(view_o, t)
            o_pass(zm(t))
            o_pass(zp(t))
            return got
        o_pass(zp(t))

    got_o = ring_send(view_o, 0)
    o_pass(z)
    w_come(1)

    @pl.when(stays)
    def _():
        x_local.wait()
        arrived(xbuf.at[1 - c], x_id)

    @pl.when(leaves)
    def _():
        for core in range(2):
            for part in range(2):
                arrived(xbuf.at[core, pl.ds(part * HEAD, HEAD)], x_base + 2 * part + core)

    def head_norm(v, g):
        return v * lax.rsqrt(jnp.mean(v * v, axis=-1, keepdims=True) + 1e-6) * g

    q_gain = gain[y, 0:1, :] * (math.log2(math.e) / math.sqrt(HEAD))
    k_gain = gain[y, 1:2, :]

    def project_in(j, store):
        def step(m, carry):
            store(m, jnp.dot(xbuf[m], wbuf[j].reshape(D, HEAD), preferred_element_type=F32))
            return carry

        lax.fori_loop(0, 2, step, 0)

    def rows_of(m):
        return pl.ds(pl.multiple_of(m * ROWS, ROWS), ROWS)

    def store_k(m, v):
        kbuf[c, z, m] = jnp.transpose(head_norm(v, k_gain)).astype(BF16)

    def store_v(m, v):
        vbuf[c, z, rows_of(m), :] = v.astype(BF16)

    def store_q(m, v):
        v = head_norm(v, q_gain).astype(BF16)
        for h in range(2):
            qbuf[h, m] = v[h * HEAD:(h + 1) * HEAD]

    def view_k(zz, h):
        return kbuf.at[c, zz] if h is None else kbuf.at[c, zz, h]

    def view_v(zz, h):
        return vbuf.at[c, zz] if h is None else vbuf.at[c, zz, pl.ds(h * ROWS, ROWS)]

    project_in(1, store_k)
    got_k = ring_send(view_k, 0)
    w_come(2)
    project_in(2, store_v)
    got_v = ring_send(view_v, 0)
    got_o = o_hop(1, got_o)

    shared = {}

    def share(buf, zz, t):
        mine = buf.at[c, zz]
        shared.setdefault(t, []).append((push(mine, mine, sib), buf.at[1 - c, zz]))

    share(kbuf, z, 0)
    share(vbuf, z, 0)
    def k_hop(t, got):
        ring_wait(view_k, t, got)
        if t < 4:
            got = ring_send(view_k, t)
            share(kbuf, zm(t), t)
        share(kbuf, zp(t), t)
        return got

    def v_hop(t, got):
        ring_wait(view_v, t, got)
        if t < 4:
            got = ring_send(view_v, t)
            share(vbuf, zm(t), t)
        share(vbuf, zp(t), t)
        return got

    acc[...] = jnp.zeros_like(acc)
    ones = jnp.ones((CHIP, HEAD), BF16)
    w_come(0)
    project_in(0, store_q)

    def attend(places, halves=(0, 2)):
        lo, hi = halves
        at = slice(lo * ROWS, hi * ROWS)
        queries = qbuf[lo:hi].reshape((hi - lo) * ROWS, HEAD)
        weights = jnp.concatenate([
            jnp.exp2(jnp.dot(queries, kbuf[r, zz, h], preferred_element_type=F32)).astype(BF16)
            for r, zz in places for h in range(2)
        ], axis=1)
        values = jnp.concatenate([
            jnp.concatenate([vbuf[r, zz], ones], axis=1) for r, zz in places
        ], axis=0)
        acc[at, :] += jnp.dot(weights, values, preferred_element_type=F32)

    def shared_come(t):
        for i, land in shared[t]:
            arrived(land, i)

    def attend_shared(t):
        shared_come(t)
        attend([(1 - c, zm(t)), (1 - c, zp(t))] if t else [(1 - c, z)])

    for t in range(1, 5):
        got_k = k_hop(t, got_k)
        got_v = v_hop(t, got_v)
        if t < 4:
            got_o = o_hop(t + 1, got_o)
        attend([(c, zp(4))] if t == 4 else [(c, zm(t)), (c, zp(t))] + [(c, z)] * (t == 1))
        if t < 4:
            @pl.when(leaves)
            def _():
                attend_shared(t - 1)

    @pl.when(leaves)
    def _():
        shared_come(3)

    @pl.when(stays)
    def _():
        for t in range(3):
            attend_shared(t)
        shared_come(3)

    shared_come(4)

    def attend_last(h):
        attend([(1 - c, zm(3)), (1 - c, zp(3)), (1 - c, zp(4))], (h, h + 1))

    a_ids, a_copies = [], {}
    for h in range(2):
        attend_last(h)
        i0 = next(ids)
        next(ids)
        a_ids.append(i0)
        for m in range(2):
            lo = h * ROWS + m * HEAD
            part = acc[lo:lo + HEAD, :]
            ast[h, m] = jnp.transpose(part[:, :HEAD] / part[:, HEAD:]).astype(BF16)
            copy = pltpu.make_async_remote_copy(
                src_ref=ast.at[h, m], dst_ref=abuf.at[h, x, y],
                send_sem=send_sems.at[i0 + m], recv_sem=recv_sems.at[i0 + y],
                device_id={"seq": seq_of(c, z, m)}, device_id_type=MESH,
            )
            is_self = jnp.logical_and(stays, c == m)
            a_copies[h, m] = copy, jnp.logical_not(is_self)

            @pl.when(is_self)
            def _():
                abuf[h, x, y] = ast[h, m]

            @pl.when(jnp.logical_not(is_self))
            def _():
                copy.start()

    x_ids = {}
    for h in range(2):
        for k, b in enumerate((y, 1 - y)):
            mine = abuf.at[h, x, b]
            if k:
                arrived(mine, a_ids[h] + b)
            else:
                @pl.when(leaves)
                def _():
                    arrived(mine, a_ids[h] + b)
            for d in (2, 1, 3):
                x_ids[h, k, d] = push(mine, mine, {"grp": (x + d) % 4})

    for i, land in o_y:
        arrived(land, i)
    for zz in range(Z):
        here = owb.at[seq_of(1 - y, zz, c)]
        o_s.append((push(here, here, sib), owb.at[seq_of(1 - y, zz, 1 - c)]))
    for i, land in o_s:
        arrived(land, i)

    def project(h, yh):
        total = None
        for xx in range(4):
            w = owb[pl.ds(xx * 8 + yh * 2, 2)].reshape(2 * WROWS, 2 * HEAD)
            a = abuf[h, xx].reshape(2 * HEAD, HEAD)
            term = jnp.dot(w, a, preferred_element_type=F32)
            total = term if total is None else total + term
        return total

    r_ids, totals = {}, []
    for h in range(2):
        for d in (1, 3, 2):
            for k, b in enumerate((y, 1 - y)):
                arrived(abuf.at[h, (x + 4 - d) % 4, b], x_ids[h, k, d])
        r_ids[h] = [next(ids) for _ in range(3)][0] - 1

        def piece(h, d):
            return remote(pst.at[h, d], rbuf.at[h, d], {"tp": (tp + d) % 4}, r_ids[h] + d)

        def step(i, carry):
            d = 1 + (i + 1) % 3
            pst[h, d] = project(h, (tp + d) % 4).astype(BF16)
            piece(h, d).start()
            return carry

        lax.fori_loop(0, 3, step, 0)
        totals.append(project(h, tp))

    for h in range(2):
        total = totals[h]
        for d in (1, 3, 2):
            arrived(rbuf.at[h, d], r_ids[h] + d)
            total = total + rbuf[h, d].astype(F32)
        at = slice(h * HEAD, (h + 1) * HEAD)
        out[:, at] = res[:, at] + total

    for copy in sent:
        copy.wait_send()
    for h in range(2):
        for d in range(1, 4):
            piece(h, d).wait_send()

    @pl.when(leaves)
    def _():
        x_remote.wait_send()

    for copy, remote_target in a_copies.values():
        @pl.when(remote_target)
        def _():
            copy.wait_send()


def body(latent, condition, modulation, qk_gain, qkv_weight, out_weight):
    modulation = jnp.transpose(modulation, (1, 0, 2))
    vm = pl.BlockSpec(memory_space=pltpu.VMEM)
    hbm = pl.BlockSpec(memory_space=pltpu.HBM)
    mixed = pl.pallas_call(
        kernel,
        out_shape=jax.ShapeDtypeStruct((2 * WROWS, ROWS), F32),
        in_specs=[hbm, hbm, hbm, vm, hbm, hbm],
        out_specs=vm,
        scratch_shapes=[
            pltpu.VMEM((ROWS, D), BF16),
            pltpu.VMEM((ROWS, D), BF16),
            pltpu.VMEM((3, 2, D), F32),
            pltpu.VMEM((2, WROWS, HEAD), BF16),
            pltpu.VMEM((WROWS, 2 * HEAD), BF16),
            pltpu.VMEM((3, 2, Z, 2, WROWS, HEAD), BF16),
            pltpu.VMEM((2, ROWS, D), BF16),
            pltpu.VMEM((2, ROWS, D), BF16),
            pltpu.VMEM((2, 2, HEAD, HEAD), BF16),
            pltpu.VMEM((2, Z, 2, HEAD, ROWS), BF16),
            pltpu.VMEM((2, Z, CHIP, HEAD), BF16),
            pltpu.VMEM((32, WROWS, 2 * HEAD), BF16),
            pltpu.VMEM((CHIP, 2 * HEAD), F32),
            pltpu.VMEM((2, 4, 2, HEAD, HEAD), BF16),
            pltpu.VMEM((2, 2, HEAD, HEAD), BF16),
            pltpu.VMEM((2, 4, 2 * WROWS, HEAD), BF16),
            pltpu.VMEM((2, 4, 2 * WROWS, HEAD), BF16),
            pltpu.VMEM((2 * WROWS, ROWS), F32),
            pltpu.SemaphoreType.DMA((N_SEMS,)),
            pltpu.SemaphoreType.DMA((N_SEMS,)),
            pltpu.SemaphoreType.DMA((8,)),
        ],
        compiler_params=pltpu.CompilerParams(
            collective_id=0, has_side_effects=True, vmem_limit_bytes=56 * 1024 * 1024
        ),
        cost_estimate=pl.CostEstimate(
            flops=3_900_000_000, bytes_accessed=4_000_000, transcendentals=4_200_000
        ),
    )(latent, condition, modulation, qk_gain, qkv_weight, jnp.transpose(out_weight, (0, 2, 1)))
    return mixed.astype(BF16).T


def solution(mesh):
    return jax.shard_map(
        body,
        mesh=mesh,
        in_specs=(
            P("seq", None),
            P("seq", None),
            P(),
            P(),
            P(None, None, "seq", ("grp", "tp")),
            P(None, ("grp", "tp"), "seq"),
        ),
        out_specs=P("seq", ("grp", "tp")),
        check_vma=False,
    )
```

```python
import math

import jax
import jax.numpy as jnp
from jax import lax
from jax.experimental import pallas as pl
from jax.experimental.pallas import tpu as pltpu
from jax.sharding import PartitionSpec as P

MESH = pl.DeviceIdType.MESH
BF16, F32 = jnp.bfloat16, jnp.float32
Z = 8
ROWS = 256
CHIP = 2 * ROWS
D = 3072
HEAD = 128
WROWS = 96
N_SEMS = 200


def kernel(
    lat_in, cond_in, mod_in, gain, wsh, ow_in, out,
    lat, cond, mod, ow, owt, wbuf, xbuf, xst, qbuf, kbuf, vbuf, owb, acc, abuf, ast, pst, rbuf, res,
    send_sems, recv_sems, load_sems,
):
    loads = []
    for i, (a, b) in enumerate(((ow_in, ow), (mod_in, mod), (lat_in, lat), (cond_in, cond))):
        loads.append(pltpu.make_async_copy(a, b, load_sems.at[i]))
        loads[-1].start()
    x, s, tp = lax.axis_index("grp"), lax.axis_index("seq"), lax.axis_index("tp")
    y, z, c = s // 16, (s // 2) % 8, s % 2

    def seq_of(y_, z_, c_):
        return y_ * 16 + z_ * 2 + c_

    sib = {"seq": seq_of(y, z, 1 - c)}
    row = {"seq": seq_of(1 - y, z, c)}
    beyond = {"tp": (tp + c * (3 - 2 * y)) % 4, "seq": seq_of(1 - y, z, y)}
    right = {"seq": seq_of(y, (z + 1) % Z, c)}
    left = {"seq": seq_of(y, (z + 7) % Z, c)}

    def zm(t):
        return (z + Z - t) % Z

    def zp(t):
        return (z + t) % Z

    px, py, pz = y * 2 + z // 4, x // 2, z % 4 + 4 * (x % 2)
    moves = px != x
    partner = {"grp": px, "seq": seq_of(py, pz, c)}

    barrier = pltpu.get_barrier_semaphore()

    def greet(device):
        pl.semaphore_signal(barrier, inc=1, device_id=device, device_id_type=MESH)

    for device in (sib, row, {"seq": seq_of(1 - y, z, 1 - c)}):
        greet(device)
    for i in range(1, 4):
        greet({"grp": (x + i) % 4})
    for device in (right, left):
        greet(device)
    for i in (1, 3):
        for core in range(2):
            greet({"tp": (tp + i) % 4, "seq": seq_of(1 - y, z, core)})
    for i in range(1, 4):
        greet({"tp": (tp + i) % 4})

    @pl.when(moves)
    def _():
        greet(partner)

    pl.semaphore_wait(barrier, 15 + jnp.where(moves, 1, 0))

    ids = iter(range(N_SEMS))
    sent = []

    def remote(src, dst, device, i):
        return pltpu.make_async_remote_copy(
            src_ref=src, dst_ref=dst, send_sem=send_sems.at[i], recv_sem=recv_sems.at[i],
            device_id=device, device_id_type=MESH,
        )

    def push(src, dst, device):
        i = next(ids)
        copy = remote(src, dst, device, i)
        copy.start()
        sent.append(copy)
        return i

    def arrived(land, i):
        remote(land, land, sib, i).wait_recv()

    def ring_send(view, t):
        if t < 3:
            a, b = view(zm(t), None), view(zp(t), None)
        else:
            a, b = view(zm(t), 0), view(zp(t), 1)
        return push(a, a, right), push(b, b, left)

    def ring_wait(view, t, got):
        if t < 4:
            arrived(view(zm(t), None), got[0])
            arrived(view(zp(t), None), got[1])
        else:
            arrived(view(zm(t), 0), got[0])
            arrived(view(zp(t), 1), got[1])

    stays = y == c
    leaves = jnp.logical_not(stays)
    w_own, w_row = {}, {}
    for j in (1, 2, 0):
        w_row[j] = push(wsh.at[1 - y, j], wbuf.at[j, y, z, c], row)
        w_own[j] = pltpu.make_async_copy(wsh.at[y, j], wbuf.at[j, y, z, c], load_sems.at[4 + j])
        w_own[j].start()

    def layer_norm(block, store, lo, hi):
        use = jnp.where(block == 0, 1.0, 0.0).astype(F32)
        scale = 1.0 + mod[1, pl.ds(block, 1), :]
        shift = mod[0, pl.ds(block, 1), :]

        def step(i, carry):
            at = pl.ds(pl.multiple_of(i * 32, 32), 32)
            v = lat[at, :].astype(F32) + use * cond[at, :].astype(F32)
            center = v - jnp.mean(v, axis=-1, keepdims=True)
            var = jnp.mean(center * center, axis=-1, keepdims=True)
            store(at, (center * lax.rsqrt(var + 1e-6) * scale + shift).astype(BF16))
            return carry

        lax.fori_loop(lo, hi, step, 0)

    def store_to(k):
        def store(at, v):
            xst[k, at, :] = v

        return store

    def view_w(j):
        def view(zz, h):
            return wbuf.at[j, :, zz, c] if h is None else wbuf.at[j, :, zz, c, pl.ds(h * 48, 48)]

        return view

    w_shared = {0: [], 1: [], 2: []}

    def w_share(j, zz):
        mine = wbuf.at[j, :, zz, c]
        w_shared[j].append((push(mine, mine, sib), wbuf.at[j, :, zz, 1 - c]))

    def w_hop(j, t, got):
        if t == 0:
            w_own[j].wait()
            arrived(wbuf.at[j, 1 - y, z, c], w_row[j])
        else:
            ring_wait(view_w(j), t, got)
        if t < 4:
            got = ring_send(view_w(j), t)
        if 0 < t < 4:
            w_share(j, zm(t))
        w_share(j, zp(t))
        return got

    def w_come(j):
        for i, land in w_shared[j]:
            arrived(land, i)

    def view_o(zz, h):
        base = seq_of(y, zz, c)
        return owb.at[base] if h is None else owb.at[base, pl.ds(h * 48, 48)]

    for load in loads[1:]:
        load.wait()
    x_base = [next(ids) for _ in range(4)][0]
    beyond_copies = [
        pltpu.make_async_remote_copy(
            src_ref=xst.at[0, pl.ds(part * HEAD, HEAD)], dst_ref=xbuf.at[c, pl.ds(part * HEAD, HEAD)],
            send_sem=send_sems.at[x_base + part], recv_sem=recv_sems.at[x_base + 2 * part + c],
            device_id=beyond, device_id_type=MESH,
        )
        for part in range(2)
    ]
    sent.extend(beyond_copies)
    layer_norm(1 - y, store_to(0), 0, 4)
    beyond_copies[0].start()
    got_w = {1: w_hop(1, 0, None)}
    layer_norm(1 - y, store_to(0), 4, 8)
    beyond_copies[1].start()
    for j in (2, 0):
        got_w[j] = w_hop(j, 0, None)
    ow_id = next(ids)
    ow_copy = remote(owt, owb.at[seq_of(py, pz, c)], partner, ow_id)

    def make_out_weight():
        loads[0].wait()
        first = s * WROWS
        base = jnp.minimum(first // HEAD * HEAD, D - 2 * HEAD)
        for block in range(2):
            gates = mod[2, block:block + 1, pl.ds(pl.multiple_of(base, HEAD), 2 * HEAD)]
            gates = pltpu.roll(jnp.broadcast_to(gates, (HEAD, 2 * HEAD)), (2 * HEAD + base - first) % (2 * HEAD), 1)
            gates = jnp.transpose(gates[:, :WROWS])
            owt[:, block * HEAD:(block + 1) * HEAD] = (ow[block].astype(F32) * gates).astype(BF16)

        @pl.when(moves)
        def _():
            ow_copy.start()

        @pl.when(jnp.logical_not(moves))
        def _():
            owb[s] = owt[...]

    def make_residual():
        g = x * 4 + tp
        near = lat[:, pl.ds(pl.multiple_of(g * 3 // 2 * HEAD, HEAD), 2 * HEAD)].astype(F32)
        near = jnp.where(g % 2 == 0, near[:, :2 * WROWS], near[:, HEAD // 2:])
        res[...] = jnp.transpose(near)

    x_id = next(ids)
    x_local = pltpu.make_async_copy(xst.at[1], xbuf.at[c], load_sems.at[7])
    x_remote = remote(xst.at[1], xbuf.at[c], sib, x_id)
    for t in range(1, 5):
        for j in (1, 2, 0):
            got_w[j] = w_hop(j, t, got_w[j])
        if t == 1:
            make_out_weight()
        if t == 3:
            make_residual()
        if t < 3:
            layer_norm(y, store_to(1), 4 * t - 4, 4 * t)
        if t == 2:
            @pl.when(stays)
            def _():
                x_local.start()

            @pl.when(leaves)
            def _():
                x_remote.start()

    @pl.when(moves)
    def _():
        ow_copy.wait_send()
        arrived(owb.at[s], ow_id)

    o_y, o_s = [], []

    def o_pass(zz):
        here, there = owb.at[seq_of(y, zz, c)], owb.at[seq_of(1 - y, zz, c)]
        o_y.append((push(here, here, row), there))
        o_s.append((push(here, here, sib), owb.at[seq_of(y, zz, 1 - c)]))

    def o_hop(t, got):
        ring_wait(view_o, t, got)
        if t < 4:
            got = ring_send(view_o, t)
            o_pass(zm(t))
            o_pass(zp(t))
            return got
        o_pass(zp(t))

    got_o = ring_send(view_o, 0)
    o_pass(z)
    w_come(1)

    @pl.when(stays)
    def _():
        x_local.wait()
        arrived(xbuf.at[1 - c], x_id)

    @pl.when(leaves)
    def _():
        for core in range(2):
            for part in range(2):
                arrived(xbuf.at[core, pl.ds(part * HEAD, HEAD)], x_base + 2 * part + core)

    def head_norm(v, g):
        return v * lax.rsqrt(jnp.mean(v * v, axis=-1, keepdims=True) + 1e-6) * g

    q_gain = gain[y, 0:1, :] * (math.log2(math.e) / math.sqrt(HEAD))
    k_gain = gain[y, 1:2, :]

    def project_in(j, store):
        def step(m, carry):
            store(m, jnp.dot(xbuf[m], wbuf[j].reshape(D, HEAD), preferred_element_type=F32))
            return carry

        lax.fori_loop(0, 2, step, 0)

    def rows_of(m):
        return pl.ds(pl.multiple_of(m * ROWS, ROWS), ROWS)

    def store_k(m, v):
        kbuf[c, z, m] = jnp.transpose(head_norm(v, k_gain)).astype(BF16)

    def store_v(m, v):
        vbuf[c, z, rows_of(m), :] = v.astype(BF16)

    def store_q(m, v):
        v = head_norm(v, q_gain).astype(BF16)
        for h in range(2):
            qbuf[h, m] = v[h * HEAD:(h + 1) * HEAD]

    def view_k(zz, h):
        return kbuf.at[c, zz] if h is None else kbuf.at[c, zz, h]

    def view_v(zz, h):
        return vbuf.at[c, zz] if h is None else vbuf.at[c, zz, pl.ds(h * ROWS, ROWS)]

    project_in(1, store_k)
    got_k = ring_send(view_k, 0)
    w_come(2)
    project_in(2, store_v)
    got_v = ring_send(view_v, 0)
    got_o = o_hop(1, got_o)

    shared = {}

    def share(buf, zz, t):
        mine = buf.at[c, zz]
        shared.setdefault(t, []).append((push(mine, mine, sib), buf.at[1 - c, zz]))

    share(kbuf, z, 0)
    share(vbuf, z, 0)
    def k_hop(t, got):
        ring_wait(view_k, t, got)
        if t < 4:
            got = ring_send(view_k, t)
            share(kbuf, zm(t), t)
        share(kbuf, zp(t), t)
        return got

    def v_hop(t, got):
        ring_wait(view_v, t, got)
        if t < 4:
            got = ring_send(view_v, t)
            share(vbuf, zm(t), t)
        share(vbuf, zp(t), t)
        return got

    acc[...] = jnp.zeros_like(acc)
    ones = jnp.ones((CHIP, HEAD), BF16)
    w_come(0)
    project_in(0, store_q)

    def attend(places, halves=(0, 2)):
        lo, hi = halves
        at = slice(lo * ROWS, hi * ROWS)
        queries = qbuf[lo:hi].reshape((hi - lo) * ROWS, HEAD)
        weights = jnp.concatenate([
            jnp.exp2(jnp.dot(queries, kbuf[r, zz, h], preferred_element_type=F32)).astype(BF16)
            for r, zz in places for h in range(2)
        ], axis=1)
        values = jnp.concatenate([
            jnp.concatenate([vbuf[r, zz], ones], axis=1) for r, zz in places
        ], axis=0)
        acc[at, :] += jnp.dot(weights, values, preferred_element_type=F32)

    def shared_come(t):
        for i, land in shared[t]:
            arrived(land, i)

    def attend_shared(t):
        shared_come(t)
        attend([(1 - c, zm(t)), (1 - c, zp(t))] if t else [(1 - c, z)])

    for t in range(1, 5):
        got_k = k_hop(t, got_k)
        got_v = v_hop(t, got_v)
        if t < 4:
            got_o = o_hop(t + 1, got_o)
        attend([(c, zp(4))] if t == 4 else [(c, zm(t)), (c, zp(t))] + [(c, z)] * (t == 1))
        if t < 4:
            @pl.when(leaves)
            def _():
                attend_shared(t - 1)

    @pl.when(leaves)
    def _():
        shared_come(3)

    @pl.when(stays)
    def _():
        for t in range(3):
            attend_shared(t)
        shared_come(3)

    shared_come(4)

    def attend_last(h):
        attend([(1 - c, zm(3)), (1 - c, zp(3)), (1 - c, zp(4))], (h, h + 1))

    a_ids, a_copies = [], {}
    for h in range(2):
        attend_last(h)
        i0 = next(ids)
        next(ids)
        a_ids.append(i0)
        for m in range(2):
            lo = h * ROWS + m * HEAD
            part = acc[lo:lo + HEAD, :]
            ast[h, m] = jnp.transpose(part[:, :HEAD] / part[:, HEAD:]).astype(BF16)
            copy = pltpu.make_async_remote_copy(
                src_ref=ast.at[h, m], dst_ref=abuf.at[h, x, y],
                send_sem=send_sems.at[i0 + m], recv_sem=recv_sems.at[i0 + y],
                device_id={"seq": seq_of(c, z, m)}, device_id_type=MESH,
            )
            is_self = jnp.logical_and(stays, c == m)
            a_copies[h, m] = copy, jnp.logical_not(is_self)

            @pl.when(is_self)
            def _():
                abuf[h, x, y] = ast[h, m]

            @pl.when(jnp.logical_not(is_self))
            def _():
                copy.start()

    x_ids = {}
    for h in range(2):
        for k, b in enumerate((y, 1 - y)):
            mine = abuf.at[h, x, b]
            if k:
                arrived(mine, a_ids[h] + b)
            else:
                @pl.when(leaves)
                def _():
                    arrived(mine, a_ids[h] + b)
            for d in (2, 1, 3):
                x_ids[h, k, d] = push(mine, mine, {"grp": (x + d) % 4})

    for i, land in o_y:
        arrived(land, i)
    for zz in range(Z):
        here = owb.at[seq_of(1 - y, zz, c)]
        o_s.append((push(here, here, sib), owb.at[seq_of(1 - y, zz, 1 - c)]))
    for i, land in o_s:
        arrived(land, i)

    def project(h, yh):
        total = None
        for xx in range(4):
            w = owb[pl.ds(xx * 8 + yh * 2, 2)].reshape(2 * WROWS, 2 * HEAD)
            a = abuf[h, xx].reshape(2 * HEAD, HEAD)
            term = jnp.dot(w, a, preferred_element_type=F32)
            total = term if total is None else total + term
        return total

    r_ids, totals = {}, []
    for h in range(2):
        for d in (1, 3, 2):
            for k, b in enumerate((y, 1 - y)):
                arrived(abuf.at[h, (x + 4 - d) % 4, b], x_ids[h, k, d])
        near = {1: {"tp": (tp + 1) % 4}, 3: {"tp": (tp + 3) % 4}}
        parts = {1: pl.ds(0, WROWS), 3: pl.ds(WROWS, WROWS)}
        pst[h, 0] = project(h, (tp + 2) % 4).astype(BF16)
        relay = {d: push(pst.at[h, 0, parts[d]], rbuf.at[h, 0, parts[d]], near[d]) for d in (1, 3)}
        pieces = {d: project(h, (tp + d) % 4) for d in (1, 3)}
        totals.append(project(h, tp))
        for d in (1, 3):
            arrived(rbuf.at[h, 0, parts[d]], relay[d])
            add = rbuf[h, 0, parts[d]].astype(F32)
            upper, lower = pieces[d][:WROWS], pieces[d][WROWS:]
            upper, lower = (upper + add, lower) if d == 1 else (upper, lower + add)
            pst[h, d] = jnp.concatenate([upper, lower], axis=0).astype(BF16)
            r_ids[h, d] = push(pst.at[h, d], rbuf.at[h, d], near[d])

    for h in range(2):
        total = totals[h]
        for d in (1, 3):
            arrived(rbuf.at[h, d], r_ids[h, d])
            total = total + rbuf[h, d].astype(F32)
        at = slice(h * HEAD, (h + 1) * HEAD)
        out[:, at] = res[:, at] + total

    for copy in sent:
        copy.wait_send()

    @pl.when(leaves)
    def _():
        x_remote.wait_send()

    for copy, remote_target in a_copies.values():
        @pl.when(remote_target)
        def _():
            copy.wait_send()


def body(latent, condition, modulation, qk_gain, qkv_weight, out_weight):
    modulation = jnp.transpose(modulation, (1, 0, 2))
    vm = pl.BlockSpec(memory_space=pltpu.VMEM)
    hbm = pl.BlockSpec(memory_space=pltpu.HBM)
    mixed = pl.pallas_call(
        kernel,
        out_shape=jax.ShapeDtypeStruct((2 * WROWS, ROWS), F32),
        in_specs=[hbm, hbm, hbm, vm, hbm, hbm],
        out_specs=vm,
        scratch_shapes=[
            pltpu.VMEM((ROWS, D), BF16),
            pltpu.VMEM((ROWS, D), BF16),
            pltpu.VMEM((3, 2, D), F32),
            pltpu.VMEM((2, WROWS, HEAD), BF16),
            pltpu.VMEM((WROWS, 2 * HEAD), BF16),
            pltpu.VMEM((3, 2, Z, 2, WROWS, HEAD), BF16),
            pltpu.VMEM((2, ROWS, D), BF16),
            pltpu.VMEM((2, ROWS, D), BF16),
            pltpu.VMEM((2, 2, HEAD, HEAD), BF16),
            pltpu.VMEM((2, Z, 2, HEAD, ROWS), BF16),
            pltpu.VMEM((2, Z, CHIP, HEAD), BF16),
            pltpu.VMEM((32, WROWS, 2 * HEAD), BF16),
            pltpu.VMEM((CHIP, 2 * HEAD), F32),
            pltpu.VMEM((2, 4, 2, HEAD, HEAD), BF16),
            pltpu.VMEM((2, 2, HEAD, HEAD), BF16),
            pltpu.VMEM((2, 4, 2 * WROWS, HEAD), BF16),
            pltpu.VMEM((2, 4, 2 * WROWS, HEAD), BF16),
            pltpu.VMEM((2 * WROWS, ROWS), F32),
            pltpu.SemaphoreType.DMA((N_SEMS,)),
            pltpu.SemaphoreType.DMA((N_SEMS,)),
            pltpu.SemaphoreType.DMA((8,)),
        ],
        compiler_params=pltpu.CompilerParams(
            collective_id=0, has_side_effects=True, vmem_limit_bytes=56 * 1024 * 1024
        ),
        cost_estimate=pl.CostEstimate(
            flops=3_900_000_000, bytes_accessed=4_000_000, transcendentals=4_200_000
        ),
    )(latent, condition, modulation, qk_gain, qkv_weight, jnp.transpose(out_weight, (0, 2, 1)))
    return mixed.astype(BF16).T


def solution(mesh):
    return jax.shard_map(
        body,
        mesh=mesh,
        in_specs=(
            P("seq", None),
            P("seq", None),
            P(),
            P(),
            P(None, None, "seq", ("grp", "tp")),
            P(None, ("grp", "tp"), "seq"),
        ),
        out_specs=P("seq", ("grp", "tp")),
        check_vma=False,
    )
```

```python
import math

import jax
import jax.numpy as jnp
from jax import lax
from jax.experimental import pallas as pl
from jax.experimental.pallas import tpu as pltpu
from jax.sharding import PartitionSpec as P

MESH = pl.DeviceIdType.MESH
BF16, F32 = jnp.bfloat16, jnp.float32
Z = 8
ROWS = 256
CHIP = 2 * ROWS
D = 3072
HEAD = 128
WROWS = 96
N_SEMS = 200


def kernel(
    lat_in, cond_in, mod_in, gain, wsh, ow_in, out,
    lat, cond, mod, ow, owt, wbuf, xbuf, xst, qbuf, kbuf, vbuf, owb, acc, abuf, ast, pst, rbuf, res,
    send_sems, recv_sems, load_sems,
):
    loads = []
    for i, (a, b) in enumerate(((ow_in, ow), (mod_in, mod), (lat_in, lat), (cond_in, cond))):
        loads.append(pltpu.make_async_copy(a, b, load_sems.at[i]))
        loads[-1].start()
    x, s, tp = lax.axis_index("grp"), lax.axis_index("seq"), lax.axis_index("tp")
    y, z, c = s // 16, (s // 2) % 8, s % 2

    def seq_of(y_, z_, c_):
        return y_ * 16 + z_ * 2 + c_

    sib = {"seq": seq_of(y, z, 1 - c)}
    row = {"seq": seq_of(1 - y, z, c)}
    beyond = {"tp": (tp + c * (3 - 2 * y)) % 4, "seq": seq_of(1 - y, z, y)}
    right = {"seq": seq_of(y, (z + 1) % Z, c)}
    left = {"seq": seq_of(y, (z + 7) % Z, c)}

    def zm(t):
        return (z + Z - t) % Z

    def zp(t):
        return (z + t) % Z

    px, py, pz = y * 2 + z // 4, x // 2, z % 4 + 4 * (x % 2)
    moves = px != x
    partner = {"grp": px, "seq": seq_of(py, pz, c)}

    barrier = pltpu.get_barrier_semaphore()

    def greet(device):
        pl.semaphore_signal(barrier, inc=1, device_id=device, device_id_type=MESH)

    for device in (sib, row, {"seq": seq_of(1 - y, z, 1 - c)}):
        greet(device)
    for i in range(1, 4):
        greet({"grp": (x + i) % 4})
    for device in (right, left):
        greet(device)
    for i in (1, 3):
        for core in range(2):
            greet({"tp": (tp + i) % 4, "seq": seq_of(1 - y, z, core)})
    for i in range(1, 4):
        greet({"tp": (tp + i) % 4})

    @pl.when(moves)
    def _():
        greet(partner)

    pl.semaphore_wait(barrier, 15 + jnp.where(moves, 1, 0))

    ids = iter(range(N_SEMS))
    sent = []

    def remote(src, dst, device, i):
        return pltpu.make_async_remote_copy(
            src_ref=src, dst_ref=dst, send_sem=send_sems.at[i], recv_sem=recv_sems.at[i],
            device_id=device, device_id_type=MESH,
        )

    def push(src, dst, device):
        i = next(ids)
        copy = remote(src, dst, device, i)
        copy.start()
        sent.append(copy)
        return i

    def arrived(land, i):
        remote(land, land, sib, i).wait_recv()

    def ring_send(view, t):
        if t < 3:
            a, b = view(zm(t), None), view(zp(t), None)
        else:
            a, b = view(zm(t), 0), view(zp(t), 1)
        return push(a, a, right), push(b, b, left)

    def ring_wait(view, t, got):
        if t < 4:
            arrived(view(zm(t), None), got[0])
            arrived(view(zp(t), None), got[1])
        else:
            arrived(view(zm(t), 0), got[0])
            arrived(view(zp(t), 1), got[1])

    stays = y == c
    leaves = jnp.logical_not(stays)
    w_own, w_row = {}, {}
    for j in (1, 2, 0):
        w_row[j] = push(wsh.at[1 - y, j], wbuf.at[j, y, z, c], row)
        w_own[j] = pltpu.make_async_copy(wsh.at[y, j], wbuf.at[j, y, z, c], load_sems.at[4 + j])
        w_own[j].start()

    def layer_norm(block, store, lo, hi):
        use = jnp.where(block == 0, 1.0, 0.0).astype(F32)
        scale = 1.0 + mod[1, pl.ds(block, 1), :]
        shift = mod[0, pl.ds(block, 1), :]

        def step(i, carry):
            at = pl.ds(pl.multiple_of(i * 32, 32), 32)
            v = lat[at, :].astype(F32) + use * cond[at, :].astype(F32)
            center = v - jnp.mean(v, axis=-1, keepdims=True)
            var = jnp.mean(center * center, axis=-1, keepdims=True)
            store(at, (center * lax.rsqrt(var + 1e-6) * scale + shift).astype(BF16))
            return carry

        lax.fori_loop(lo, hi, step, 0)

    def store_to(k):
        def store(at, v):
            xst[k, at, :] = v

        return store

    def view_w(j):
        def view(zz, h):
            return wbuf.at[j, :, zz, c] if h is None else wbuf.at[j, :, zz, c, pl.ds(h * 48, 48)]

        return view

    w_shared = {0: [], 1: [], 2: []}

    def w_share(j, zz):
        mine = wbuf.at[j, :, zz, c]
        w_shared[j].append((push(mine, mine, sib), wbuf.at[j, :, zz, 1 - c]))

    def w_hop(j, t, got):
        if t == 0:
            w_own[j].wait()
            arrived(wbuf.at[j, 1 - y, z, c], w_row[j])
        else:
            ring_wait(view_w(j), t, got)
        if t < 4:
            got = ring_send(view_w(j), t)
        if 0 < t < 4:
            w_share(j, zm(t))
        w_share(j, zp(t))
        return got

    def w_come(j):
        for i, land in w_shared[j]:
            arrived(land, i)

    def view_o(zz, h):
        base = seq_of(y, zz, c)
        return owb.at[base] if h is None else owb.at[base, pl.ds(h * 48, 48)]

    for load in loads[1:]:
        load.wait()
    x_base = [next(ids) for _ in range(4)][0]
    beyond_copies = [
        pltpu.make_async_remote_copy(
            src_ref=xst.at[0, pl.ds(part * HEAD, HEAD)], dst_ref=xbuf.at[c, pl.ds(part * HEAD, HEAD)],
            send_sem=send_sems.at[x_base + part], recv_sem=recv_sems.at[x_base + 2 * part + c],
            device_id=beyond, device_id_type=MESH,
        )
        for part in range(2)
    ]
    sent.extend(beyond_copies)
    layer_norm(1 - y, store_to(0), 0, 4)
    beyond_copies[0].start()
    got_w = {1: w_hop(1, 0, None)}
    layer_norm(1 - y, store_to(0), 4, 8)
    beyond_copies[1].start()
    for j in (2, 0):
        got_w[j] = w_hop(j, 0, None)
    ow_id = next(ids)
    ow_copy = remote(owt, owb.at[seq_of(py, pz, c)], partner, ow_id)

    def make_out_weight():
        loads[0].wait()
        first = s * WROWS
        base = jnp.minimum(first // HEAD * HEAD, D - 2 * HEAD)
        for block in range(2):
            gates = mod[2, block:block + 1, pl.ds(pl.multiple_of(base, HEAD), 2 * HEAD)]
            gates = pltpu.roll(jnp.broadcast_to(gates, (HEAD, 2 * HEAD)), (2 * HEAD + base - first) % (2 * HEAD), 1)
            gates = jnp.transpose(gates[:, :WROWS])
            owt[:, block * HEAD:(block + 1) * HEAD] = (ow[block].astype(F32) * gates).astype(BF16)

        @pl.when(moves)
        def _():
            ow_copy.start()

        @pl.when(jnp.logical_not(moves))
        def _():
            owb[s] = owt[...]

    def make_residual():
        g = x * 4 + tp
        near = lat[:, pl.ds(pl.multiple_of(g * 3 // 2 * HEAD, HEAD), 2 * HEAD)].astype(F32)
        near = jnp.where(g % 2 == 0, near[:, :2 * WROWS], near[:, HEAD // 2:])
        res[...] = jnp.transpose(near)

    x_id = next(ids)
    x_local = pltpu.make_async_copy(xst.at[1], xbuf.at[c], load_sems.at[7])
    x_remote = remote(xst.at[1], xbuf.at[c], sib, x_id)
    for t in range(1, 5):
        for j in (1, 2, 0):
            got_w[j] = w_hop(j, t, got_w[j])
        if t == 1:
            make_out_weight()
        if t == 3:
            make_residual()
        if t < 3:
            layer_norm(y, store_to(1), 4 * t - 4, 4 * t)
        if t == 2:
            @pl.when(stays)
            def _():
                x_local.start()

            @pl.when(leaves)
            def _():
                x_remote.start()

    @pl.when(moves)
    def _():
        ow_copy.wait_send()
        arrived(owb.at[s], ow_id)

    o_y, o_s = [], []

    def o_pass(zz):
        here, there = owb.at[seq_of(y, zz, c)], owb.at[seq_of(1 - y, zz, c)]
        o_y.append((push(here, here, row), there))
        o_s.append((push(here, here, sib), owb.at[seq_of(y, zz, 1 - c)]))

    def o_hop(t, got):
        ring_wait(view_o, t, got)
        if t < 4:
            got = ring_send(view_o, t)
            o_pass(zm(t))
            o_pass(zp(t))
            return got
        o_pass(zp(t))

    got_o = ring_send(view_o, 0)
    o_pass(z)
    w_come(1)

    @pl.when(stays)
    def _():
        x_local.wait()
        arrived(xbuf.at[1 - c], x_id)

    @pl.when(leaves)
    def _():
        for core in range(2):
            for part in range(2):
                arrived(xbuf.at[core, pl.ds(part * HEAD, HEAD)], x_base + 2 * part + core)

    def head_norm(v, g):
        return v * lax.rsqrt(jnp.mean(v * v, axis=-1, keepdims=True) + 1e-6) * g

    q_gain = gain[y, 0:1, :] * (math.log2(math.e) / math.sqrt(HEAD))
    k_gain = gain[y, 1:2, :]

    def project_in(j, store):
        def step(m, carry):
            store(m, jnp.dot(xbuf[m], wbuf[j].reshape(D, HEAD), preferred_element_type=F32))
            return carry

        lax.fori_loop(0, 2, step, 0)

    def rows_of(m):
        return pl.ds(pl.multiple_of(m * ROWS, ROWS), ROWS)

    def store_k(m, v):
        kbuf[c, z, m] = jnp.transpose(head_norm(v, k_gain)).astype(BF16)

    def store_v(m, v):
        vbuf[c, z, rows_of(m), :] = v.astype(BF16)

    def store_q(m, v):
        v = head_norm(v, q_gain).astype(BF16)
        for h in range(2):
            qbuf[h, m] = v[h * HEAD:(h + 1) * HEAD]

    def view_k(zz, h):
        return kbuf.at[c, zz] if h is None else kbuf.at[c, zz, h]

    def view_v(zz, h):
        return vbuf.at[c, zz] if h is None else vbuf.at[c, zz, pl.ds(h * ROWS, ROWS)]

    project_in(1, store_k)
    got_k = ring_send(view_k, 0)
    w_come(2)
    project_in(2, store_v)
    got_v = ring_send(view_v, 0)
    got_o = o_hop(1, got_o)

    shared = {}

    def share(buf, zz, t):
        mine = buf.at[c, zz]
        shared.setdefault(t, []).append((push(mine, mine, sib), buf.at[1 - c, zz]))

    share(kbuf, z, 0)
    share(vbuf, z, 0)
    def k_hop(t, got):
        ring_wait(view_k, t, got)
        if t < 4:
            got = ring_send(view_k, t)
            share(kbuf, zm(t), t)
        share(kbuf, zp(t), t)
        return got

    def v_hop(t, got):
        ring_wait(view_v, t, got)
        if t < 4:
            got = ring_send(view_v, t)
            share(vbuf, zm(t), t)
        share(vbuf, zp(t), t)
        return got

    acc[...] = jnp.zeros_like(acc)
    ones = jnp.ones((CHIP, HEAD), BF16)
    w_come(0)
    project_in(0, store_q)

    def attend(places, halves=(0, 2)):
        lo, hi = halves
        at = slice(lo * ROWS, hi * ROWS)
        queries = qbuf[lo:hi].reshape((hi - lo) * ROWS, HEAD)
        weights = jnp.concatenate([
            jnp.exp2(jnp.dot(queries, kbuf[r, zz, h], preferred_element_type=F32)).astype(BF16)
            for r, zz in places for h in range(2)
        ], axis=1)
        values = jnp.concatenate([
            jnp.concatenate([vbuf[r, zz], ones], axis=1) for r, zz in places
        ], axis=0)
        acc[at, :] += jnp.dot(weights, values, preferred_element_type=F32)

    def shared_come(t):
        for i, land in shared[t]:
            arrived(land, i)

    def attend_shared(t):
        shared_come(t)
        attend([(1 - c, zm(t)), (1 - c, zp(t))] if t else [(1 - c, z)])

    for t in range(1, 5):
        got_k = k_hop(t, got_k)
        got_v = v_hop(t, got_v)
        if t < 4:
            got_o = o_hop(t + 1, got_o)
        attend([(c, zp(4))] if t == 4 else [(c, zm(t)), (c, zp(t))] + [(c, z)] * (t == 1))
        if t < 4:
            @pl.when(leaves)
            def _():
                attend_shared(t - 1)

    @pl.when(leaves)
    def _():
        shared_come(3)

    @pl.when(stays)
    def _():
        for t in range(3):
            attend_shared(t)
        shared_come(3)

    shared_come(4)

    def attend_last(h):
        attend([(1 - c, zm(3)), (1 - c, zp(3)), (1 - c, zp(4))], (h, h + 1))

    a_ids, a_copies = [], {}
    for h in range(2):
        attend_last(h)
        i0 = next(ids)
        next(ids)
        a_ids.append(i0)
        for m in range(2):
            lo = h * ROWS + m * HEAD
            part = acc[lo:lo + HEAD, :]
            ast[h, m] = jnp.transpose(part[:, :HEAD] / part[:, HEAD:]).astype(BF16)
            copy = pltpu.make_async_remote_copy(
                src_ref=ast.at[h, m], dst_ref=abuf.at[h, x, y],
                send_sem=send_sems.at[i0 + m], recv_sem=recv_sems.at[i0 + y],
                device_id={"seq": seq_of(c, z, m)}, device_id_type=MESH,
            )
            is_self = jnp.logical_and(stays, c == m)
            a_copies[h, m] = copy, jnp.logical_not(is_self)

            @pl.when(is_self)
            def _():
                abuf[h, x, y] = ast[h, m]

            @pl.when(jnp.logical_not(is_self))
            def _():
                copy.start()

    x_ids = {}
    for h in range(2):
        for k, b in enumerate((y, 1 - y)):
            mine = abuf.at[h, x, b]
            if k:
                arrived(mine, a_ids[h] + b)
            else:
                @pl.when(leaves)
                def _():
                    arrived(mine, a_ids[h] + b)
            for d in (2, 1, 3):
                x_ids[h, k, d] = push(mine, mine, {"grp": (x + d) % 4})

    for i, land in o_y:
        arrived(land, i)
    for zz in range(Z):
        here = owb.at[seq_of(1 - y, zz, c)]
        o_s.append((push(here, here, sib), owb.at[seq_of(1 - y, zz, 1 - c)]))
    for i, land in o_s:
        arrived(land, i)

    def project(h, yh):
        total = None
        for xx in range(4):
            w = owb[pl.ds(xx * 8 + yh * 2, 2)].reshape(2 * WROWS, 2 * HEAD)
            a = abuf[h, xx].reshape(2 * HEAD, HEAD)
            term = jnp.dot(w, a, preferred_element_type=F32)
            total = term if total is None else total + term
        return total

    r_ids, totals = {}, []
    for h in range(2):
        for d in (1, 3, 2):
            for k, b in enumerate((y, 1 - y)):
                arrived(abuf.at[h, (x + 4 - d) % 4, b], x_ids[h, k, d])
        r_ids[h] = [next(ids) for _ in range(3)][0] - 1

        def piece(h, d):
            return remote(pst.at[h, d], rbuf.at[h, d], {"tp": (tp + d) % 4}, r_ids[h] + d)

        def step(i, carry):
            d = 1 + (i + 1) % 3
            pst[h, d] = project(h, (tp + d) % 4).astype(BF16)
            piece(h, d).start()
            return carry

        lax.fori_loop(0, 3, step, 0)
        totals.append(project(h, tp))

    for h in range(2):
        total = totals[h]
        for d in (1, 3, 2):
            arrived(rbuf.at[h, d], r_ids[h] + d)
            total = total + rbuf[h, d].astype(F32)
        at = slice(h * HEAD, (h + 1) * HEAD)
        out[:, at] = res[:, at] + total

    for copy in sent:
        copy.wait_send()
    for h in range(2):
        for d in range(1, 4):
            piece(h, d).wait_send()

    @pl.when(leaves)
    def _():
        x_remote.wait_send()

    for copy, remote_target in a_copies.values():
        @pl.when(remote_target)
        def _():
            copy.wait_send()


def body(latent, condition, modulation, qk_gain, qkv_weight, out_weight):
    modulation = jnp.transpose(modulation, (1, 0, 2))
    vm = pl.BlockSpec(memory_space=pltpu.VMEM)
    hbm = pl.BlockSpec(memory_space=pltpu.HBM)
    mixed = pl.pallas_call(
        kernel,
        out_shape=jax.ShapeDtypeStruct((2 * WROWS, ROWS), F32),
        in_specs=[hbm, hbm, hbm, vm, hbm, hbm],
        out_specs=vm,
        scratch_shapes=[
            pltpu.VMEM((ROWS, D), BF16),
            pltpu.VMEM((ROWS, D), BF16),
            pltpu.VMEM((3, 2, D), F32),
            pltpu.VMEM((2, WROWS, HEAD), BF16),
            pltpu.VMEM((WROWS, 2 * HEAD), BF16),
            pltpu.VMEM((3, 2, Z, 2, WROWS, HEAD), BF16),
            pltpu.VMEM((2, ROWS, D), BF16),
            pltpu.VMEM((2, ROWS, D), BF16),
            pltpu.VMEM((2, 2, HEAD, HEAD), BF16),
            pltpu.VMEM((2, Z, 2, HEAD, ROWS), BF16),
            pltpu.VMEM((2, Z, CHIP, HEAD), BF16),
            pltpu.VMEM((32, WROWS, 2 * HEAD), BF16),
            pltpu.VMEM((CHIP, 2 * HEAD), F32),
            pltpu.VMEM((2, 4, 2, HEAD, HEAD), BF16),
            pltpu.VMEM((2, 2, HEAD, HEAD), BF16),
            pltpu.VMEM((2, 4, 2 * WROWS, HEAD), BF16),
            pltpu.VMEM((2, 4, 2 * WROWS, HEAD), BF16),
            pltpu.VMEM((2 * WROWS, ROWS), F32),
            pltpu.SemaphoreType.DMA((N_SEMS,)),
            pltpu.SemaphoreType.DMA((N_SEMS,)),
            pltpu.SemaphoreType.DMA((8,)),
        ],
        compiler_params=pltpu.CompilerParams(
            collective_id=0, has_side_effects=True, vmem_limit_bytes=56 * 1024 * 1024
        ),
        cost_estimate=pl.CostEstimate(
            flops=3_900_000_000, bytes_accessed=4_000_000, transcendentals=4_200_000
        ),
    )(latent, condition, modulation, qk_gain, qkv_weight, jnp.transpose(out_weight, (0, 2, 1)))
    return mixed.astype(BF16).T


def solution(mesh):
    return jax.shard_map(
        body,
        mesh=mesh,
        in_specs=(
            P("seq", None),
            P("seq", None),
            P(),
            P(),
            P(None, None, "seq", ("grp", "tp")),
            P(None, ("grp", "tp"), "seq"),
        ),
        out_specs=P("seq", ("grp", "tp")),
        check_vma=False,
    )
```

```python
import math

import jax
import jax.numpy as jnp
from jax import lax
from jax.experimental import pallas as pl
from jax.experimental.pallas import tpu as pltpu
from jax.sharding import PartitionSpec as P

MESH = pl.DeviceIdType.MESH
BF16, F32 = jnp.bfloat16, jnp.float32
Z = 8
ROWS = 256
CHIP = 2 * ROWS
D = 3072
HEAD = 128
WROWS = 96
N_SEMS = 200


def kernel(
    lat_in, cond_in, mod_in, gain, wsh, ow_in, out,
    lat, cond, mod, ow, owt, wbuf, xbuf, xst, qbuf, kbuf, vbuf, owb, acc, abuf, ast, pst, rbuf, res,
    send_sems, recv_sems, load_sems,
):
    loads = []
    for i, (a, b) in enumerate(((ow_in, ow), (mod_in, mod), (lat_in, lat), (cond_in, cond))):
        loads.append(pltpu.make_async_copy(a, b, load_sems.at[i]))
        loads[-1].start()
    x, s, tp = lax.axis_index("grp"), lax.axis_index("seq"), lax.axis_index("tp")
    y, z, c = s // 16, (s // 2) % 8, s % 2

    def seq_of(y_, z_, c_):
        return y_ * 16 + z_ * 2 + c_

    sib = {"seq": seq_of(y, z, 1 - c)}
    row = {"seq": seq_of(1 - y, z, c)}
    beyond = {"tp": (tp + c * (3 - 2 * y)) % 4, "seq": seq_of(1 - y, z, y)}
    right = {"seq": seq_of(y, (z + 1) % Z, c)}
    left = {"seq": seq_of(y, (z + 7) % Z, c)}

    def zm(t):
        return (z + Z - t) % Z

    def zp(t):
        return (z + t) % Z

    px, py, pz = y * 2 + z // 4, x // 2, z % 4 + 4 * (x % 2)
    moves = px != x
    partner = {"grp": px, "seq": seq_of(py, pz, c)}

    barrier = pltpu.get_barrier_semaphore()

    def greet(device):
        pl.semaphore_signal(barrier, inc=1, device_id=device, device_id_type=MESH)

    for device in (sib, row, {"seq": seq_of(1 - y, z, 1 - c)}):
        greet(device)
    for i in range(1, 4):
        greet({"grp": (x + i) % 4})
    for device in (right, left):
        greet(device)
    for i in (1, 3):
        for core in range(2):
            greet({"tp": (tp + i) % 4, "seq": seq_of(1 - y, z, core)})
    for i in range(1, 4):
        greet({"tp": (tp + i) % 4})

    @pl.when(moves)
    def _():
        greet(partner)

    pl.semaphore_wait(barrier, 15 + jnp.where(moves, 1, 0))

    ids = iter(range(N_SEMS))
    sent = []

    def remote(src, dst, device, i):
        return pltpu.make_async_remote_copy(
            src_ref=src, dst_ref=dst, send_sem=send_sems.at[i], recv_sem=recv_sems.at[i],
            device_id=device, device_id_type=MESH,
        )

    def push(src, dst, device):
        i = next(ids)
        copy = remote(src, dst, device, i)
        copy.start()
        sent.append(copy)
        return i

    def arrived(land, i):
        remote(land, land, sib, i).wait_recv()

    def ring_send(view, t):
        if t < 3:
            a, b = view(zm(t), None), view(zp(t), None)
        else:
            a, b = view(zm(t), 0), view(zp(t), 1)
        return push(a, a, right), push(b, b, left)

    def ring_wait(view, t, got):
        if t < 4:
            arrived(view(zm(t), None), got[0])
            arrived(view(zp(t), None), got[1])
        else:
            arrived(view(zm(t), 0), got[0])
            arrived(view(zp(t), 1), got[1])

    stays = y == c
    leaves = jnp.logical_not(stays)
    w_own, w_row = {}, {}
    for j in (1, 2, 0):
        w_row[j] = push(wsh.at[1 - y, j], wbuf.at[j, y, z, c], row)
        w_own[j] = pltpu.make_async_copy(wsh.at[y, j], wbuf.at[j, y, z, c], load_sems.at[4 + j])
        w_own[j].start()

    def layer_norm(block, store, lo, hi):
        use = jnp.where(block == 0, 1.0, 0.0).astype(F32)
        scale = 1.0 + mod[1, pl.ds(block, 1), :]
        shift = mod[0, pl.ds(block, 1), :]

        def step(i, carry):
            at = pl.ds(pl.multiple_of(i * 32, 32), 32)
            v = lat[at, :].astype(F32) + use * cond[at, :].astype(F32)
            center = v - jnp.mean(v, axis=-1, keepdims=True)
            var = jnp.mean(center * center, axis=-1, keepdims=True)
            store(at, (center * lax.rsqrt(var + 1e-6) * scale + shift).astype(BF16))
            return carry

        lax.fori_loop(lo, hi, step, 0)

    def store_to(k):
        def store(at, v):
            xst[k, at, :] = v

        return store

    def view_w(j):
        def view(zz, h):
            return wbuf.at[j, :, zz, c] if h is None else wbuf.at[j, :, zz, c, pl.ds(h * 48, 48)]

        return view

    w_shared = {0: [], 1: [], 2: []}

    def w_share(j, zz):
        mine = wbuf.at[j, :, zz, c]
        w_shared[j].append((push(mine, mine, sib), wbuf.at[j, :, zz, 1 - c]))

    def w_hop(j, t, got):
        if t == 0:
            w_own[j].wait()
            arrived(wbuf.at[j, 1 - y, z, c], w_row[j])
        else:
            ring_wait(view_w(j), t, got)
        if t < 4:
            got = ring_send(view_w(j), t)
        if 0 < t < 4:
            w_share(j, zm(t))
        w_share(j, zp(t))
        return got

    def w_come(j):
        for i, land in w_shared[j]:
            arrived(land, i)

    def view_o(zz, h):
        base = seq_of(y, zz, c)
        return owb.at[base] if h is None else owb.at[base, pl.ds(h * 48, 48)]

    got_w = {j: w_hop(j, 0, None) for j in (1, 2, 0)}
    for load in loads[1:]:
        load.wait()
    x_base = [next(ids) for _ in range(4)][0]
    beyond_copies = [
        pltpu.make_async_remote_copy(
            src_ref=xst.at[0, pl.ds(part * HEAD, HEAD)], dst_ref=xbuf.at[c, pl.ds(part * HEAD, HEAD)],
            send_sem=send_sems.at[x_base + part], recv_sem=recv_sems.at[x_base + 2 * part + c],
            device_id=beyond, device_id_type=MESH,
        )
        for part in range(2)
    ]
    sent.extend(beyond_copies)
    layer_norm(1 - y, store_to(0), 0, 4)
    beyond_copies[0].start()
    layer_norm(1 - y, store_to(0), 4, 8)
    beyond_copies[1].start()
    ow_id = next(ids)
    ow_copy = remote(owt, owb.at[seq_of(py, pz, c)], partner, ow_id)

    def make_out_weight():
        loads[0].wait()
        first = s * WROWS
        base = jnp.minimum(first // HEAD * HEAD, D - 2 * HEAD)
        for block in range(2):
            gates = mod[2, block:block + 1, pl.ds(pl.multiple_of(base, HEAD), 2 * HEAD)]
            gates = pltpu.roll(jnp.broadcast_to(gates, (HEAD, 2 * HEAD)), (2 * HEAD + base - first) % (2 * HEAD), 1)
            gates = jnp.transpose(gates[:, :WROWS])
            owt[:, block * HEAD:(block + 1) * HEAD] = (ow[block].astype(F32) * gates).astype(BF16)

        @pl.when(moves)
        def _():
            ow_copy.start()

        @pl.when(jnp.logical_not(moves))
        def _():
            owb[s] = owt[...]

    def make_residual():
        g = x * 4 + tp
        near = lat[:, pl.ds(pl.multiple_of(g * 3 // 2 * HEAD, HEAD), 2 * HEAD)].astype(F32)
        near = jnp.where(g % 2 == 0, near[:, :2 * WROWS], near[:, HEAD // 2:])
        res[...] = jnp.transpose(near)

    x_id = next(ids)
    x_local = pltpu.make_async_copy(xst.at[1], xbuf.at[c], load_sems.at[7])
    x_remote = remote(xst.at[1], xbuf.at[c], sib, x_id)
    for t in range(1, 5):
        for j in (1, 2, 0):
            got_w[j] = w_hop(j, t, got_w[j])
        if t == 1:
            make_out_weight()
        if t == 3:
            make_residual()
        if t < 3:
            layer_norm(y, store_to(1), 4 * t - 4, 4 * t)
        if t == 2:
            @pl.when(stays)
            def _():
                x_local.start()

            @pl.when(leaves)
            def _():
                x_remote.start()

    @pl.when(moves)
    def _():
        ow_copy.wait_send()
        arrived(owb.at[s], ow_id)

    o_y, o_s = [], []

    def o_pass(zz):
        here, there = owb.at[seq_of(y, zz, c)], owb.at[seq_of(1 - y, zz, c)]
        o_y.append((push(here, here, row), there))
        o_s.append((push(here, here, sib), owb.at[seq_of(y, zz, 1 - c)]))

    def o_hop(t, got):
        ring_wait(view_o, t, got)
        if t < 4:
            got = ring_send(view_o, t)
            o_pass(zm(t))
            o_pass(zp(t))
            return got
        o_pass(zp(t))

    got_o = ring_send(view_o, 0)
    o_pass(z)
    w_come(1)

    @pl.when(stays)
    def _():
        x_local.wait()
        arrived(xbuf.at[1 - c], x_id)

    @pl.when(leaves)
    def _():
        for core in range(2):
            for part in range(2):
                arrived(xbuf.at[core, pl.ds(part * HEAD, HEAD)], x_base + 2 * part + core)

    def head_norm(v, g):
        return v * lax.rsqrt(jnp.mean(v * v, axis=-1, keepdims=True) + 1e-6) * g

    q_gain = gain[y, 0:1, :] * (math.log2(math.e) / math.sqrt(HEAD))
    k_gain = gain[y, 1:2, :]

    def project_in(j, store):
        def step(m, carry):
            store(m, jnp.dot(xbuf[m], wbuf[j].reshape(D, HEAD), preferred_element_type=F32))
            return carry

        lax.fori_loop(0, 2, step, 0)

    def rows_of(m):
        return pl.ds(pl.multiple_of(m * ROWS, ROWS), ROWS)

    def store_k(m, v):
        kbuf[c, z, m] = jnp.transpose(head_norm(v, k_gain)).astype(BF16)

    def store_v(m, v):
        vbuf[c, z, rows_of(m), :] = v.astype(BF16)

    def store_q(m, v):
        v = head_norm(v, q_gain).astype(BF16)
        for h in range(2):
            qbuf[h, m] = v[h * HEAD:(h + 1) * HEAD]

    def view_k(zz, h):
        return kbuf.at[c, zz] if h is None else kbuf.at[c, zz, h]

    def view_v(zz, h):
        return vbuf.at[c, zz] if h is None else vbuf.at[c, zz, pl.ds(h * ROWS, ROWS)]

    project_in(1, store_k)
    got_k = ring_send(view_k, 0)
    w_come(2)
    project_in(2, store_v)
    got_v = ring_send(view_v, 0)
    got_o = o_hop(1, got_o)

    shared = {}

    def share(buf, zz, t):
        mine = buf.at[c, zz]
        shared.setdefault(t, []).append((push(mine, mine, sib), buf.at[1 - c, zz]))

    share(kbuf, z, 0)
    share(vbuf, z, 0)
    def k_hop(t, got):
        ring_wait(view_k, t, got)
        if t < 4:
            got = ring_send(view_k, t)
            share(kbuf, zm(t), t)
        share(kbuf, zp(t), t)
        return got

    def v_hop(t, got):
        ring_wait(view_v, t, got)
        if t < 4:
            got = ring_send(view_v, t)
            share(vbuf, zm(t), t)
        share(vbuf, zp(t), t)
        return got

    acc[...] = jnp.zeros_like(acc)
    ones = jnp.ones((CHIP, HEAD), BF16)
    w_come(0)
    project_in(0, store_q)

    def attend(places, halves=(0, 2)):
        lo, hi = halves
        at = slice(lo * ROWS, hi * ROWS)
        queries = qbuf[lo:hi].reshape((hi - lo) * ROWS, HEAD)
        weights = jnp.concatenate([
            jnp.exp2(jnp.dot(queries, kbuf[r, zz, h], preferred_element_type=F32)).astype(BF16)
            for r, zz in places for h in range(2)
        ], axis=1)
        values = jnp.concatenate([
            jnp.concatenate([vbuf[r, zz], ones], axis=1) for r, zz in places
        ], axis=0)
        acc[at, :] += jnp.dot(weights, values, preferred_element_type=F32)

    def shared_come(t):
        for i, land in shared[t]:
            arrived(land, i)

    def attend_shared(t):
        shared_come(t)
        attend([(1 - c, zm(t)), (1 - c, zp(t))] if t else [(1 - c, z)])

    for t in range(1, 5):
        got_k = k_hop(t, got_k)
        got_v = v_hop(t, got_v)
        if t < 4:
            got_o = o_hop(t + 1, got_o)
        attend([(c, zp(4))] if t == 4 else [(c, zm(t)), (c, zp(t))] + [(c, z)] * (t == 1))
        if t < 4:
            @pl.when(leaves)
            def _():
                attend_shared(t - 1)

    @pl.when(leaves)
    def _():
        shared_come(3)

    @pl.when(stays)
    def _():
        for t in range(3):
            attend_shared(t)
        shared_come(3)

    shared_come(4)

    def attend_last(h):
        attend([(1 - c, zm(3)), (1 - c, zp(3)), (1 - c, zp(4))], (h, h + 1))

    a_ids, a_copies = [], {}
    for h in range(2):
        attend_last(h)
        i0 = next(ids)
        next(ids)
        a_ids.append(i0)
        for m in range(2):
            lo = h * ROWS + m * HEAD
            part = acc[lo:lo + HEAD, :]
            ast[h, m] = jnp.transpose(part[:, :HEAD] / part[:, HEAD:]).astype(BF16)
            copy = pltpu.make_async_remote_copy(
                src_ref=ast.at[h, m], dst_ref=abuf.at[h, x, y],
                send_sem=send_sems.at[i0 + m], recv_sem=recv_sems.at[i0 + y],
                device_id={"seq": seq_of(c, z, m)}, device_id_type=MESH,
            )
            is_self = jnp.logical_and(stays, c == m)
            a_copies[h, m] = copy, jnp.logical_not(is_self)

            @pl.when(is_self)
            def _():
                abuf[h, x, y] = ast[h, m]

            @pl.when(jnp.logical_not(is_self))
            def _():
                copy.start()

    x_ids = {}
    for h in range(2):
        for k, b in enumerate((y, 1 - y)):
            mine = abuf.at[h, x, b]
            if k:
                arrived(mine, a_ids[h] + b)
            else:
                @pl.when(leaves)
                def _():
                    arrived(mine, a_ids[h] + b)
            for d in (2, 1, 3):
                x_ids[h, k, d] = push(mine, mine, {"grp": (x + d) % 4})

    for i, land in o_y:
        arrived(land, i)
    for zz in range(Z):
        here = owb.at[seq_of(1 - y, zz, c)]
        o_s.append((push(here, here, sib), owb.at[seq_of(1 - y, zz, 1 - c)]))
    for i, land in o_s:
        arrived(land, i)

    def project(h, yh):
        total = None
        for xx in range(4):
            w = owb[pl.ds(xx * 8 + yh * 2, 2)].reshape(2 * WROWS, 2 * HEAD)
            a = abuf[h, xx].reshape(2 * HEAD, HEAD)
            term = jnp.dot(w, a, preferred_element_type=F32)
            total = term if total is None else total + term
        return total

    r_ids, totals = {}, []
    for h in range(2):
        for d in (1, 3, 2):
            for k, b in enumerate((y, 1 - y)):
                arrived(abuf.at[h, (x + 4 - d) % 4, b], x_ids[h, k, d])
        r_ids[h] = [next(ids) for _ in range(3)][0] - 1

        def piece(h, d):
            return remote(pst.at[h, d], rbuf.at[h, d], {"tp": (tp + d) % 4}, r_ids[h] + d)

        def step(i, carry):
            d = 1 + (i + 1) % 3
            pst[h, d] = project(h, (tp + d) % 4).astype(BF16)
            piece(h, d).start()
            return carry

        lax.fori_loop(0, 3, step, 0)
        totals.append(project(h, tp))

    for h in range(2):
        total = totals[h]
        for d in (1, 3, 2):
            arrived(rbuf.at[h, d], r_ids[h] + d)
            total = total + rbuf[h, d].astype(F32)
        at = slice(h * HEAD, (h + 1) * HEAD)
        out[:, at] = res[:, at] + total

    for copy in sent:
        copy.wait_send()
    for h in range(2):
        for d in range(1, 4):
            piece(h, d).wait_send()

    @pl.when(leaves)
    def _():
        x_remote.wait_send()

    for copy, remote_target in a_copies.values():
        @pl.when(remote_target)
        def _():
            copy.wait_send()


def body(latent, condition, modulation, qk_gain, qkv_weight, out_weight):
    modulation = jnp.transpose(modulation, (1, 0, 2))
    vm = pl.BlockSpec(memory_space=pltpu.VMEM)
    hbm = pl.BlockSpec(memory_space=pltpu.HBM)
    mixed = pl.pallas_call(
        kernel,
        out_shape=jax.ShapeDtypeStruct((2 * WROWS, ROWS), F32),
        in_specs=[hbm, hbm, hbm, vm, hbm, hbm],
        out_specs=vm,
        scratch_shapes=[
            pltpu.VMEM((ROWS, D), BF16),
            pltpu.VMEM((ROWS, D), BF16),
            pltpu.VMEM((3, 2, D), F32),
            pltpu.VMEM((2, WROWS, HEAD), BF16),
            pltpu.VMEM((WROWS, 2 * HEAD), BF16),
            pltpu.VMEM((3, 2, Z, 2, WROWS, HEAD), BF16),
            pltpu.VMEM((2, ROWS, D), BF16),
            pltpu.VMEM((2, ROWS, D), BF16),
            pltpu.VMEM((2, 2, HEAD, HEAD), BF16),
            pltpu.VMEM((2, Z, 2, HEAD, ROWS), BF16),
            pltpu.VMEM((2, Z, CHIP, HEAD), BF16),
            pltpu.VMEM((32, WROWS, 2 * HEAD), BF16),
            pltpu.VMEM((CHIP, 2 * HEAD), F32),
            pltpu.VMEM((2, 4, 2, HEAD, HEAD), BF16),
            pltpu.VMEM((2, 2, HEAD, HEAD), BF16),
            pltpu.VMEM((2, 4, 2 * WROWS, HEAD), BF16),
            pltpu.VMEM((2, 4, 2 * WROWS, HEAD), BF16),
            pltpu.VMEM((2 * WROWS, ROWS), F32),
            pltpu.SemaphoreType.DMA((N_SEMS,)),
            pltpu.SemaphoreType.DMA((N_SEMS,)),
            pltpu.SemaphoreType.DMA((8,)),
        ],
        compiler_params=pltpu.CompilerParams(
            collective_id=0, has_side_effects=True, vmem_limit_bytes=56 * 1024 * 1024
        ),
        cost_estimate=pl.CostEstimate(
            flops=3_900_000_000, bytes_accessed=4_000_000, transcendentals=4_200_000
        ),
    )(latent, condition, modulation, qk_gain, qkv_weight, jnp.transpose(out_weight, (0, 2, 1)))
    return mixed.astype(BF16).T


def solution(mesh):
    return jax.shard_map(
        body,
        mesh=mesh,
        in_specs=(
            P("seq", None),
            P("seq", None),
            P(),
            P(),
            P(None, None, "seq", ("grp", "tp")),
            P(None, ("grp", "tp"), "seq"),
        ),
        out_specs=P("seq", ("grp", "tp")),
        check_vma=False,
    )
```

```python
import math

import jax
import jax.numpy as jnp
from jax import lax
from jax.experimental import pallas as pl
from jax.experimental.pallas import tpu as pltpu
from jax.sharding import PartitionSpec as P

MESH = pl.DeviceIdType.MESH
BF16, F32 = jnp.bfloat16, jnp.float32
Z = 8
ROWS = 256
CHIP = 2 * ROWS
D = 3072
HEAD = 128
WROWS = 96
N_SEMS = 200


def kernel(
    lat_in, cond_in, mod_in, gain, wsh, ow_in, out,
    lat, cond, mod, ow, owt, wbuf, xbuf, xst, qbuf, kbuf, vbuf, owb, acc, abuf, ast, pst, rbuf, res, give, take,
    send_sems, recv_sems, load_sems,
):
    loads = []
    for i, (a, b) in enumerate(((ow_in, ow), (mod_in, mod), (lat_in, lat), (cond_in, cond))):
        loads.append(pltpu.make_async_copy(a, b, load_sems.at[i]))
        loads[-1].start()
    x, s, tp = lax.axis_index("grp"), lax.axis_index("seq"), lax.axis_index("tp")
    y, z, c = s // 16, (s // 2) % 8, s % 2

    def seq_of(y_, z_, c_):
        return y_ * 16 + z_ * 2 + c_

    sib = {"seq": seq_of(y, z, 1 - c)}
    row = {"seq": seq_of(1 - y, z, c)}
    beyond = {"tp": (tp + c * (3 - 2 * y)) % 4, "seq": seq_of(1 - y, z, y)}
    right = {"seq": seq_of(y, (z + 1) % Z, c)}
    left = {"seq": seq_of(y, (z + 7) % Z, c)}

    def zm(t):
        return (z + Z - t) % Z

    def zp(t):
        return (z + t) % Z

    px, py, pz = y * 2 + z // 4, x // 2, z % 4 + 4 * (x % 2)
    moves = px != x
    partner = {"grp": px, "seq": seq_of(py, pz, c)}

    barrier = pltpu.get_barrier_semaphore()

    def greet(device):
        pl.semaphore_signal(barrier, inc=1, device_id=device, device_id_type=MESH)

    flat = x * 4 + y * 2 + c
    for i in range(1, 16):
        f = (flat + i) % 16
        greet({"grp": f // 4, "seq": seq_of((f // 2) % 2, z, f % 2)})
    for device in (right, left):
        greet(device)
    for i in (1, 3):
        for core in range(2):
            greet({"tp": (tp + i) % 4, "seq": seq_of(1 - y, z, core)})
    for i in range(1, 4):
        greet({"tp": (tp + i) % 4})

    @pl.when(moves)
    def _():
        greet(partner)

    pl.semaphore_wait(barrier, 24 + jnp.where(moves, 1, 0))

    ids = iter(range(N_SEMS))
    sent = []

    def remote(src, dst, device, i):
        return pltpu.make_async_remote_copy(
            src_ref=src, dst_ref=dst, send_sem=send_sems.at[i], recv_sem=recv_sems.at[i],
            device_id=device, device_id_type=MESH,
        )

    def push(src, dst, device):
        i = next(ids)
        copy = remote(src, dst, device, i)
        copy.start()
        sent.append(copy)
        return i

    def arrived(land, i):
        remote(land, land, sib, i).wait_recv()

    def ring_send(view, t):
        if t < 3:
            a, b = view(zm(t), None), view(zp(t), None)
        else:
            a, b = view(zm(t), 0), view(zp(t), 1)
        return push(a, a, right), push(b, b, left)

    def ring_wait(view, t, got):
        if t < 4:
            arrived(view(zm(t), None), got[0])
            arrived(view(zp(t), None), got[1])
        else:
            arrived(view(zm(t), 0), got[0])
            arrived(view(zp(t), 1), got[1])

    stays = y == c
    leaves = jnp.logical_not(stays)
    w_own, w_row = {}, {}
    for j in (1, 2, 0):
        w_row[j] = push(wsh.at[1 - y, j], wbuf.at[j, y, z, c], row)
        w_own[j] = pltpu.make_async_copy(wsh.at[y, j], wbuf.at[j, y, z, c], load_sems.at[4 + j])
        w_own[j].start()

    ow_id = next(ids)
    ow_copy = remote(owt, owb.at[seq_of(py, pz, c)], partner, ow_id)
    loads[0].wait()
    loads[1].wait()
    first = s * WROWS
    base = jnp.minimum(first // HEAD * HEAD, D - 2 * HEAD)
    for block in range(2):
        gates = mod[2, block:block + 1, pl.ds(pl.multiple_of(base, HEAD), 2 * HEAD)]
        gates = pltpu.roll(jnp.broadcast_to(gates, (HEAD, 2 * HEAD)), (2 * HEAD + base - first) % (2 * HEAD), 1)
        gates = jnp.transpose(gates[:, :WROWS])
        owt[:, block * HEAD:(block + 1) * HEAD] = (ow[block].astype(F32) * gates).astype(BF16)

    @pl.when(moves)
    def _():
        ow_copy.start()

    @pl.when(jnp.logical_not(moves))
    def _():
        owb[s] = owt[...]

    def layer_norm(block, store, lo, hi):
        use = jnp.where(block == 0, 1.0, 0.0).astype(F32)
        scale = 1.0 + mod[1, pl.ds(block, 1), :]
        shift = mod[0, pl.ds(block, 1), :]

        def step(i, carry):
            at = pl.ds(pl.multiple_of(i * 32, 32), 32)
            v = lat[at, :].astype(F32) + use * cond[at, :].astype(F32)
            center = v - jnp.mean(v, axis=-1, keepdims=True)
            var = jnp.mean(center * center, axis=-1, keepdims=True)
            store(at, (center * lax.rsqrt(var + 1e-6) * scale + shift).astype(BF16))
            return carry

        lax.fori_loop(lo, hi, step, 0)

    def store_to(k):
        def store(at, v):
            xst[k, at, :] = v

        return store

    def view_w(j):
        def view(zz, h):
            return wbuf.at[j, :, zz, c] if h is None else wbuf.at[j, :, zz, c, pl.ds(h * 48, 48)]

        return view

    w_shared = {0: [], 1: [], 2: []}

    def w_share(j, zz):
        mine = wbuf.at[j, :, zz, c]
        w_shared[j].append((push(mine, mine, sib), wbuf.at[j, :, zz, 1 - c]))

    def w_hop(j, t, got):
        if t == 0:
            w_own[j].wait()
            arrived(wbuf.at[j, 1 - y, z, c], w_row[j])
        else:
            ring_wait(view_w(j), t, got)
        if 0 < t < 4:
            w_share(j, zm(t))
        if t < 4:
            got = ring_send(view_w(j), t)
        w_share(j, zp(t))
        return got

    def w_come(j):
        for i, land in w_shared[j]:
            arrived(land, i)

    def view_o(zz, h):
        base = seq_of(y, zz, c)
        return owb.at[base] if h is None else owb.at[base, pl.ds(h * 48, 48)]

    got_w = {j: w_hop(j, 0, None) for j in (1, 2, 0)}
    for load in loads[2:]:
        load.wait()
    x_base = [next(ids) for _ in range(4)][0]
    beyond_copies = [
        pltpu.make_async_remote_copy(
            src_ref=xst.at[0, pl.ds(part * HEAD, HEAD)], dst_ref=xbuf.at[c, pl.ds(part * HEAD, HEAD)],
            send_sem=send_sems.at[x_base + part], recv_sem=recv_sems.at[x_base + 2 * part + c],
            device_id=beyond, device_id_type=MESH,
        )
        for part in range(2)
    ]
    sent.extend(beyond_copies)
    layer_norm(1 - y, store_to(0), 0, 4)
    beyond_copies[0].start()
    layer_norm(1 - y, store_to(0), 4, 8)
    beyond_copies[1].start()
    g = x * 4 + tp
    near = lat[:, pl.ds(pl.multiple_of(g * 3 // 2 * HEAD, HEAD), 2 * HEAD)].astype(F32)
    near = jnp.where(g % 2 == 0, near[:, :2 * WROWS], near[:, HEAD // 2:])
    res[...] = jnp.transpose(near)

    x_id = next(ids)
    x_local = pltpu.make_async_copy(xst.at[1], xbuf.at[c], load_sems.at[7])
    x_remote = remote(xst.at[1], xbuf.at[c], sib, x_id)
    for t in range(1, 5):
        for j in (1, 2, 0):
            got_w[j] = w_hop(j, t, got_w[j])
        if t < 3:
            layer_norm(y, store_to(1), 4 * t - 4, 4 * t)
        if t == 2:
            @pl.when(stays)
            def _():
                x_local.start()

            @pl.when(leaves)
            def _():
                x_remote.start()

    @pl.when(moves)
    def _():
        ow_copy.wait_send()
        arrived(owb.at[s], ow_id)

    o_y, o_s = [], []

    def o_pass(zz):
        here, there = owb.at[seq_of(y, zz, c)], owb.at[seq_of(1 - y, zz, c)]
        o_y.append((push(here, here, row), there))
        o_s.append((push(here, here, sib), owb.at[seq_of(y, zz, 1 - c)]))

    def o_hop(t, got):
        ring_wait(view_o, t, got)
        if t < 4:
            got = ring_send(view_o, t)
            o_pass(zm(t))
            o_pass(zp(t))
            return got
        o_pass(zp(t))

    got_o = ring_send(view_o, 0)
    o_pass(z)
    w_come(1)

    @pl.when(stays)
    def _():
        x_local.wait()
        arrived(xbuf.at[1 - c], x_id)

    @pl.when(leaves)
    def _():
        for core in range(2):
            for part in range(2):
                arrived(xbuf.at[core, pl.ds(part * HEAD, HEAD)], x_base + 2 * part + core)

    def head_norm(v, g):
        return v * lax.rsqrt(jnp.mean(v * v, axis=-1, keepdims=True) + 1e-6) * g

    q_gain = gain[y, 0:1, :] * (math.log2(math.e) / math.sqrt(HEAD))
    k_gain = gain[y, 1:2, :]

    def project_in(j, store):
        def step(m, carry):
            store(m, jnp.dot(xbuf[m], wbuf[j].reshape(D, HEAD), preferred_element_type=F32))
            return carry

        lax.fori_loop(0, 2, step, 0)

    def rows_of(m):
        return pl.ds(pl.multiple_of(m * ROWS, ROWS), ROWS)

    def store_k(m, v):
        kbuf[z, m] = jnp.transpose(head_norm(v, k_gain)).astype(BF16)

    def store_v(m, v):
        vbuf[z, rows_of(m), :] = v.astype(BF16)

    def store_q(m, v):
        v = head_norm(v, q_gain).astype(BF16)
        for h in range(2):
            qbuf[c, h, m] = v[h * HEAD:(h + 1) * HEAD]

    def view_k(zz, h):
        return kbuf.at[zz] if h is None else kbuf.at[zz, h]

    def view_v(zz, h):
        return vbuf.at[zz] if h is None else vbuf.at[zz, pl.ds(h * ROWS, ROWS)]

    def hop(view, t, got):
        ring_wait(view, t, got)
        return ring_send(view, t) if t < 4 else None

    project_in(1, store_k)
    got_k = ring_send(view_k, 0)
    w_come(2)
    project_in(2, store_v)
    got_v = ring_send(view_v, 0)
    got_o = o_hop(1, got_o)

    acc[...] = jnp.zeros_like(acc)
    ones = jnp.ones((CHIP, HEAD), BF16)
    w_come(0)
    project_in(0, store_q)
    q_id = push(qbuf.at[c], qbuf.at[c], sib)

    def attend(places, r, halves=(0, 2)):
        lo, hi = halves
        at = slice(lo * ROWS, hi * ROWS)
        queries = qbuf[r, lo:hi].reshape((hi - lo) * ROWS, HEAD)
        weights = jnp.concatenate([
            jnp.exp2(jnp.dot(queries, kbuf[zz, h], preferred_element_type=F32)).astype(BF16)
            for zz in places for h in range(2)
        ], axis=1)
        values = jnp.concatenate([
            jnp.concatenate([vbuf[zz], ones], axis=1) for zz in places
        ], axis=0)
        acc[r, at, :] += jnp.dot(weights, values, preferred_element_type=F32)

    for t in range(1, 5):
        got_k = hop(view_k, t, got_k)
        got_v = hop(view_v, t, got_v)
        if t < 4:
            got_o = o_hop(t + 1, got_o)
            places = [zm(t), zp(t)] + [z] * (t == 1)
            attend(places, c)

            @pl.when(leaves)
            def _():
                if t == 1:
                    arrived(qbuf.at[1 - c], q_id)
                attend(places, 1 - c)

    @pl.when(stays)
    def _():
        arrived(qbuf.at[1 - c], q_id)
        for t in range(1, 4):
            attend([zm(t), zp(t)] + [z] * (t == 1), 1 - c)

    given = []
    for h in range(2):
        attend([zp(4)], 1 - c, (h, h + 1))
        give[h] = acc[1 - c, h * ROWS:(h + 1) * ROWS, :].astype(BF16)
        given.append(push(give.at[h], take.at[h], sib))

    def attend_last(h):
        attend([zp(4)], c, (h, h + 1))
        arrived(take.at[h], given[h])

    a_ids, a_copies = [], {}
    for h in range(2):
        attend_last(h)
        i0 = next(ids)
        next(ids)
        a_ids.append(i0)
        for m in range(2):
            lo = h * ROWS + m * HEAD
            part = acc[c, lo:lo + HEAD, :] + take[h, m * HEAD:(m + 1) * HEAD, :].astype(F32)
            ast[h, m] = jnp.transpose(part[:, :HEAD] / part[:, HEAD:]).astype(BF16)
            copy = pltpu.make_async_remote_copy(
                src_ref=ast.at[h, m], dst_ref=abuf.at[h, x, y],
                send_sem=send_sems.at[i0 + m], recv_sem=recv_sems.at[i0 + y],
                device_id={"seq": seq_of(c, z, m)}, device_id_type=MESH,
            )
            is_self = jnp.logical_and(stays, c == m)
            a_copies[h, m] = copy, jnp.logical_not(is_self)

            @pl.when(is_self)
            def _():
                abuf[h, x, y] = ast[h, m]

            @pl.when(jnp.logical_not(is_self))
            def _():
                copy.start()

    x_ids = {}
    for h in range(2):
        for k, b in enumerate((y, 1 - y)):
            mine = abuf.at[h, x, b]
            if k:
                arrived(mine, a_ids[h] + b)
            else:
                @pl.when(leaves)
                def _():
                    arrived(mine, a_ids[h] + b)
            for d in (2, 1, 3):
                x_ids[h, k, d] = push(mine, mine, {"grp": (x + d) % 4})

    for i, land in o_y:
        arrived(land, i)
    for zz in range(Z):
        here = owb.at[seq_of(1 - y, zz, c)]
        o_s.append((push(here, here, sib), owb.at[seq_of(1 - y, zz, 1 - c)]))
    for i, land in o_s:
        arrived(land, i)

    def project(h, yh):
        total = None
        for xx in range(4):
            w = owb[pl.ds(xx * 8 + yh * 2, 2)].reshape(2 * WROWS, 2 * HEAD)
            a = abuf[h, xx].reshape(2 * HEAD, HEAD)
            term = jnp.dot(w, a, preferred_element_type=F32)
            total = term if total is None else total + term
        return total

    r_ids, totals = {}, []
    for h in range(2):
        for d in (1, 3, 2):
            for k, b in enumerate((y, 1 - y)):
                arrived(abuf.at[h, (x + 4 - d) % 4, b], x_ids[h, k, d])
        r_ids[h] = [next(ids) for _ in range(3)][0] - 1

        def piece(h, d):
            return remote(pst.at[h, d], rbuf.at[h, d], {"tp": (tp + d) % 4}, r_ids[h] + d)

        def step(i, carry):
            d = 1 + (i + 1) % 3
            pst[h, d] = project(h, (tp + d) % 4).astype(BF16)
            piece(h, d).start()
            return carry

        lax.fori_loop(0, 3, step, 0)
        totals.append(project(h, tp))

    for h in range(2):
        total = totals[h]
        for d in (1, 3, 2):
            arrived(rbuf.at[h, d], r_ids[h] + d)
            total = total + rbuf[h, d].astype(F32)
        at = slice(h * HEAD, (h + 1) * HEAD)
        out[:, at] = res[:, at] + total

    for copy in sent:
        copy.wait_send()
    for h in range(2):
        for d in range(1, 4):
            piece(h, d).wait_send()

    @pl.when(leaves)
    def _():
        x_remote.wait_send()

    for copy, remote_target in a_copies.values():
        @pl.when(remote_target)
        def _():
            copy.wait_send()


def body(latent, condition, modulation, qk_gain, qkv_weight, out_weight):
    modulation = jnp.transpose(modulation, (1, 0, 2))
    vm = pl.BlockSpec(memory_space=pltpu.VMEM)
    hbm = pl.BlockSpec(memory_space=pltpu.HBM)
    mixed = pl.pallas_call(
        kernel,
        out_shape=jax.ShapeDtypeStruct((2 * WROWS, ROWS), F32),
        in_specs=[hbm, hbm, hbm, vm, hbm, hbm],
        out_specs=vm,
        scratch_shapes=[
            pltpu.VMEM((ROWS, D), BF16),
            pltpu.VMEM((ROWS, D), BF16),
            pltpu.VMEM((3, 2, D), F32),
            pltpu.VMEM((2, WROWS, HEAD), BF16),
            pltpu.VMEM((WROWS, 2 * HEAD), BF16),
            pltpu.VMEM((3, 2, Z, 2, WROWS, HEAD), BF16),
            pltpu.VMEM((2, ROWS, D), BF16),
            pltpu.VMEM((2, ROWS, D), BF16),
            pltpu.VMEM((2, 2, 2, HEAD, HEAD), BF16),
            pltpu.VMEM((Z, 2, HEAD, ROWS), BF16),
            pltpu.VMEM((Z, CHIP, HEAD), BF16),
            pltpu.VMEM((32, WROWS, 2 * HEAD), BF16),
            pltpu.VMEM((2, CHIP, 2 * HEAD), F32),
            pltpu.VMEM((2, 4, 2, HEAD, HEAD), BF16),
            pltpu.VMEM((2, 2, HEAD, HEAD), BF16),
            pltpu.VMEM((2, 4, 2 * WROWS, HEAD), BF16),
            pltpu.VMEM((2, 4, 2 * WROWS, HEAD), BF16),
            pltpu.VMEM((2 * WROWS, ROWS), F32),
            pltpu.VMEM((2, ROWS, 2 * HEAD), BF16),
            pltpu.VMEM((2, ROWS, 2 * HEAD), BF16),
            pltpu.SemaphoreType.DMA((N_SEMS,)),
            pltpu.SemaphoreType.DMA((N_SEMS,)),
            pltpu.SemaphoreType.DMA((8,)),
        ],
        compiler_params=pltpu.CompilerParams(
            collective_id=0, has_side_effects=True, vmem_limit_bytes=56 * 1024 * 1024
        ),
        cost_estimate=pl.CostEstimate(
            flops=3_900_000_000, bytes_accessed=4_000_000, transcendentals=4_200_000
        ),
    )(latent, condition, modulation, qk_gain, qkv_weight, jnp.transpose(out_weight, (0, 2, 1)))
    return mixed.astype(BF16).T


def solution(mesh):
    return jax.shard_map(
        body,
        mesh=mesh,
        in_specs=(
            P("seq", None),
            P("seq", None),
            P(),
            P(),
            P(None, None, "seq", ("grp", "tp")),
            P(None, ("grp", "tp"), "seq"),
        ),
        out_specs=P("seq", ("grp", "tp")),
        check_vma=False,
    )
```

```python
import math

import jax
import jax.numpy as jnp
from jax import lax
from jax.experimental import pallas as pl
from jax.experimental.pallas import tpu as pltpu
from jax.sharding import PartitionSpec as P

MESH = pl.DeviceIdType.MESH
BF16, F32 = jnp.bfloat16, jnp.float32
Z = 8
ROWS = 256
CHIP = 2 * ROWS
D = 3072
HEAD = 128
WROWS = 96
N_SEMS = 200


def kernel(
    lat_in, cond_in, mod_in, gain, wsh, ow_in, out,
    lat, cond, mod, ow, owt, wbuf, xbuf, xst, qbuf, kbuf, vbuf, owb, acc, abuf, ast, pst, rbuf, res, give, take,
    send_sems, recv_sems, load_sems,
):
    loads = []
    for i, (a, b) in enumerate(((ow_in, ow), (mod_in, mod), (lat_in, lat), (cond_in, cond))):
        loads.append(pltpu.make_async_copy(a, b, load_sems.at[i]))
        loads[-1].start()
    x, s, tp = lax.axis_index("grp"), lax.axis_index("seq"), lax.axis_index("tp")
    y, z, c = s // 16, (s // 2) % 8, s % 2

    def seq_of(y_, z_, c_):
        return y_ * 16 + z_ * 2 + c_

    sib = {"seq": seq_of(y, z, 1 - c)}
    row = {"seq": seq_of(1 - y, z, c)}
    beyond = {"tp": (tp + c * (3 - 2 * y)) % 4, "seq": seq_of(1 - y, z, y)}
    right = {"seq": seq_of(y, (z + 1) % Z, c)}
    left = {"seq": seq_of(y, (z + 7) % Z, c)}

    def zm(t):
        return (z + Z - t) % Z

    def zp(t):
        return (z + t) % Z

    px, py, pz = y * 2 + z // 4, x // 2, z % 4 + 4 * (x % 2)
    moves = px != x
    partner = {"grp": px, "seq": seq_of(py, pz, c)}

    barrier = pltpu.get_barrier_semaphore()

    def greet(device):
        pl.semaphore_signal(barrier, inc=1, device_id=device, device_id_type=MESH)

    flat = x * 4 + y * 2 + c
    for i in range(1, 16):
        f = (flat + i) % 16
        greet({"grp": f // 4, "seq": seq_of((f // 2) % 2, z, f % 2)})
    for device in (right, left):
        greet(device)
    for i in (1, 3):
        for core in range(2):
            greet({"tp": (tp + i) % 4, "seq": seq_of(1 - y, z, core)})
    for i in range(1, 4):
        greet({"tp": (tp + i) % 4})

    @pl.when(moves)
    def _():
        greet(partner)

    pl.semaphore_wait(barrier, 24 + jnp.where(moves, 1, 0))

    ids = iter(range(N_SEMS))
    sent = []

    def remote(src, dst, device, i):
        return pltpu.make_async_remote_copy(
            src_ref=src, dst_ref=dst, send_sem=send_sems.at[i], recv_sem=recv_sems.at[i],
            device_id=device, device_id_type=MESH,
        )

    def push(src, dst, device):
        i = next(ids)
        copy = remote(src, dst, device, i)
        copy.start()
        sent.append(copy)
        return i

    def arrived(land, i):
        remote(land, land, sib, i).wait_recv()

    def ring_send(view, t):
        if t < 3:
            a, b = view(zm(t), None), view(zp(t), None)
        else:
            a, b = view(zm(t), 0), view(zp(t), 1)
        return push(a, a, right), push(b, b, left)

    def ring_wait(view, t, got):
        if t < 4:
            arrived(view(zm(t), None), got[0])
            arrived(view(zp(t), None), got[1])
        else:
            arrived(view(zm(t), 0), got[0])
            arrived(view(zp(t), 1), got[1])

    stays = y == c
    leaves = jnp.logical_not(stays)
    w_own, w_row = {}, {}
    for j in (1, 2, 0):
        w_row[j] = push(wsh.at[1 - y, j], wbuf.at[j, y, z, c], row)
        w_own[j] = pltpu.make_async_copy(wsh.at[y, j], wbuf.at[j, y, z, c], load_sems.at[4 + j])
        w_own[j].start()

    ow_id = next(ids)
    ow_copy = remote(owt, owb.at[seq_of(py, pz, c)], partner, ow_id)
    loads[0].wait()
    loads[1].wait()
    first = s * WROWS
    base = jnp.minimum(first // HEAD * HEAD, D - 2 * HEAD)
    for block in range(2):
        gates = mod[2, block:block + 1, pl.ds(pl.multiple_of(base, HEAD), 2 * HEAD)]
        gates = pltpu.roll(jnp.broadcast_to(gates, (HEAD, 2 * HEAD)), (2 * HEAD + base - first) % (2 * HEAD), 1)
        gates = jnp.transpose(gates[:, :WROWS])
        owt[:, block * HEAD:(block + 1) * HEAD] = (ow[block].astype(F32) * gates).astype(BF16)

    @pl.when(moves)
    def _():
        ow_copy.start()

    @pl.when(jnp.logical_not(moves))
    def _():
        owb[s] = owt[...]

    def layer_norm(block, store, lo, hi):
        use = jnp.where(block == 0, 1.0, 0.0).astype(F32)
        scale = 1.0 + mod[1, pl.ds(block, 1), :]
        shift = mod[0, pl.ds(block, 1), :]

        def step(i, carry):
            at = pl.ds(pl.multiple_of(i * 32, 32), 32)
            v = lat[at, :].astype(F32) + use * cond[at, :].astype(F32)
            center = v - jnp.mean(v, axis=-1, keepdims=True)
            var = jnp.mean(center * center, axis=-1, keepdims=True)
            store(at, (center * lax.rsqrt(var + 1e-6) * scale + shift).astype(BF16))
            return carry

        lax.fori_loop(lo, hi, step, 0)

    def store_to(k):
        def store(at, v):
            xst[k, at, :] = v

        return store

    def view_w(j):
        def view(zz, h):
            return wbuf.at[j, :, zz, c] if h is None else wbuf.at[j, :, zz, c, pl.ds(h * 48, 48)]

        return view

    w_shared = {0: [], 1: [], 2: []}

    def w_share(j, zz):
        mine = wbuf.at[j, :, zz, c]
        w_shared[j].append((push(mine, mine, sib), wbuf.at[j, :, zz, 1 - c]))

    def w_hop(j, t, got):
        if t == 0:
            w_own[j].wait()
            arrived(wbuf.at[j, 1 - y, z, c], w_row[j])
        else:
            ring_wait(view_w(j), t, got)
        if 0 < t < 4:
            w_share(j, zm(t))
        if t < 4:
            got = ring_send(view_w(j), t)
        w_share(j, zp(t))
        return got

    def w_come(j):
        for i, land in w_shared[j]:
            arrived(land, i)

    def view_o(zz, h):
        base = seq_of(y, zz, c)
        return owb.at[base] if h is None else owb.at[base, pl.ds(h * 48, 48)]

    got_w = {j: w_hop(j, 0, None) for j in (1, 2, 0)}
    for load in loads[2:]:
        load.wait()
    x_base = [next(ids) for _ in range(4)][0]
    beyond_copies = [
        pltpu.make_async_remote_copy(
            src_ref=xst.at[0, pl.ds(part * HEAD, HEAD)], dst_ref=xbuf.at[c, pl.ds(part * HEAD, HEAD)],
            send_sem=send_sems.at[x_base + part], recv_sem=recv_sems.at[x_base + 2 * part + c],
            device_id=beyond, device_id_type=MESH,
        )
        for part in range(2)
    ]
    sent.extend(beyond_copies)
    layer_norm(1 - y, store_to(0), 0, 4)
    beyond_copies[0].start()
    layer_norm(1 - y, store_to(0), 4, 8)
    beyond_copies[1].start()
    g = x * 4 + tp
    near = lat[:, pl.ds(pl.multiple_of(g * 3 // 2 * HEAD, HEAD), 2 * HEAD)].astype(F32)
    near = jnp.where(g % 2 == 0, near[:, :2 * WROWS], near[:, HEAD // 2:])
    res[...] = jnp.transpose(near)

    x_id = next(ids)
    x_local = pltpu.make_async_copy(xst.at[1], xbuf.at[c], load_sems.at[7])
    x_remote = remote(xst.at[1], xbuf.at[c], sib, x_id)
    for t in range(1, 5):
        for j in (1, 2, 0):
            got_w[j] = w_hop(j, t, got_w[j])
        if t == 1:
            @pl.when(moves)
            def _():
                ow_copy.wait_send()
                arrived(owb.at[s], ow_id)

        else:
            ring_wait(view_o, t - 1, got_o)
        got_o = ring_send(view_o, t - 1)
        if t < 3:
            layer_norm(y, store_to(1), 4 * t - 4, 4 * t)
        if t == 2:
            @pl.when(stays)
            def _():
                x_local.start()

            @pl.when(leaves)
            def _():
                x_remote.start()

    o_y, o_s = [], []

    def o_pass(zz):
        here, there = owb.at[seq_of(y, zz, c)], owb.at[seq_of(1 - y, zz, c)]
        o_y.append((push(here, here, row), there))
        o_s.append((push(here, here, sib), owb.at[seq_of(y, zz, 1 - c)]))

    w_come(1)

    @pl.when(stays)
    def _():
        x_local.wait()
        arrived(xbuf.at[1 - c], x_id)

    @pl.when(leaves)
    def _():
        for core in range(2):
            for part in range(2):
                arrived(xbuf.at[core, pl.ds(part * HEAD, HEAD)], x_base + 2 * part + core)

    def head_norm(v, g):
        return v * lax.rsqrt(jnp.mean(v * v, axis=-1, keepdims=True) + 1e-6) * g

    q_gain = gain[y, 0:1, :] * (math.log2(math.e) / math.sqrt(HEAD))
    k_gain = gain[y, 1:2, :]

    def project_in(j, store):
        def step(m, carry):
            store(m, jnp.dot(xbuf[m], wbuf[j].reshape(D, HEAD), preferred_element_type=F32))
            return carry

        lax.fori_loop(0, 2, step, 0)

    def rows_of(m):
        return pl.ds(pl.multiple_of(m * ROWS, ROWS), ROWS)

    def store_k(m, v):
        kbuf[z, m] = jnp.transpose(head_norm(v, k_gain)).astype(BF16)

    def store_v(m, v):
        vbuf[z, rows_of(m), :] = v.astype(BF16)

    def store_q(m, v):
        v = head_norm(v, q_gain).astype(BF16)
        for h in range(2):
            qbuf[c, h, m] = v[h * HEAD:(h + 1) * HEAD]

    def view_k(zz, h):
        return kbuf.at[zz] if h is None else kbuf.at[zz, h]

    def view_v(zz, h):
        return vbuf.at[zz] if h is None else vbuf.at[zz, pl.ds(h * ROWS, ROWS)]

    def hop(view, t, got):
        ring_wait(view, t, got)
        return ring_send(view, t) if t < 4 else None

    project_in(1, store_k)
    got_k = ring_send(view_k, 0)
    w_come(2)
    project_in(2, store_v)
    got_v = ring_send(view_v, 0)
    ring_wait(view_o, 4, got_o)

    acc[...] = jnp.zeros_like(acc)
    ones = jnp.ones((CHIP, HEAD), BF16)
    w_come(0)
    project_in(0, store_q)
    q_id = push(qbuf.at[c], qbuf.at[c], sib)

    def attend(places, r, halves=(0, 2)):
        lo, hi = halves
        at = slice(lo * ROWS, hi * ROWS)
        queries = qbuf[r, lo:hi].reshape((hi - lo) * ROWS, HEAD)
        weights = jnp.concatenate([
            jnp.exp2(jnp.dot(queries, kbuf[zz, h], preferred_element_type=F32)).astype(BF16)
            for zz in places for h in range(2)
        ], axis=1)
        values = jnp.concatenate([
            jnp.concatenate([vbuf[zz], ones], axis=1) for zz in places
        ], axis=0)
        acc[r, at, :] += jnp.dot(weights, values, preferred_element_type=F32)

    for t in range(1, 5):
        got_k = hop(view_k, t, got_k)
        got_v = hop(view_v, t, got_v)
        if t < 4:
            for zz in ((z, zm(1), zp(1)), (zm(2), zp(2), zm(3)), (zp(3), zp(4)))[t - 1]:
                o_pass(zz)
            places = [zm(t), zp(t)] + [z] * (t == 1)
            attend(places, c)

            @pl.when(leaves)
            def _():
                if t == 1:
                    arrived(qbuf.at[1 - c], q_id)
                attend(places, 1 - c)

    @pl.when(stays)
    def _():
        arrived(qbuf.at[1 - c], q_id)
        for t in range(1, 4):
            attend([zm(t), zp(t)] + [z] * (t == 1), 1 - c)

    given = []
    for h in range(2):
        attend([zp(4)], 1 - c, (h, h + 1))
        give[h] = acc[1 - c, h * ROWS:(h + 1) * ROWS, :].astype(BF16)
        given.append(push(give.at[h], take.at[h], sib))

    def attend_last(h):
        attend([zp(4)], c, (h, h + 1))
        arrived(take.at[h], given[h])

    a_ids, a_copies = [], {}
    for h in range(2):
        attend_last(h)
        i0 = next(ids)
        next(ids)
        a_ids.append(i0)
        for m in range(2):
            lo = h * ROWS + m * HEAD
            part = acc[c, lo:lo + HEAD, :] + take[h, m * HEAD:(m + 1) * HEAD, :].astype(F32)
            ast[h, m] = jnp.transpose(part[:, :HEAD] / part[:, HEAD:]).astype(BF16)
            copy = pltpu.make_async_remote_copy(
                src_ref=ast.at[h, m], dst_ref=abuf.at[h, x, y],
                send_sem=send_sems.at[i0 + m], recv_sem=recv_sems.at[i0 + y],
                device_id={"seq": seq_of(c, z, m)}, device_id_type=MESH,
            )
            is_self = jnp.logical_and(stays, c == m)
            a_copies[h, m] = copy, jnp.logical_not(is_self)

            @pl.when(is_self)
            def _():
                abuf[h, x, y] = ast[h, m]

            @pl.when(jnp.logical_not(is_self))
            def _():
                copy.start()

    x_ids = {}
    for h in range(2):
        for k, b in enumerate((y, 1 - y)):
            mine = abuf.at[h, x, b]
            if k:
                arrived(mine, a_ids[h] + b)
            else:
                @pl.when(leaves)
                def _():
                    arrived(mine, a_ids[h] + b)
            for d in (2, 1, 3):
                x_ids[h, k, d] = push(mine, mine, {"grp": (x + d) % 4})

    for i, land in o_y:
        arrived(land, i)
    for zz in range(Z):
        here = owb.at[seq_of(1 - y, zz, c)]
        o_s.append((push(here, here, sib), owb.at[seq_of(1 - y, zz, 1 - c)]))
    for i, land in o_s:
        arrived(land, i)

    def project(h, yh):
        total = None
        for xx in range(4):
            w = owb[pl.ds(xx * 8 + yh * 2, 2)].reshape(2 * WROWS, 2 * HEAD)
            a = abuf[h, xx].reshape(2 * HEAD, HEAD)
            term = jnp.dot(w, a, preferred_element_type=F32)
            total = term if total is None else total + term
        return total

    r_ids, totals = {}, []
    for h in range(2):
        for d in (1, 3, 2):
            for k, b in enumerate((y, 1 - y)):
                arrived(abuf.at[h, (x + 4 - d) % 4, b], x_ids[h, k, d])
        r_ids[h] = [next(ids) for _ in range(3)][0] - 1

        def piece(h, d):
            return remote(pst.at[h, d], rbuf.at[h, d], {"tp": (tp + d) % 4}, r_ids[h] + d)

        def step(i, carry):
            d = 1 + (i + 1) % 3
            pst[h, d] = project(h, (tp + d) % 4).astype(BF16)
            piece(h, d).start()
            return carry

        lax.fori_loop(0, 3, step, 0)
        totals.append(project(h, tp))

    for h in range(2):
        total = totals[h]
        for d in (1, 3, 2):
            arrived(rbuf.at[h, d], r_ids[h] + d)
            total = total + rbuf[h, d].astype(F32)
        at = slice(h * HEAD, (h + 1) * HEAD)
        out[:, at] = res[:, at] + total

    for copy in sent:
        copy.wait_send()
    for h in range(2):
        for d in range(1, 4):
            piece(h, d).wait_send()

    @pl.when(leaves)
    def _():
        x_remote.wait_send()

    for copy, remote_target in a_copies.values():
        @pl.when(remote_target)
        def _():
            copy.wait_send()


def body(latent, condition, modulation, qk_gain, qkv_weight, out_weight):
    modulation = jnp.transpose(modulation, (1, 0, 2))
    vm = pl.BlockSpec(memory_space=pltpu.VMEM)
    hbm = pl.BlockSpec(memory_space=pltpu.HBM)
    mixed = pl.pallas_call(
        kernel,
        out_shape=jax.ShapeDtypeStruct((2 * WROWS, ROWS), F32),
        in_specs=[hbm, hbm, hbm, vm, hbm, hbm],
        out_specs=vm,
        scratch_shapes=[
            pltpu.VMEM((ROWS, D), BF16),
            pltpu.VMEM((ROWS, D), BF16),
            pltpu.VMEM((3, 2, D), F32),
            pltpu.VMEM((2, WROWS, HEAD), BF16),
            pltpu.VMEM((WROWS, 2 * HEAD), BF16),
            pltpu.VMEM((3, 2, Z, 2, WROWS, HEAD), BF16),
            pltpu.VMEM((2, ROWS, D), BF16),
            pltpu.VMEM((2, ROWS, D), BF16),
            pltpu.VMEM((2, 2, 2, HEAD, HEAD), BF16),
            pltpu.VMEM((Z, 2, HEAD, ROWS), BF16),
            pltpu.VMEM((Z, CHIP, HEAD), BF16),
            pltpu.VMEM((32, WROWS, 2 * HEAD), BF16),
            pltpu.VMEM((2, CHIP, 2 * HEAD), F32),
            pltpu.VMEM((2, 4, 2, HEAD, HEAD), BF16),
            pltpu.VMEM((2, 2, HEAD, HEAD), BF16),
            pltpu.VMEM((2, 4, 2 * WROWS, HEAD), BF16),
            pltpu.VMEM((2, 4, 2 * WROWS, HEAD), BF16),
            pltpu.VMEM((2 * WROWS, ROWS), F32),
            pltpu.VMEM((2, ROWS, 2 * HEAD), BF16),
            pltpu.VMEM((2, ROWS, 2 * HEAD), BF16),
            pltpu.SemaphoreType.DMA((N_SEMS,)),
            pltpu.SemaphoreType.DMA((N_SEMS,)),
            pltpu.SemaphoreType.DMA((8,)),
        ],
        compiler_params=pltpu.CompilerParams(
            collective_id=0, has_side_effects=True, vmem_limit_bytes=56 * 1024 * 1024
        ),
        cost_estimate=pl.CostEstimate(
            flops=3_900_000_000, bytes_accessed=4_000_000, transcendentals=4_200_000
        ),
    )(latent, condition, modulation, qk_gain, qkv_weight, jnp.transpose(out_weight, (0, 2, 1)))
    return mixed.astype(BF16).T


def solution(mesh):
    return jax.shard_map(
        body,
        mesh=mesh,
        in_specs=(
            P("seq", None),
            P("seq", None),
            P(),
            P(),
            P(None, None, "seq", ("grp", "tp")),
            P(None, ("grp", "tp"), "seq"),
        ),
        out_specs=P("seq", ("grp", "tp")),
        check_vma=False,
    )
```

```python
import math

import jax
import jax.numpy as jnp
from jax import lax
from jax.experimental import pallas as pl
from jax.experimental.pallas import tpu as pltpu
from jax.sharding import PartitionSpec as P

MESH = pl.DeviceIdType.MESH
BF16, F32 = jnp.bfloat16, jnp.float32
Z = 8
ROWS = 256
CHIP = 2 * ROWS
D = 3072
HEAD = 128
WROWS = 96
N_SEMS = 240


def kernel(
    lat_in, cond_in, mod_in, gain, wsh, ow_in, out,
    lat, cond, mod, ow, owt, wbuf, xbuf, xst, qbuf, kbuf, vbuf, owb, acc, abuf, ast, pst, rbuf, res, give, take,
    send_sems, recv_sems, load_sems,
):
    loads = []
    for i, (a, b) in enumerate(((ow_in, ow), (mod_in, mod), (lat_in, lat), (cond_in, cond))):
        loads.append(pltpu.make_async_copy(a, b, load_sems.at[i]))
        loads[-1].start()
    x, s, tp = lax.axis_index("grp"), lax.axis_index("seq"), lax.axis_index("tp")
    y, z, c = s // 16, (s // 2) % 8, s % 2

    def seq_of(y_, z_, c_):
        return y_ * 16 + z_ * 2 + c_

    sib = {"seq": seq_of(y, z, 1 - c)}
    row = {"seq": seq_of(1 - y, z, c)}
    beyond = {"tp": (tp + c * (3 - 2 * y)) % 4, "seq": seq_of(1 - y, z, y)}
    right = {"seq": seq_of(y, (z + 1) % Z, c)}
    left = {"seq": seq_of(y, (z + 7) % Z, c)}

    def zm(t):
        return (z + Z - t) % Z

    def zp(t):
        return (z + t) % Z

    px, py, pz = y * 2 + z // 4, x // 2, z % 4 + 4 * (x % 2)
    moves = px != x
    partner = {"grp": px, "seq": seq_of(py, pz, c)}

    barrier = pltpu.get_barrier_semaphore()

    def greet(device):
        pl.semaphore_signal(barrier, inc=1, device_id=device, device_id_type=MESH)

    flat = x * 4 + y * 2 + c
    for i in range(1, 16):
        f = (flat + i) % 16
        greet({"grp": f // 4, "seq": seq_of((f // 2) % 2, z, f % 2)})
    for device in (right, left):
        greet(device)
    for i in (1, 3):
        for core in range(2):
            greet({"tp": (tp + i) % 4, "seq": seq_of(1 - y, z, core)})
    for i in range(1, 4):
        greet({"tp": (tp + i) % 4})

    @pl.when(moves)
    def _():
        greet(partner)

    pl.semaphore_wait(barrier, 24 + jnp.where(moves, 1, 0))

    ids = iter(range(N_SEMS))
    sent = []

    def remote(src, dst, device, i):
        return pltpu.make_async_remote_copy(
            src_ref=src, dst_ref=dst, send_sem=send_sems.at[i], recv_sem=recv_sems.at[i],
            device_id=device, device_id_type=MESH,
        )

    def push(src, dst, device):
        i = next(ids)
        copy = remote(src, dst, device, i)
        copy.start()
        sent.append(copy)
        return i

    def arrived(land, i):
        remote(land, land, sib, i).wait_recv()

    def ring_send(view, t):
        if t < 3:
            a, b = view(zm(t), None), view(zp(t), None)
        else:
            a, b = view(zm(t), 0), view(zp(t), 1)
        return push(a, a, right), push(b, b, left)

    def ring_wait(view, t, got):
        if t < 4:
            arrived(view(zm(t), None), got[0])
            arrived(view(zp(t), None), got[1])
        else:
            arrived(view(zm(t), 0), got[0])
            arrived(view(zp(t), 1), got[1])

    stays = y == c
    leaves = jnp.logical_not(stays)
    w_own, w_row = {}, {}
    for j in (1, 2, 0):
        w_row[j] = push(wsh.at[1 - y, j], wbuf.at[j, y, z, c], row)
        w_own[j] = pltpu.make_async_copy(wsh.at[y, j], wbuf.at[j, y, z, c], load_sems.at[4 + j])
        w_own[j].start()

    ow_id = next(ids)
    ow_copy = remote(owt, owb.at[seq_of(py, pz, c)], partner, ow_id)
    loads[0].wait()
    loads[1].wait()
    first = s * WROWS
    base = jnp.minimum(first // HEAD * HEAD, D - 2 * HEAD)
    for block in range(2):
        gates = mod[2, block:block + 1, pl.ds(pl.multiple_of(base, HEAD), 2 * HEAD)]
        gates = pltpu.roll(jnp.broadcast_to(gates, (HEAD, 2 * HEAD)), (2 * HEAD + base - first) % (2 * HEAD), 1)
        gates = jnp.transpose(gates[:, :WROWS])
        owt[:, block * HEAD:(block + 1) * HEAD] = (ow[block].astype(F32) * gates).astype(BF16)

    @pl.when(moves)
    def _():
        ow_copy.start()

    @pl.when(jnp.logical_not(moves))
    def _():
        owb[s] = owt[...]

    def layer_norm(block, store, lo, hi):
        use = jnp.where(block == 0, 1.0, 0.0).astype(F32)
        scale = 1.0 + mod[1, pl.ds(block, 1), :]
        shift = mod[0, pl.ds(block, 1), :]

        def step(i, carry):
            at = pl.ds(pl.multiple_of(i * 32, 32), 32)
            v = lat[at, :].astype(F32) + use * cond[at, :].astype(F32)
            center = v - jnp.mean(v, axis=-1, keepdims=True)
            var = jnp.mean(center * center, axis=-1, keepdims=True)
            store(at, (center * lax.rsqrt(var + 1e-6) * scale + shift).astype(BF16))
            return carry

        lax.fori_loop(lo, hi, step, 0)

    def store_to(k):
        def store(at, v):
            xst[k, at, :] = v

        return store

    def view_w(j):
        def view(zz, h):
            return wbuf.at[j, :, zz, c] if h is None else wbuf.at[j, :, zz, c, pl.ds(h * 48, 48)]

        return view

    w_shared = {0: [], 1: [], 2: []}

    def w_share(j, zz):
        mine = wbuf.at[j, :, zz, c]
        w_shared[j].append((push(mine, mine, sib), wbuf.at[j, :, zz, 1 - c]))

    def w_hop(j, t, got):
        if t == 0:
            w_own[j].wait()
            arrived(wbuf.at[j, 1 - y, z, c], w_row[j])
        else:
            ring_wait(view_w(j), t, got)
        if 0 < t < 4:
            w_share(j, zm(t))
        if t < 4:
            got = ring_send(view_w(j), t)
        w_share(j, zp(t))
        return got

    def w_come(j):
        for i, land in w_shared[j]:
            arrived(land, i)

    def view_o(zz, h):
        base = seq_of(y, zz, c)
        return owb.at[base] if h is None else owb.at[base, pl.ds(h * 48, 48)]

    got_w = {j: w_hop(j, 0, None) for j in (1, 2, 0)}
    for load in loads[2:]:
        load.wait()
    x_base = [next(ids) for _ in range(4)][0]
    beyond_copies = [
        pltpu.make_async_remote_copy(
            src_ref=xst.at[0, pl.ds(part * HEAD, HEAD)], dst_ref=xbuf.at[c, pl.ds(part * HEAD, HEAD)],
            send_sem=send_sems.at[x_base + part], recv_sem=recv_sems.at[x_base + 2 * part + c],
            device_id=beyond, device_id_type=MESH,
        )
        for part in range(2)
    ]
    sent.extend(beyond_copies)
    layer_norm(1 - y, store_to(0), 0, 4)
    beyond_copies[0].start()
    layer_norm(1 - y, store_to(0), 4, 8)
    beyond_copies[1].start()
    g = x * 4 + tp
    near = lat[:, pl.ds(pl.multiple_of(g * 3 // 2 * HEAD, HEAD), 2 * HEAD)].astype(F32)
    near = jnp.where(g % 2 == 0, near[:, :2 * WROWS], near[:, HEAD // 2:])
    res[...] = jnp.transpose(near)

    x_id = next(ids)
    x_local = pltpu.make_async_copy(xst.at[1], xbuf.at[c], load_sems.at[7])
    x_remote = remote(xst.at[1], xbuf.at[c], sib, x_id)
    for t in range(1, 5):
        for j in (1, 2, 0):
            got_w[j] = w_hop(j, t, got_w[j])
        if t == 1:
            @pl.when(moves)
            def _():
                ow_copy.wait_send()
                arrived(owb.at[s], ow_id)

        else:
            ring_wait(view_o, t - 1, got_o)
        got_o = ring_send(view_o, t - 1)
        if t < 3:
            layer_norm(y, store_to(1), 4 * t - 4, 4 * t)
        if t == 2:
            @pl.when(stays)
            def _():
                x_local.start()

            @pl.when(leaves)
            def _():
                x_remote.start()

    o_y, o_s = [], []

    def o_pass(zz):
        here, there = owb.at[seq_of(y, zz, c)], owb.at[seq_of(1 - y, zz, c)]
        o_y.append((push(here, here, row), there))
        o_s.append((push(here, here, sib), owb.at[seq_of(y, zz, 1 - c)]))

    w_come(1)

    def tokens_come(part):
        @pl.when(leaves)
        def _():
            for core in range(2):
                arrived(xbuf.at[core, pl.ds(part * HEAD, HEAD)], x_base + 2 * part + core)

        if part == 0:
            @pl.when(stays)
            def _():
                x_local.wait()
                arrived(xbuf.at[1 - c], x_id)

    def head_norm(v, g):
        return v * lax.rsqrt(jnp.mean(v * v, axis=-1, keepdims=True) + 1e-6) * g

    q_gain = gain[y, 0:1, :] * (math.log2(math.e) / math.sqrt(HEAD))
    k_gain = gain[y, 1:2, :]

    def project_in(j, m, store):
        rows = xbuf[:, m * HEAD:(m + 1) * HEAD, :].reshape(ROWS, D)
        store(m, jnp.dot(rows, wbuf[j].reshape(D, HEAD), preferred_element_type=F32))

    def rows_of(m):
        return pl.ds(pl.multiple_of(m * ROWS, ROWS), ROWS)

    def store_k(m, v):
        kbuf[z, m] = jnp.transpose(head_norm(v, k_gain)).astype(BF16)

    def store_v(m, v):
        vbuf[z, rows_of(m), :] = v.astype(BF16)

    def store_q(m, v):
        v = head_norm(v, q_gain).astype(BF16)
        for core in range(2):
            qbuf[c, m, core] = v[core * HEAD:(core + 1) * HEAD]

    def view_k(zz, h):
        return kbuf.at[zz, h]

    def view_v(zz, h):
        return vbuf.at[zz, pl.ds(h * ROWS, ROWS)]

    def flow(view, h, t):
        a, b = view(zm(t), h), view(zp(t), h)
        return (push(a, a, right) if t < 3 or h == 0 else None,
                push(b, b, left) if t < 3 or h == 1 else None)

    def hop(view, h, t, got):
        for i, zz in zip(got, (zm(t), zp(t))):
            if i is not None:
                arrived(view(zz, h), i)
        return flow(view, h, t) if t < 4 else None

    got_kv = {}
    for part in range(2):
        tokens_come(part)
        project_in(1, part, store_k)
        got_kv[part, 0] = flow(view_k, part, 0)
        if part == 0:
            w_come(2)
        project_in(2, part, store_v)
        got_kv[part, 1] = flow(view_v, part, 0)
    ring_wait(view_o, 4, got_o)

    acc[...] = jnp.zeros_like(acc)
    ones = jnp.ones((CHIP, HEAD), BF16)
    w_come(0)
    for part in range(2):
        project_in(0, part, store_q)
    q_id = push(qbuf.at[c], qbuf.at[c], sib)

    def attend(places, r, halves=(0, 2)):
        lo, hi = halves
        at = slice(lo * ROWS, hi * ROWS)
        queries = qbuf[r, lo:hi].reshape((hi - lo) * ROWS, HEAD)
        weights = jnp.concatenate([
            jnp.exp2(jnp.dot(queries, kbuf[zz, h], preferred_element_type=F32)).astype(BF16)
            for zz in places for h in range(2)
        ], axis=1)
        values = jnp.concatenate([
            jnp.concatenate([vbuf[zz], ones], axis=1) for zz in places
        ], axis=0)
        acc[r, at, :] += jnp.dot(weights, values, preferred_element_type=F32)

    for t in range(1, 5):
        for part in range(2):
            for i, view in enumerate((view_k, view_v)):
                got_kv[part, i] = hop(view, part, t, got_kv[part, i])
        if t < 4:
            for zz in ((z, zm(1), zp(1)), (zm(2), zp(2), zm(3)), (zp(3), zp(4)))[t - 1]:
                o_pass(zz)
            places = [zm(t), zp(t)] + [z] * (t == 1)
            attend(places, c)

            @pl.when(leaves)
            def _():
                if t == 1:
                    arrived(qbuf.at[1 - c], q_id)
                attend(places, 1 - c)

    @pl.when(stays)
    def _():
        arrived(qbuf.at[1 - c], q_id)
        for t in range(1, 4):
            attend([zm(t), zp(t)] + [z] * (t == 1), 1 - c)

    given = []
    for h in range(2):
        attend([zp(4)], 1 - c, (h, h + 1))
        give[h] = acc[1 - c, h * ROWS:(h + 1) * ROWS, :].astype(BF16)
        given.append(push(give.at[h], take.at[h], sib))

    def attend_last(h):
        attend([zp(4)], c, (h, h + 1))
        arrived(take.at[h], given[h])

    a_ids, a_copies = [], {}
    for h in range(2):
        attend_last(h)
        i0 = next(ids)
        next(ids)
        a_ids.append(i0)
        for m in range(2):
            lo = h * ROWS + m * HEAD
            part = acc[c, lo:lo + HEAD, :] + take[h, m * HEAD:(m + 1) * HEAD, :].astype(F32)
            ast[h, m] = jnp.transpose(part[:, :HEAD] / part[:, HEAD:]).astype(BF16)
            copy = pltpu.make_async_remote_copy(
                src_ref=ast.at[h, m], dst_ref=abuf.at[h, x, y],
                send_sem=send_sems.at[i0 + m], recv_sem=recv_sems.at[i0 + y],
                device_id={"seq": seq_of(c, z, m)}, device_id_type=MESH,
            )
            is_self = jnp.logical_and(stays, c == m)
            a_copies[h, m] = copy, jnp.logical_not(is_self)

            @pl.when(is_self)
            def _():
                abuf[h, x, y] = ast[h, m]

            @pl.when(jnp.logical_not(is_self))
            def _():
                copy.start()

    x_ids = {}
    for h in range(2):
        for k, b in enumerate((y, 1 - y)):
            mine = abuf.at[h, x, b]
            if k:
                arrived(mine, a_ids[h] + b)
            else:
                @pl.when(leaves)
                def _():
                    arrived(mine, a_ids[h] + b)
            for d in (2, 1, 3):
                x_ids[h, k, d] = push(mine, mine, {"grp": (x + d) % 4})

    for i, land in o_y:
        arrived(land, i)
    for zz in range(Z):
        here = owb.at[seq_of(1 - y, zz, c)]
        o_s.append((push(here, here, sib), owb.at[seq_of(1 - y, zz, 1 - c)]))
    for i, land in o_s:
        arrived(land, i)

    def project(h, yh):
        total = None
        for xx in range(4):
            w = owb[pl.ds(xx * 8 + yh * 2, 2)].reshape(2 * WROWS, 2 * HEAD)
            a = abuf[h, xx].reshape(2 * HEAD, HEAD)
            term = jnp.dot(w, a, preferred_element_type=F32)
            total = term if total is None else total + term
        return total

    r_ids, totals = {}, []
    for h in range(2):
        for d in (1, 3, 2):
            for k, b in enumerate((y, 1 - y)):
                arrived(abuf.at[h, (x + 4 - d) % 4, b], x_ids[h, k, d])
        r_ids[h] = [next(ids) for _ in range(3)][0] - 1

        def piece(h, d):
            return remote(pst.at[h, d], rbuf.at[h, d], {"tp": (tp + d) % 4}, r_ids[h] + d)

        def step(i, carry):
            d = 1 + (i + 1) % 3
            pst[h, d] = project(h, (tp + d) % 4).astype(BF16)
            piece(h, d).start()
            return carry

        lax.fori_loop(0, 3, step, 0)
        totals.append(project(h, tp))

    for h in range(2):
        total = totals[h]
        for d in (1, 3, 2):
            arrived(rbuf.at[h, d], r_ids[h] + d)
            total = total + rbuf[h, d].astype(F32)
        at = slice(h * HEAD, (h + 1) * HEAD)
        out[:, at] = res[:, at] + total

    for copy in sent:
        copy.wait_send()
    for h in range(2):
        for d in range(1, 4):
            piece(h, d).wait_send()

    @pl.when(leaves)
    def _():
        x_remote.wait_send()

    for copy, remote_target in a_copies.values():
        @pl.when(remote_target)
        def _():
            copy.wait_send()


def body(latent, condition, modulation, qk_gain, qkv_weight, out_weight):
    modulation = jnp.transpose(modulation, (1, 0, 2))
    vm = pl.BlockSpec(memory_space=pltpu.VMEM)
    hbm = pl.BlockSpec(memory_space=pltpu.HBM)
    mixed = pl.pallas_call(
        kernel,
        out_shape=jax.ShapeDtypeStruct((2 * WROWS, ROWS), F32),
        in_specs=[hbm, hbm, hbm, vm, hbm, hbm],
        out_specs=vm,
        scratch_shapes=[
            pltpu.VMEM((ROWS, D), BF16),
            pltpu.VMEM((ROWS, D), BF16),
            pltpu.VMEM((3, 2, D), F32),
            pltpu.VMEM((2, WROWS, HEAD), BF16),
            pltpu.VMEM((WROWS, 2 * HEAD), BF16),
            pltpu.VMEM((3, 2, Z, 2, WROWS, HEAD), BF16),
            pltpu.VMEM((2, ROWS, D), BF16),
            pltpu.VMEM((2, ROWS, D), BF16),
            pltpu.VMEM((2, 2, 2, HEAD, HEAD), BF16),
            pltpu.VMEM((Z, 2, HEAD, ROWS), BF16),
            pltpu.VMEM((Z, CHIP, HEAD), BF16),
            pltpu.VMEM((32, WROWS, 2 * HEAD), BF16),
            pltpu.VMEM((2, CHIP, 2 * HEAD), F32),
            pltpu.VMEM((2, 4, 2, HEAD, HEAD), BF16),
            pltpu.VMEM((2, 2, HEAD, HEAD), BF16),
            pltpu.VMEM((2, 4, 2 * WROWS, HEAD), BF16),
            pltpu.VMEM((2, 4, 2 * WROWS, HEAD), BF16),
            pltpu.VMEM((2 * WROWS, ROWS), F32),
            pltpu.VMEM((2, ROWS, 2 * HEAD), BF16),
            pltpu.VMEM((2, ROWS, 2 * HEAD), BF16),
            pltpu.SemaphoreType.DMA((N_SEMS,)),
            pltpu.SemaphoreType.DMA((N_SEMS,)),
            pltpu.SemaphoreType.DMA((8,)),
        ],
        compiler_params=pltpu.CompilerParams(
            collective_id=0, has_side_effects=True, vmem_limit_bytes=56 * 1024 * 1024
        ),
        cost_estimate=pl.CostEstimate(
            flops=3_900_000_000, bytes_accessed=4_000_000, transcendentals=4_200_000
        ),
    )(latent, condition, modulation, qk_gain, qkv_weight, jnp.transpose(out_weight, (0, 2, 1)))
    return mixed.astype(BF16).T


def solution(mesh):
    return jax.shard_map(
        body,
        mesh=mesh,
        in_specs=(
            P("seq", None),
            P("seq", None),
            P(),
            P(),
            P(None, None, "seq", ("grp", "tp")),
            P(None, ("grp", "tp"), "seq"),
        ),
        out_specs=P("seq", ("grp", "tp")),
        check_vma=False,
    )
```
